32 devices in a mesh: gx: 2 (over x), gy: 4 (over z), gz: 4 (over y, core).
Axes of the slice: x: 2, y: 2, z: 4, core: 2. Of those that a mesh axis runs over, the one named last changes fastest.
Arguments:
- right_side: float32 [16, 64, 512], P('gx', 'gy', 'gz'), may hold values from -6 to 6
- coefficient: float32 [16, 64, 512], P('gx', 'gy', 'gz'), may hold values from 0.25 to 4
Outputs:
- solution: float32 [16, 64, 512], P('gx', 'gy', 'gz')
- residual: float32 [16, 64, 512], P('gx', 'gy', 'gz')
The draws below stay inside these ranges and needn't reach their ends.
All inputs are finite; a program needn't handle non-finite values.
Results may differ from the reference program's by a relative error of at most 0.0003.
Values sent between devices are 32-bit elements; how exact they have to be, the bound alone decides.
No kernel may reach another device: no remote copies, remote signals or barrier semaphores. Data moves between devices by JAX's collectives and lax.ppermute only.
A program may use at most 64 MiB of HBM per device.

```python
import math
import jax
import jax.numpy as jnp

LEVELS = 3
DEGREE = 4
NX = 16
NY = 64
NZ = 512


def draw_right_side(key, part):
    return jnp.clip(jax.random.normal(key, (NX, NY, NZ), jnp.float32), -6.0, 6.0)


def block_levels(rng, shape, shards, smallest, top_value):
    def one(dim, parts):
        heights = jax.random.uniform(jax.random.fold_in(jax.random.fold_in(rng, 6), dim), (parts,), jnp.float32, smallest / len(shards), top_value / len(shards))
        return jnp.repeat(jnp.exp(heights), shape[dim] // parts).reshape((-1,) + (1,) * (len(shape) - dim - 1))

    factor_of = one(*shards[0])
    for cut in shards[1:]:
        factor_of = factor_of * one(*cut)
    return factor_of


def setup_inputs(seed: int = 0) -> dict:
    key_list = jax.random.split(jax.random.key(seed), 3)
    right_side = draw_right_side(jax.random.fold_in(key_list[2], 71), 0)
    coefficient = jnp.clip(jnp.exp(math.log(4.0) - 2.7725887 * jax.random.uniform(key_list[1], (NX, NY, NZ), jnp.float32) ** block_levels(key_list[1], (NX, NY, NZ), ((0, 2), (1, 4), (2, 4)), -0.2, 0.2)), 0.25, 4.0)
    return {"right_side": right_side, "coefficient": coefficient}


cheb_low = 0.3
cheb_high = 2.0


def face_terms(padded):
    face_x = 0.5 * (padded[1:, 1:-1, 1:-1] + padded[:-1, 1:-1, 1:-1])
    face_y = 0.5 * (padded[1:-1, 1:, 1:-1] + padded[1:-1, :-1, 1:-1])
    face_z = 0.5 * (padded[1:-1, 1:-1, 1:] + padded[1:-1, 1:-1, :-1])
    diagonal = face_x[1:] + face_x[:-1] + face_y[:, 1:] + face_y[:, :-1] + face_z[:, :, 1:] + face_z[:, :, :-1]
    return face_x, face_y, face_z, diagonal


def apply_padded(padded, face_set, factor):
    face_x, face_y, face_z, diagonal = face_set
    flux_x = face_x * (padded[1:, 1:-1, 1:-1] - padded[:-1, 1:-1, 1:-1])
    flux_y = face_y * (padded[1:-1, 1:, 1:-1] - padded[1:-1, :-1, 1:-1])
    flux_z = face_z * (padded[1:-1, 1:-1, 1:] - padded[1:-1, 1:-1, :-1])
    result = (flux_x[:-1] - flux_x[1:]) + (flux_y[:, :-1] - flux_y[:, 1:]) + (flux_z[:, :, :-1] - flux_z[:, :, 1:])
    return factor * result


def zero_pad(values):
    return jnp.pad(values, 1)


def restrict(values):
    size_x, size_y, size_z = values.shape
    blocks = values.reshape(size_x // 2, 2, size_y // 2, 2, size_z // 2, 2)
    return jnp.mean(blocks, axis=(1, 3, 5))


def prolong(values):
    size_x, size_y, size_z = values.shape
    spread = jnp.broadcast_to(values[:, None, :, None, :, None], (size_x, 2, size_y, 2, size_z, 2))
    return spread.reshape(2 * size_x, 2 * size_y, 2 * size_z)


def smooth(right, initial, face_set, factor, padder):
    diagonal = face_set[3]
    centre = 0.5 * (cheb_high + cheb_low)
    half_width = 0.5 * (cheb_high - cheb_low)
    sigma_val = centre / half_width
    rho_now = 1.0 / sigma_val
    if initial is None:
        iterate = jnp.zeros_like(right)
        leftover = right
    else:
        iterate = initial
        leftover = right - apply_padded(padder(initial), face_set, factor)
    update = leftover / (factor * diagonal) / centre
    iterate = iterate + update
    for sweep_no in range(DEGREE - 1):
        leftover = right - apply_padded(padder(iterate), face_set, factor)
        rho_next = 1.0 / (2.0 * sigma_val - rho_now)
        update = rho_next * rho_now * update + (2.0 * rho_next / half_width) * (leftover / (factor * diagonal))
        iterate = iterate + update
        rho_now = rho_next
    return iterate


def reference(right_side, coefficient):
    rights = [right_side]
    coarse_coef = coefficient
    face_sets = []
    iterates = []
    for level_no in range(LEVELS):
        factor = 0.25 ** level_no
        face_set = face_terms(zero_pad(coarse_coef))
        face_sets.append(face_set)
        current = smooth(rights[-1], None, face_set, factor, zero_pad)
        iterates.append(current)
        if level_no < LEVELS - 1:
            leftover = rights[-1] - apply_padded(zero_pad(current), face_set, factor)
            rights.append(restrict(leftover))
            coarse_coef = restrict(coarse_coef)
    for level_no in range(LEVELS - 2, -1, -1):
        iterates[level_no] = smooth(rights[level_no], iterates[level_no] + prolong(iterates[level_no + 1]), face_sets[level_no], 0.25 ** level_no, zero_pad)
    solution = iterates[0]
    residual = right_side - apply_padded(zero_pad(solution), face_sets[0], 1.0)
    return solution, residual
```

```python
import jax
import jax.numpy as jnp
from jax import lax
from jax.experimental import pallas as pl
from jax.experimental.pallas import tpu as pltpu
from jax.sharding import PartitionSpec as P

LEVELS = 3
DEGREE = 4


cheb_low = 0.3
cheb_high = 2.0


def extended(block, sides, width):
    for axis, dim in sides:
        count = lax.axis_size(axis)
        forward = [(i, i + 1) for i in range(count - 1)]
        backward = [(target, source) for source, target in forward]
        low = lax.ppermute(
            lax.slice_in_dim(block, block.shape[dim] - width, None, axis=dim), axis, forward
        )
        high = lax.ppermute(lax.slice_in_dim(block, 0, width, axis=dim), axis, backward)
        block = jnp.concatenate([low, block, high], axis=dim)
    return block


def face_terms(padded):
    face_x = 0.5 * (padded[1:, 1:-1, 1:-1] + padded[:-1, 1:-1, 1:-1])
    face_y = 0.5 * (padded[1:-1, 1:, 1:-1] + padded[1:-1, :-1, 1:-1])
    face_z = 0.5 * (padded[1:-1, 1:-1, 1:] + padded[1:-1, 1:-1, :-1])
    diagonal = (
        face_x[1:]
        + face_x[:-1]
        + face_y[:, 1:]
        + face_y[:, :-1]
        + face_z[:, :, 1:]
        + face_z[:, :, :-1]
    )
    return (face_x, face_y, face_z, diagonal)


def apply_padded(padded, face_set, factor):
    face_x, face_y, face_z, diagonal = face_set
    flux_x = face_x * (padded[1:, 1:-1, 1:-1] - padded[:-1, 1:-1, 1:-1])
    flux_y = face_y * (padded[1:-1, 1:, 1:-1] - padded[1:-1, :-1, 1:-1])
    flux_z = face_z * (padded[1:-1, 1:-1, 1:] - padded[1:-1, 1:-1, :-1])
    result = (
        flux_x[:-1]
        - flux_x[1:]
        + (flux_y[:, :-1] - flux_y[:, 1:])
        + (flux_z[:, :, :-1] - flux_z[:, :, 1:])
    )
    return factor * result


def fine_halo(values):
    return extended(values, (("gx", 0), ("gy", 1), ("gz", 2)), 1)


def spread_halo(values):
    return extended(values, (("gx", 0), ("gy", 1), ("gz", 2)), 1)


def restrict(values):
    size_x, size_y, size_z = values.shape
    blocks = values.reshape(size_x // 2, 2, size_y // 2, 2, size_z // 2, 2)
    return jnp.mean(blocks, axis=(1, 3, 5))


def prolong(values):
    size_x, size_y, size_z = values.shape
    spread = jnp.broadcast_to(values[:, None, :, None, :, None], (size_x, 2, size_y, 2, size_z, 2))
    return spread.reshape(2 * size_x, 2 * size_y, 2 * size_z)


def trim_cells(values, layers):
    return values[
        layers : values.shape[0] - layers,
        layers : values.shape[1] - layers,
        layers : values.shape[2] - layers,
    ]


def trim_faces(face_set, layers):
    return tuple((trim_cells(member, layers) for member in face_set))


def inside_mask(shape, margin):
    count_x = shape[0]
    count_y = shape[1]
    count_z = shape[2]
    along_x = lax.axis_index("gx") * count_x + jnp.arange(
        -margin, count_x + margin, dtype=jnp.int32
    )
    along_y = lax.axis_index("gy") * count_y + jnp.arange(
        -margin, count_y + margin, dtype=jnp.int32
    )
    along_z = lax.axis_index("gz") * count_z + jnp.arange(
        -margin, count_z + margin, dtype=jnp.int32
    )
    valid_x = (along_x >= 0) & (along_x < count_x * lax.axis_size("gx"))
    valid_y = (along_y >= 0) & (along_y < count_y * lax.axis_size("gy"))
    valid_z = (along_z >= 0) & (along_z < count_z * lax.axis_size("gz"))
    return valid_x[:, None, None] & valid_y[None, :, None] & valid_z[None, None, :]


def deep_smooth(right_wide, start_wide, face_wide, valid_wide):
    centre = 0.5 * (cheb_high + cheb_low)
    half_width = 0.5 * (cheb_high - cheb_low)
    sigma_val = centre / half_width
    rho_now = 1.0 / sigma_val
    safe_diag = jnp.where(valid_wide, face_wide[3], 1.0)
    if start_wide is None:
        update = jnp.where(valid_wide, right_wide / (1.0 * safe_diag) / centre, 0.0)
        iterate = update
        lost = 0
    else:
        leftover = trim_cells(right_wide, 1) - apply_padded(
            start_wide, trim_faces(face_wide, 1), 1.0
        )
        update = jnp.where(
            trim_cells(valid_wide, 1), leftover / (1.0 * trim_cells(safe_diag, 1)) / centre, 0.0
        )
        iterate = trim_cells(start_wide, 1) + update
        lost = 1
    for sweep_no in range(DEGREE - 1):
        lost = lost + 1
        leftover = trim_cells(right_wide, lost) - apply_padded(
            iterate, trim_faces(face_wide, lost), 1.0
        )
        rho_next = 1.0 / (2.0 * sigma_val - rho_now)
        fresh = rho_next * rho_now * trim_cells(update, 1) + 2.0 * rho_next / half_width * (
            leftover / (1.0 * trim_cells(safe_diag, lost))
        )
        update = jnp.where(trim_cells(valid_wide, lost), fresh, 0.0)
        iterate = trim_cells(iterate, 1) + update
        rho_now = rho_next
    return (iterate, lost)


def smooth(right, initial, face_set, factor, padder):
    diagonal = face_set[3]
    centre = 0.5 * (cheb_high + cheb_low)
    half_width = 0.5 * (cheb_high - cheb_low)
    sigma_val = centre / half_width
    rho_now = 1.0 / sigma_val
    if initial is None:
        iterate = jnp.zeros_like(right)
        leftover = right
    else:
        iterate = initial
        leftover = right - apply_padded(padder(initial), face_set, factor)
    update = leftover / (factor * diagonal) / centre
    iterate = iterate + update
    for sweep_no in range(DEGREE - 1):
        leftover = right - apply_padded(padder(iterate), face_set, factor)
        rho_next = 1.0 / (2.0 * sigma_val - rho_now)
        update = rho_next * rho_now * update + 2.0 * rho_next / half_width * (
            leftover / (factor * diagonal)
        )
        iterate = iterate + update
        rho_now = rho_next
    return iterate


def per_device(right_side, coefficient):
    depth = DEGREE
    stacked = jnp.stack([right_side, coefficient])
    widened = extended(stacked, (("gx", 1), ("gy", 2), ("gz", 3)), depth + 1)
    right_wide = trim_cells(widened[0], 1)
    face_wide = face_terms(widened[1])
    valid_wide = inside_mask(right_side.shape, depth)
    fine_set = trim_faces(face_wide, depth)
    partial_value, lost = deep_smooth(right_wide, None, face_wide, valid_wide)
    leftover = right_side - apply_padded(partial_value, trim_faces(face_wide, depth), 1.0)
    iterate = trim_cells(partial_value, 1)
    coarse_right = restrict(leftover)
    coarse_coef = restrict(coefficient)
    rights = [coarse_right]
    face_sets = []
    iterates = []
    for level_no in range(1, LEVELS):
        factor = 0.25**level_no
        face_set = face_terms(spread_halo(coarse_coef))
        face_sets.append(face_set)
        current = smooth(rights[-1], None, face_set, factor, spread_halo)
        iterates.append(current)
        if level_no < LEVELS - 1:
            remains = rights[-1] - apply_padded(spread_halo(current), face_set, factor)
            rights.append(restrict(remains))
            coarse_coef = restrict(coarse_coef)
    level_no = 1
    slot_no = level_no - 1
    iterates[slot_no] = smooth(
        rights[slot_no],
        iterates[slot_no] + prolong(iterates[slot_no + 1]),
        face_sets[slot_no],
        0.25**level_no,
        spread_halo,
    )
    correction = iterates[0]
    start = iterate + prolong(correction)
    start_wide = extended(start, (("gx", 0), ("gy", 1), ("gz", 2)), depth)
    solution, lost = deep_smooth(right_wide, start_wide, face_wide, valid_wide)
    residual = right_side - apply_padded(fine_halo(solution), fine_set, 1.0)
    return (solution, residual)


def smoothing_weights():
    centre = 0.5 * (cheb_high + cheb_low)
    half_width = 0.5 * (cheb_high - cheb_low)
    sigma_val = centre / half_width
    rho_now = 1.0 / sigma_val
    weights = [(0.0, 1.0 / centre)]
    for _ in range(DEGREE - 1):
        rho_next = 1.0 / (2.0 * sigma_val - rho_now)
        weights.append((rho_next * rho_now, 2.0 * rho_next / half_width))
        rho_now = rho_next
    return weights


def turn(values, shift, axis):
    return pltpu.roll(values, shift % values.shape[axis], axis)


def set_faces(coef, face_x, face_y, face_z, inverse, count, scale):
    half = 0.5 * scale

    def body(i, below):
        here = coef[i + 1]
        above = half * (here + coef[i + 2])
        along_y = half * (here + turn(here, -1, 0))
        along_z = half * (here + turn(here, -1, 1))
        face_x[i + 1] = above
        face_y[i] = along_y
        face_z[i] = along_z
        diagonal = (below + above) + (along_y + turn(along_y, 1, 0)) + (along_z + turn(along_z, 1, 1))
        inverse[i] = jnp.where(here > 0.0, 1.0 / jnp.where(here > 0.0, diagonal, 1.0), 0.0)
        return above

    first = half * coef[1]
    face_x[0] = first
    lax.fori_loop(0, count, body, first)


def sweep_over(low, high, values, face_x, face_y, face_z, use):
    def body(i, carry):
        here, flux_low = carry
        above = values[i + 2]
        flux_high = face_x[i + 1] * (above - here)
        flux_y = face_y[i] * (turn(here, -1, 0) - here)
        flux_z = face_z[i] * (turn(here, -1, 1) - here)
        applied = (flux_low - flux_high) + (turn(flux_y, 1, 0) - flux_y) + (turn(flux_z, 1, 1) - flux_z)
        use(i, applied, here)
        return above, flux_high

    here = values[low + 1]
    lax.fori_loop(low, high, body, (here, face_x[low] * (here - values[low])))


def smooth_from_zero(count, right, values, update, inverse):
    first = smoothing_weights()[0][1]

    def body(i, carry):
        step = right[i] * (inverse[i] * first)
        update[i] = step
        values[i + 1] = step
        return carry

    lax.fori_loop(0, count, body, 0)


def smooth_sweep(low, high, weight, right, values, update, faces, inverse):
    keep, gain = weight

    def use(i, applied, here):
        step = (right[i] - applied) * (inverse[i] * gain)
        if keep:
            step = keep * update[i] + step
        update[i] = step
        values[i + 1] = here + step

    sweep_over(low, high, values, *faces, use)


def exact_dot(left, right):
    return jnp.dot(left, right, precision=lax.Precision.HIGHEST, preferred_element_type=jnp.float32)


def pairing(rows, columns, weight, period, along_rows):
    row = lax.broadcasted_iota(jnp.int32, (rows, columns), 0)
    column = lax.broadcasted_iota(jnp.int32, (rows, columns), 1)
    if along_rows:
        hit = row // 2 == column % period
    else:
        hit = column // 2 == row
    return jnp.where(hit, weight, 0.0).astype(jnp.float32)


def pair_rows(ref, count):
    return ref[pl.ds(0, count, stride=2), :] + ref[pl.ds(1, count, stride=2), :]


def down_kernel(
    pos, own, prev, nxt, sib, mid,
    start_out, right_out, coef_out, pay_out, edge_out,
    coef, right, face_x, face_y, face_z, inverse, values, update, sums0, sums1, coarse
):
    count_x, rows, lanes = right.shape
    by = rows // 3
    bz = lanes // 2
    core, odd, _, _ = pos[0], pos[1], pos[2], pos[3]
    from_sib = (lax.broadcasted_iota(jnp.int32, (rows, bz), 1) < bz // 2) == (core == 0)
    zero = jnp.zeros((rows, lanes), jnp.float32)
    coef[0] = zero
    coef[count_x + 1] = zero
    values[0] = zero
    values[count_x + 1] = zero

    def assemble(i, carry):
        middle = mid[i]
        for which in (0, 1):
            main = jnp.concatenate([prev[which, i], own[which, i], nxt[which, i]], axis=0)
            far = middle if which == 0 else turn(middle, bz // 2, 1)
            side = jnp.where(from_sib, sib[which, i], far)
            if which == 0:
                right[i, :, :bz] = main
                right[i, :, bz:] = side
            else:
                coef[i + 1, :, :bz] = main
                coef[i + 1, :, bz:] = side
        return carry

    lax.fori_loop(0, count_x, assemble, 0)
    set_faces(coef, face_x, face_y, face_z, inverse, count_x, 1.0)
    faces = (face_x, face_y, face_z)
    weights = smoothing_weights()
    smooth_from_zero(count_x, right, values, update, inverse)
    for weight in weights[1:]:
        smooth_sweep(0, count_x, weight, right, values, update, faces, inverse)

    def leftover(i, applied, here):
        left = right[i] - applied
        update[i] = left

    sweep_over(0, count_x, values, *faces, leftover)

    half = rows // 2
    for j in range(count_x // 2):
        for slot, pair in enumerate(
            (update[2 * j] + update[2 * j + 1], coef[2 * j + 1] + coef[2 * j + 2])
        ):
            at = slot * (count_x // 2) + j
            sums0[at * rows : (at + 1) * rows, :] = pair[:, :bz]
            sums1[at * rows : (at + 1) * rows, :] = pair[:, bz:]
    matrix = pairing(lanes, bz, 0.125, bz, True)
    total = count_x * half
    coarse[...] = exact_dot(pair_rows(sums0, total), matrix[:bz]) + exact_dot(
        pair_rows(sums1, total), matrix[bz:]
    )
    edge = by // 4
    for slot in (0, 1):
        for j in range(count_x // 2):
            at = (slot * (count_x // 2) + j) * half
            block = coarse[at + edge : at + edge + by, :]
            pay_out[slot, j] = block
            edge_out[slot, j] = jnp.where(odd == 1, block[by // 2 :], block[: by // 2])

    def copy_out(i, carry):
        window = pl.ds(by // 2, 2 * by)
        start_out[i] = values[i + 1, window, :]
        right_out[i] = right[i, window, :]
        coef_out[i] = coef[i + 1, window, :]
        return carry

    lax.fori_loop(0, count_x, copy_out, 0)


def up_kernel(
    pos, pay, far, near, start, right, coef_in,
    solution_out, residual_out,
    coef1, right1, fx1, fy1, fz1, inverse1, values1, update1,
    coef2, right2, fx2, fy2, fz2, inverse2, values2, update2,
    sums, wide0, wide1,
    coef, face_x, face_y, face_z, inverse, values, update,
):
    count_x, rows, lanes = right.shape
    by = rows // 2
    bz = lanes // 2
    n1, rows1, _ = right1.shape
    n2, rows2, _ = right2.shape
    odd, upper, at_x = pos[1], pos[2], pos[3]
    weights = smoothing_weights()
    zero1 = jnp.zeros((rows1, bz), jnp.float32)
    zero2 = jnp.zeros((rows2, bz), jnp.float32)
    zero = jnp.zeros((rows, lanes), jnp.float32)
    for ref in (coef1, values1):
        ref[0] = zero1
        ref[n1 + 1] = zero1
    for ref in (coef2, values2):
        ref[0] = zero2
        ref[n2 + 1] = zero2
    for ref in (coef, values):
        ref[0] = zero
        ref[count_x + 1] = zero

    blank = jnp.zeros((by // 2, bz), jnp.float32)
    for j in range(n1):
        for which in (0, 1):
            mine, other, side = pay[which, j], far[which, j], near[which, j]
            whole = jnp.concatenate(
                [
                    jnp.where(upper == 1, other, mine),
                    jnp.where(upper == 1, mine, other),
                    jnp.where(odd == 1, blank, side),
                    jnp.where(odd == 1, side, blank),
                ],
                axis=0,
            )
            if which == 0:
                right1[j] = whole
            else:
                coef1[j + 1] = whole

    faces1 = (fx1, fy1, fz1)
    set_faces(coef1, fx1, fy1, fz1, inverse1, n1, 0.25)
    smooth_from_zero(n1, right1, values1, update1, inverse1)
    for weight in weights[1:]:
        smooth_sweep(0, n1, weight, right1, values1, update1, faces1, inverse1)

    def leftover1(i, applied, here):
        update1[i] = right1[i] - applied

    sweep_over(0, n1, values1, *faces1, leftover1)
    for j in range(n2):
        for slot, pair in enumerate(
            (update1[2 * j] + update1[2 * j + 1], coef1[2 * j + 1] + coef1[2 * j + 2])
        ):
            at = slot * n2 + j
            sums[at * rows1 : (at + 1) * rows1, :] = pair
    lower = exact_dot(pair_rows(sums, n1 * rows2), pairing(bz, bz, 0.125, bz // 2, True))
    for j in range(n2):
        right2[j] = lower[j * rows2 : (j + 1) * rows2]
        coef2[j + 1] = lower[(n2 + j) * rows2 : (n2 + j + 1) * rows2]

    faces2 = (fx2, fy2, fz2)
    set_faces(coef2, fx2, fy2, fz2, inverse2, n2, 0.0625)
    smooth_from_zero(n2, right2, values2, update2, inverse2)
    for weight in weights[1:]:
        smooth_sweep(0, n2, weight, right2, values2, update2, faces2, inverse2)

    stacked = jnp.concatenate([values2[j + 1] for j in range(n2)], axis=0)
    spread = exact_dot(stacked, pairing(bz, bz, 1.0, bz, False))
    sums[pl.ds(0, n2 * rows2, stride=2), :] = spread
    sums[pl.ds(1, n2 * rows2, stride=2), :] = spread
    for j in range(n1):
        values1[j + 1] = values1[j + 1] + sums[(j // 2) * rows1 : (j // 2 + 1) * rows1, :]
    for weight in weights:
        smooth_sweep(0, n1, weight, right1, values1, update1, faces1, inverse1)

    def copy_in(i, carry):
        coef[i + 1] = coef_in[i]
        return carry

    lax.fori_loop(0, count_x, copy_in, 0)
    faces = (face_x, face_y, face_z)
    set_faces(coef, face_x, face_y, face_z, inverse, count_x, 1.0)
    stacked = jnp.concatenate(
        [
            jnp.where(upper == 1, values1[j + 1, by : 2 * by, :], values1[j + 1, :by, :])
            for j in range(n1)
        ],
        axis=0,
    )
    matrix = pairing(bz, lanes, 1.0, bz, False)
    spread0 = exact_dot(stacked, matrix[:, :bz])
    spread1 = exact_dot(stacked, matrix[:, bz:])
    for wide, spread in ((wide0, spread0), (wide1, spread1)):
        wide[pl.ds(0, n1 * by, stride=2), :] = spread
        wide[pl.ds(1, n1 * by, stride=2), :] = spread
    for j in range(n1):
        part = slice(j * rows, (j + 1) * rows)
        for i in (2 * j, 2 * j + 1):
            values[i + 1, :, :bz] = start[i, :, :bz] + wide0[part, :]
            values[i + 1, :, bz:] = start[i, :, bz:] + wide1[part, :]
    bx = count_x // 2
    for number, weight in enumerate(weights):
        reach = DEGREE - number
        low = jnp.where(at_x == 0, 0, bx - reach)
        high = jnp.where(at_x == 0, bx + reach, count_x)
        smooth_sweep(low, high, weight, right, values, update, faces, inverse)

    inner = slice(by // 2, by // 2 + by)
    base = at_x * bx

    def finish(i, applied, here):
        left = right[i] - applied
        solution_out[i - base] = here[inner, :bz]
        residual_out[i - base] = left[inner, :bz]

    sweep_over(base, base + bx, values, *faces, finish)


def vmem(*shape):
    return pltpu.VMEM(shape, jnp.float32)


def per_device_two_rounds(right_side, coefficient):
    bx, by, bz = right_side.shape
    at_x, at_y, at_z = (lax.axis_index(name) for name in ("gx", "gy", "gz"))
    core = at_z % 2
    pos = jnp.stack([core, at_y % 2, at_y // 2, at_x]).astype(jnp.int32)
    mine = jnp.stack([right_side, coefficient])
    other = lax.ppermute(mine, "gx", [(0, 1), (1, 0)])
    own = jnp.where(
        at_x == 0,
        jnp.concatenate([mine, other], axis=1),
        jnp.concatenate([other, mine], axis=1),
    )
    count_y = lax.axis_size("gy")
    forward = [(i, i + 1) for i in range(count_y - 1)]
    prev = lax.ppermute(own, "gy", forward)
    nxt = lax.ppermute(own, "gy", [(b, a) for a, b in forward])
    tall = jnp.concatenate([prev, own, nxt], axis=2)
    half = bz // 2
    packed = jnp.where(
        core == 0,
        jnp.concatenate([tall[0, :, :, :half], tall[1, :, :, :half]], axis=2),
        jnp.concatenate([tall[1, :, :, half:], tall[0, :, :, half:]], axis=2),
    )
    mid = lax.ppermute(packed, "gz", [(1, 2), (2, 1)])
    sib = lax.ppermute(tall, "gz", [(0, 1), (1, 0), (2, 3), (3, 2)])
    nx = 2 * bx
    rows = 3 * by
    lanes = 2 * bz
    in_smem = pl.BlockSpec(memory_space=pltpu.SMEM)
    in_vmem = pl.BlockSpec(memory_space=pltpu.VMEM)
    window = jax.ShapeDtypeStruct((nx, 2 * by, lanes), jnp.float32)
    start, right_wide, coef_wide, pay, edge = pl.pallas_call(
        down_kernel,
        out_shape=(
            window,
            window,
            window,
            jax.ShapeDtypeStruct((2, bx, by, bz), jnp.float32),
            jax.ShapeDtypeStruct((2, bx, by // 2, bz), jnp.float32),
        ),
        in_specs=[in_smem] + [in_vmem] * 5,
        out_specs=(in_vmem,) * 5,
        scratch_shapes=[
            vmem(nx + 2, rows, lanes),
            vmem(nx, rows, lanes),
            vmem(nx + 1, rows, lanes),
            vmem(nx, rows, lanes),
            vmem(nx, rows, lanes),
            vmem(nx, rows, lanes),
            vmem(nx + 2, rows, lanes),
            vmem(nx, rows, lanes),
            vmem(nx * rows, bz),
            vmem(nx * rows, bz),
            vmem(nx * rows // 2, bz),
        ],
        compiler_params=pltpu.CompilerParams(vmem_limit_bytes=40 * 2**20),
        name="down",
    )(pos, own, prev, nxt, sib, mid)
    far = lax.ppermute(pay, "gy", [(0, 2), (2, 0), (1, 3), (3, 1)])
    near = lax.ppermute(edge, "gy", [(0, 1), (3, 2)])

    def level_scratch(n, r, l, with_right):
        return [
            vmem(n + 2, r, l),
            *([vmem(n, r, l)] if with_right else []),
            vmem(n + 1, r, l),
            vmem(n, r, l),
            vmem(n, r, l),
            vmem(n, r, l),
            vmem(n + 2, r, l),
            vmem(n, r, l),
        ]

    return pl.pallas_call(
        up_kernel,
        out_shape=(jax.ShapeDtypeStruct((bx, by, bz), jnp.float32),) * 2,
        in_specs=[in_smem] + [in_vmem] * 6,
        out_specs=(in_vmem,) * 2,
        scratch_shapes=[
            *level_scratch(bx, rows, bz, True),
            *level_scratch(bx // 2, rows // 2, bz, True),
            vmem(bx * rows, bz),
            vmem(bx * 2 * by, bz),
            vmem(bx * 2 * by, bz),
            *level_scratch(nx, 2 * by, lanes, False),
        ],
        compiler_params=pltpu.CompilerParams(vmem_limit_bytes=40 * 2**20),
        name="up",
    )(pos, pay, far, near, start, right_wide, coef_wide)


def two_rounds_fit(mesh, shape):
    counts = tuple(mesh.shape[name] for name in ("gx", "gy", "gz"))
    bx, by, bz = (size // count for size, count in zip(shape, counts))
    edge = by // 4
    reach_coarse = 4 * DEGREE + 2
    return (
        counts == (2, 4, 4)
        and LEVELS == 3
        and bx % 4 == 0
        and by % 16 == 0
        and bz % 128 == 0
        and bz == 128
        and 2 * edge + DEGREE + 1 <= by
        and by // 2 + reach_coarse <= 2 * by - edge
        and 2 * reach_coarse + DEGREE + 1 <= bz // 2
    )


def solution(mesh):
    in_specs = (P("gx", "gy", "gz"), P("gx", "gy", "gz"))
    out_specs = (P("gx", "gy", "gz"), P("gx", "gy", "gz"))

    def whole(right_side, coefficient):
        fits = two_rounds_fit(mesh, right_side.shape)
        return jax.shard_map(
            per_device_two_rounds if fits else per_device,
            mesh=mesh,
            in_specs=in_specs,
            out_specs=out_specs,
            check_vma=False,
        )(right_side, coefficient)

    return whole
```

```python
import jax
import jax.numpy as jnp
from jax import lax
from jax.experimental import pallas as pl
from jax.experimental.pallas import tpu as pltpu
from jax.sharding import PartitionSpec as P

LEVELS = 3
DEGREE = 4


cheb_low = 0.3
cheb_high = 2.0


def extended(block, sides, width):
    for axis, dim in sides:
        count = lax.axis_size(axis)
        forward = [(i, i + 1) for i in range(count - 1)]
        backward = [(target, source) for source, target in forward]
        low = lax.ppermute(
            lax.slice_in_dim(block, block.shape[dim] - width, None, axis=dim), axis, forward
        )
        high = lax.ppermute(lax.slice_in_dim(block, 0, width, axis=dim), axis, backward)
        block = jnp.concatenate([low, block, high], axis=dim)
    return block


def face_terms(padded):
    face_x = 0.5 * (padded[1:, 1:-1, 1:-1] + padded[:-1, 1:-1, 1:-1])
    face_y = 0.5 * (padded[1:-1, 1:, 1:-1] + padded[1:-1, :-1, 1:-1])
    face_z = 0.5 * (padded[1:-1, 1:-1, 1:] + padded[1:-1, 1:-1, :-1])
    diagonal = (
        face_x[1:]
        + face_x[:-1]
        + face_y[:, 1:]
        + face_y[:, :-1]
        + face_z[:, :, 1:]
        + face_z[:, :, :-1]
    )
    return (face_x, face_y, face_z, diagonal)


def apply_padded(padded, face_set, factor):
    face_x, face_y, face_z, diagonal = face_set
    flux_x = face_x * (padded[1:, 1:-1, 1:-1] - padded[:-1, 1:-1, 1:-1])
    flux_y = face_y * (padded[1:-1, 1:, 1:-1] - padded[1:-1, :-1, 1:-1])
    flux_z = face_z * (padded[1:-1, 1:-1, 1:] - padded[1:-1, 1:-1, :-1])
    result = (
        flux_x[:-1]
        - flux_x[1:]
        + (flux_y[:, :-1] - flux_y[:, 1:])
        + (flux_z[:, :, :-1] - flux_z[:, :, 1:])
    )
    return factor * result


def fine_halo(values):
    return extended(values, (("gx", 0), ("gy", 1), ("gz", 2)), 1)


def spread_halo(values):
    return extended(values, (("gx", 0), ("gy", 1), ("gz", 2)), 1)


def restrict(values):
    size_x, size_y, size_z = values.shape
    blocks = values.reshape(size_x // 2, 2, size_y // 2, 2, size_z // 2, 2)
    return jnp.mean(blocks, axis=(1, 3, 5))


def prolong(values):
    size_x, size_y, size_z = values.shape
    spread = jnp.broadcast_to(values[:, None, :, None, :, None], (size_x, 2, size_y, 2, size_z, 2))
    return spread.reshape(2 * size_x, 2 * size_y, 2 * size_z)


def trim_cells(values, layers):
    return values[
        layers : values.shape[0] - layers,
        layers : values.shape[1] - layers,
        layers : values.shape[2] - layers,
    ]


def trim_faces(face_set, layers):
    return tuple((trim_cells(member, layers) for member in face_set))


def inside_mask(shape, margin):
    count_x = shape[0]
    count_y = shape[1]
    count_z = shape[2]
    along_x = lax.axis_index("gx") * count_x + jnp.arange(
        -margin, count_x + margin, dtype=jnp.int32
    )
    along_y = lax.axis_index("gy") * count_y + jnp.arange(
        -margin, count_y + margin, dtype=jnp.int32
    )
    along_z = lax.axis_index("gz") * count_z + jnp.arange(
        -margin, count_z + margin, dtype=jnp.int32
    )
    valid_x = (along_x >= 0) & (along_x < count_x * lax.axis_size("gx"))
    valid_y = (along_y >= 0) & (along_y < count_y * lax.axis_size("gy"))
    valid_z = (along_z >= 0) & (along_z < count_z * lax.axis_size("gz"))
    return valid_x[:, None, None] & valid_y[None, :, None] & valid_z[None, None, :]


def deep_smooth(right_wide, start_wide, face_wide, valid_wide):
    centre = 0.5 * (cheb_high + cheb_low)
    half_width = 0.5 * (cheb_high - cheb_low)
    sigma_val = centre / half_width
    rho_now = 1.0 / sigma_val
    safe_diag = jnp.where(valid_wide, face_wide[3], 1.0)
    if start_wide is None:
        update = jnp.where(valid_wide, right_wide / (1.0 * safe_diag) / centre, 0.0)
        iterate = update
        lost = 0
    else:
        leftover = trim_cells(right_wide, 1) - apply_padded(
            start_wide, trim_faces(face_wide, 1), 1.0
        )
        update = jnp.where(
            trim_cells(valid_wide, 1), leftover / (1.0 * trim_cells(safe_diag, 1)) / centre, 0.0
        )
        iterate = trim_cells(start_wide, 1) + update
        lost = 1
    for sweep_no in range(DEGREE - 1):
        lost = lost + 1
        leftover = trim_cells(right_wide, lost) - apply_padded(
            iterate, trim_faces(face_wide, lost), 1.0
        )
        rho_next = 1.0 / (2.0 * sigma_val - rho_now)
        fresh = rho_next * rho_now * trim_cells(update, 1) + 2.0 * rho_next / half_width * (
            leftover / (1.0 * trim_cells(safe_diag, lost))
        )
        update = jnp.where(trim_cells(valid_wide, lost), fresh, 0.0)
        iterate = trim_cells(iterate, 1) + update
        rho_now = rho_next
    return (iterate, lost)


def smooth(right, initial, face_set, factor, padder):
    diagonal = face_set[3]
    centre = 0.5 * (cheb_high + cheb_low)
    half_width = 0.5 * (cheb_high - cheb_low)
    sigma_val = centre / half_width
    rho_now = 1.0 / sigma_val
    if initial is None:
        iterate = jnp.zeros_like(right)
        leftover = right
    else:
        iterate = initial
        leftover = right - apply_padded(padder(initial), face_set, factor)
    update = leftover / (factor * diagonal) / centre
    iterate = iterate + update
    for sweep_no in range(DEGREE - 1):
        leftover = right - apply_padded(padder(iterate), face_set, factor)
        rho_next = 1.0 / (2.0 * sigma_val - rho_now)
        update = rho_next * rho_now * update + 2.0 * rho_next / half_width * (
            leftover / (factor * diagonal)
        )
        iterate = iterate + update
        rho_now = rho_next
    return iterate


def per_device(right_side, coefficient):
    depth = DEGREE
    stacked = jnp.stack([right_side, coefficient])
    widened = extended(stacked, (("gx", 1), ("gy", 2), ("gz", 3)), depth + 1)
    right_wide = trim_cells(widened[0], 1)
    face_wide = face_terms(widened[1])
    valid_wide = inside_mask(right_side.shape, depth)
    fine_set = trim_faces(face_wide, depth)
    partial_value, lost = deep_smooth(right_wide, None, face_wide, valid_wide)
    leftover = right_side - apply_padded(partial_value, trim_faces(face_wide, depth), 1.0)
    iterate = trim_cells(partial_value, 1)
    coarse_right = restrict(leftover)
    coarse_coef = restrict(coefficient)
    rights = [coarse_right]
    face_sets = []
    iterates = []
    for level_no in range(1, LEVELS):
        factor = 0.25**level_no
        face_set = face_terms(spread_halo(coarse_coef))
        face_sets.append(face_set)
        current = smooth(rights[-1], None, face_set, factor, spread_halo)
        iterates.append(current)
        if level_no < LEVELS - 1:
            remains = rights[-1] - apply_padded(spread_halo(current), face_set, factor)
            rights.append(restrict(remains))
            coarse_coef = restrict(coarse_coef)
    level_no = 1
    slot_no = level_no - 1
    iterates[slot_no] = smooth(
        rights[slot_no],
        iterates[slot_no] + prolong(iterates[slot_no + 1]),
        face_sets[slot_no],
        0.25**level_no,
        spread_halo,
    )
    correction = iterates[0]
    start = iterate + prolong(correction)
    start_wide = extended(start, (("gx", 0), ("gy", 1), ("gz", 2)), depth)
    solution, lost = deep_smooth(right_wide, start_wide, face_wide, valid_wide)
    residual = right_side - apply_padded(fine_halo(solution), fine_set, 1.0)
    return (solution, residual)


UNROLL_FINE = 4
UNROLL_COARSE = 16


def smoothing_weights():
    centre = 0.5 * (cheb_high + cheb_low)
    half_width = 0.5 * (cheb_high - cheb_low)
    sigma_val = centre / half_width
    rho_now = 1.0 / sigma_val
    weights = [(0.0, 1.0 / centre)]
    for _ in range(DEGREE - 1):
        rho_next = 1.0 / (2.0 * sigma_val - rho_now)
        weights.append((rho_next * rho_now, 2.0 * rho_next / half_width))
        rho_now = rho_next
    return weights


def turn(values, shift, axis):
    return pltpu.roll(values, shift % values.shape[axis], axis)


def run(low, count, body, carry, unroll):
    unroll = min(unroll, count)

    def several(step, state):
        for k in range(unroll):
            state = body(low + step * unroll + k, state)
        return state

    if count // unroll == 1:
        carry = several(0, carry)
    else:
        carry = lax.fori_loop(0, count // unroll, several, carry)
    for k in range(count // unroll * unroll, count):
        carry = body(low + k, carry)
    return carry


class Level:
    def __init__(self, refs, split_y, split_z, step, scale, unroll):
        self.coef, self.right, self.face_x, self.face_y, self.face_z, self.inverse, self.values, self.update = refs
        self.count = self.face_y.shape[1]
        self.parts = self.face_y.shape[0]
        self.split_y, self.split_z, self.step = split_y, split_z, step
        self.half, self.unroll = 0.5 * scale, unroll
        self.pairs_z = 2 if split_z else 1

    def read(self, ref, i):
        return [ref[part, i] for part in range(self.parts)]

    def write(self, ref, i, values):
        for part in range(self.parts):
            ref[part, i] = values[part]

    def clear_ends(self):
        zero = jnp.zeros(self.coef.shape[2:], jnp.float32)
        for part in range(self.parts):
            for ref in (self.coef, self.values):
                ref[part, 0] = zero
                ref[part, self.count + 1] = zero

    def next_y(self, v, part):
        if not self.split_y:
            return turn(v[part], -1, 0)
        if part < self.pairs_z:
            return v[part + self.pairs_z]
        return turn(v[part - self.pairs_z], -1, 0)

    def last_y(self, v, part):
        if not self.split_y:
            return turn(v[part], 1, 0)
        if part < self.pairs_z:
            return turn(v[part + self.pairs_z], 1, 0)
        return v[part - self.pairs_z]

    def next_z(self, v, part):
        if not self.split_z:
            return turn(v[part], -self.step, 1)
        if part % 2 == 0:
            return v[part + 1]
        return turn(v[part - 1], -1, 1)

    def last_z(self, v, part):
        if not self.split_z:
            return turn(v[part], self.step, 1)
        if part % 2 == 0:
            return turn(v[part + 1], 1, 1)
        return v[part - 1]

    def set_faces(self, use):
        half = self.half
        parts = range(self.parts)

        def body(i, carry):
            here, below = carry
            above = self.read(self.coef, i + 2)
            upper = [half * (here[p] + above[p]) for p in parts]
            along_y = [half * (here[p] + self.next_y(here, p)) for p in parts]
            along_z = [half * (here[p] + self.next_z(here, p)) for p in parts]
            inverse = []
            for p in parts:
                diagonal = (
                    (below[p] + upper[p])
                    + (along_y[p] + self.last_y(along_y, p))
                    + (along_z[p] + self.last_z(along_z, p))
                )
                inside = here[p] > 0.0
                inverse.append(jnp.where(inside, 1.0 / jnp.where(inside, diagonal, 1.0), 0.0))
            self.write(self.face_x, i + 1, upper)
            self.write(self.face_y, i, along_y)
            self.write(self.face_z, i, along_z)
            self.write(self.inverse, i, inverse)
            use(i, here, inverse)
            return above, upper

        here = self.read(self.coef, 1)
        first = [half * here[p] for p in parts]
        self.write(self.face_x, 0, first)
        run(0, self.count, body, (here, first), self.unroll)

    def sweep(self, low, count, use):
        parts = range(self.parts)

        def body(i, carry):
            here, flux_low = carry
            above = self.read(self.values, i + 2)
            face_x, face_y, face_z = (self.read(ref, at) for ref, at in ((self.face_x, i + 1), (self.face_y, i), (self.face_z, i)))
            flux_high = [face_x[p] * (above[p] - here[p]) for p in parts]
            flux_y = [face_y[p] * (self.next_y(here, p) - here[p]) for p in parts]
            flux_z = [face_z[p] * (self.next_z(here, p) - here[p]) for p in parts]
            applied = [
                (flux_low[p] - flux_high[p])
                + (self.last_y(flux_y, p) - flux_y[p])
                + (self.last_z(flux_z, p) - flux_z[p])
                for p in parts
            ]
            use(i, applied, here)
            return above, flux_high

        here = self.read(self.values, low + 1)
        before = self.read(self.values, low)
        face = self.read(self.face_x, low)
        run(low, count, body, (here, [face[p] * (here[p] - before[p]) for p in parts]), self.unroll)

    def from_zero(self, i, inverse):
        first = smoothing_weights()[0][1]
        right = self.read(self.right, i)
        step = [right[p] * (inverse[p] * first) for p in range(self.parts)]
        self.write(self.update, i, step)
        self.write(self.values, i + 1, step)

    def smooth(self, low, count, weight):
        keep, gain = weight

        def use(i, applied, here):
            right = self.read(self.right, i)
            inverse = self.read(self.inverse, i)
            step = [(right[p] - applied[p]) * (inverse[p] * gain) for p in range(self.parts)]
            if keep:
                update = self.read(self.update, i)
                step = [keep * update[p] + step[p] for p in range(self.parts)]
            self.write(self.update, i, step)
            self.write(self.values, i + 1, [here[p] + step[p] for p in range(self.parts)])

        self.sweep(low, count, use)


def total(items):
    items = list(items)
    while len(items) > 1:
        items = [sum(items[k : k + 2][1:], items[k]) for k in range(0, len(items), 2)]
    return items[0]


def exact_dot(left, right):
    return jnp.dot(left, right, precision=lax.Precision.HIGHEST, preferred_element_type=jnp.float32)


def parity_matrix(size, back):
    row = lax.broadcasted_iota(jnp.int32, (size, size), 0)
    column = lax.broadcasted_iota(jnp.int32, (size, size), 1)
    if back:
        row, column = column, row
    hit = column == row // 2 + (row % 2) * (size // 2)
    return jnp.where(hit, 1.0, 0.0).astype(jnp.float32)


def split_kernel(right_side, coefficient, out, rows):
    bx, by, bz = right_side.shape
    matrix = parity_matrix(bz, False)
    for which, ref in enumerate((right_side, coefficient)):
        rows[...] = exact_dot(ref[...].reshape(bx * by, bz), matrix)
        for odd in (0, 1):
            out[which, odd] = rows[pl.ds(odd, bx * by // 2, stride=2), :].reshape(bx, by // 2, bz)


def down_kernel(pos, own, sib, mid, start_out, right_out, coef_out, pay_out, edge_out, *refs):
    level = Level(refs[:8], True, True, 1, 1.0, UNROLL_FINE)
    sums, coefs = refs[8:]
    bx, rows, bz = own.shape[3:]
    core, odd, at_x, middle_valid, next_valid = (pos[k] for k in (0, 1, 3, 4, 5))
    lane = lax.broadcasted_iota(jnp.int32, (rows, bz), 1)
    quarter = bz // 4
    is_own = lane < bz // 2
    is_sib = (lane < 3 * quarter) == (core == 0)
    level.clear_ends()

    for block in range(6):
        at = at_x * bx if block in (0, 2, 3) else (1 - at_x) * bx
        row = {0: 1, 1: 1, 2: 2 * (1 - odd), 4: 2 * (1 - odd), 3: 2 * odd, 5: 2 * odd}[block] * rows
        if block > 1:
            row = pl.multiple_of(row, rows)
        window = pl.ds(row, rows)

        def assemble(x, carry, block=block, at=at, window=window):
            for odd_y in (0, 1):
                packed = mid[block, odd_y, x]
                once, back = turn(packed, quarter, 1), turn(packed, -quarter, 1)
                swapped = turn(packed, bz // 2, 1)
                for which in (0, 1):
                    mine = own[block, which, odd_y, x]
                    side = sib[block, which, odd_y, x]
                    if which == 0:
                        far = (swapped, packed)
                    else:
                        far = (jnp.where(core == 1, once, back), jnp.where(core == 1, back, once))
                        far = [jnp.where(middle_valid == 1, value, 0.0) for value in far]
                    for odd_z in (0, 1):
                        value = jnp.where(
                            is_own,
                            turn(mine, bz // 2, 1) if odd_z else mine,
                            jnp.where(is_sib, side if odd_z else turn(side, bz // 2, 1), far[odd_z]),
                        )
                        if which == 1 and block in (3, 5):
                            value = jnp.where(next_valid == 1, value, 0.0)
                        ref, shift = ((level.right, 0), (level.coef, 1))[which]
                        ref[2 * odd_y + odd_z, at + x + shift, window, :] = value
            return carry

        lax.fori_loop(0, bx, assemble, 0)

    def begin(i, here, inverse):
        level.from_zero(i, inverse)
        coefs[i] = total(here)

    level.set_faces(begin)
    for weight in smoothing_weights()[1:]:
        level.smooth(0, level.count, weight)

    def leftover(i, applied, here):
        right = level.read(level.right, i)
        sums[i] = total(right[p] - applied[p] for p in range(level.parts))

    level.sweep(0, level.count, leftover)

    edge = rows // 2
    upper_half = lax.broadcasted_iota(jnp.int32, (rows, bz), 0) < edge
    for which, ref in enumerate((sums, coefs)):
        for x in range(bx):
            ref[x] = 0.125 * (ref[2 * x] + ref[2 * x + 1])
            halves = [ref[x, pl.ds(edge + parity, rows, stride=2), :] for parity in (0, 1)]
            for parity in (0, 1):
                pay_out[which, parity, x] = halves[parity]
            edge_out[which, x] = jnp.where(
                upper_half,
                jnp.where(odd == 1, turn(halves[0], edge, 0), halves[0]),
                jnp.where(odd == 1, halves[1], turn(halves[1], edge, 0)),
            )

    window = pl.ds(edge, 2 * rows)

    def copy_out(i, carry):
        for part in range(level.parts):
            start_out[part, i] = turn(level.values[part, i + 1, window, :], -edge, 0)
            right_out[part, i] = turn(level.right[part, i, window, :], -edge, 0)
            coef_out[part, i] = turn(level.coef[part, i + 1, window, :], -edge, 0)
        return carry

    lax.fori_loop(0, level.count, copy_out, 0)


def up_kernel(pos, pay, far, near, start, right, coef_in, solution_out, residual_out, *refs):
    level1 = Level(refs[:8], True, False, 1, 0.25, UNROLL_COARSE)
    level2 = Level(refs[8:16], False, False, 2, 0.0625, UNROLL_COARSE)
    fine = Level((refs[16], right, *refs[17:23]), True, True, 1, 1.0, UNROLL_FINE)
    window, rows_out = refs[23:]
    n1, rows, bz = pay.shape[2:]
    edge = rows // 2
    odd, upper, at_x, near_valid = (pos[k] for k in (1, 2, 3, 6))
    weights = smoothing_weights()
    for level in (level1, level2, fine):
        level.clear_ends()

    top = lax.broadcasted_iota(jnp.int32, (rows, bz), 0) < edge
    near_here = (top == (odd == 0)) & (near_valid == 1)
    for j in range(n1):
        for which, (ref, shift) in enumerate(((level1.right, 0), (level1.coef, 1))):
            piece = near[which, j]
            other = turn(piece, edge, 0)
            for parity in (0, 1):
                mine, theirs = pay[which, parity, j], far[which, parity, j]
                ref[parity, j + shift, :rows] = jnp.where(upper == 1, theirs, mine)
                ref[parity, j + shift, rows : 2 * rows] = jnp.where(upper == 1, mine, theirs)
                if parity == 0:
                    side = jnp.where(odd == 0, piece, other)
                else:
                    side = jnp.where(odd == 0, other, piece)
                ref[parity, j + shift, 2 * rows :] = jnp.where(near_here, side, 0.0)

    even_lane = lax.broadcasted_iota(jnp.int32, (3 * rows, bz), 1) % 2 == 0

    def pair_lanes(values):
        return values + jnp.where(even_lane, turn(values, -1, 1), turn(values, 1, 1))

    coefs, sums = [], []

    def begin1(i, here, inverse):
        level1.from_zero(i, inverse)
        coefs.append(total(here))

    level1.set_faces(begin1)
    for weight in weights[1:]:
        level1.smooth(0, n1, weight)

    def leftover1(i, applied, here):
        values = level1.read(level1.right, i)
        sums.append(total(values[p] - applied[p] for p in range(level1.parts)))

    level1.sweep(0, n1, leftover1)
    for j in range(n1 // 2):
        level2.right[0, j] = 0.125 * pair_lanes(sums[2 * j] + sums[2 * j + 1])
        level2.coef[0, j + 1] = 0.125 * pair_lanes(coefs[2 * j] + coefs[2 * j + 1])

    level2.set_faces(lambda i, here, inverse: level2.from_zero(i, inverse))
    for weight in weights[1:]:
        level2.smooth(0, n1 // 2, weight)

    for j in range(n1):
        for parity in (0, 1):
            level1.values[parity, j + 1] = level1.values[parity, j + 1] + level2.values[0, j // 2 + 1]
    for weight in weights:
        level1.smooth(0, n1, weight)

    def copy_in(i, carry):
        for part in range(fine.parts):
            fine.coef[part, i + 1] = coef_in[part, i]
        return carry

    lax.fori_loop(0, fine.count, copy_in, 0)
    fine.set_faces(lambda i, here, inverse: None)
    for j in range(n1):
        for parity in (0, 1):
            rows_of = level1.values[parity, j + 1, :rows], level1.values[parity, j + 1, rows : 2 * rows]
            window[j, pl.ds(parity, rows, stride=2), :] = jnp.where(upper == 1, rows_of[1], rows_of[0])
        spread = turn(window[j], -edge, 0)
        for i in (2 * j, 2 * j + 1):
            for part in range(fine.parts):
                fine.values[part, i + 1] = start[part, i] + spread
    bx = fine.count // 2
    for number, weight in enumerate(weights):
        reach = DEGREE - number
        fine.smooth(jnp.where(at_x == 0, 0, bx - reach), bx + reach, weight)

    base = at_x * bx
    own_lane = lax.broadcasted_iota(jnp.int32, (rows, bz), 1) < bz // 2

    def finish(i, applied, here):
        values = fine.read(right, i)
        for slot, field in enumerate((here, [values[p] - applied[p] for p in range(fine.parts)])):
            for odd_y in (0, 1):
                even, other = field[2 * odd_y][:rows], field[2 * odd_y + 1][:rows]
                rows_out[slot, i - base, pl.ds(odd_y, rows, stride=2), :] = jnp.where(
                    own_lane, even, turn(other, bz // 2, 1)
                )

    fine.sweep(base, bx, finish)
    matrix = parity_matrix(bz, True)
    for slot, ref in enumerate((solution_out, residual_out)):
        ref[...] = exact_dot(rows_out[slot].reshape(bx * 2 * rows, bz), matrix).reshape(ref.shape)


def vmem(*shape):
    return pltpu.VMEM(shape, jnp.float32)


def level_scratch(parts, n, rows, lanes, with_right):
    tall, plain = vmem(parts, n + 2, rows, lanes), vmem(parts, n, rows, lanes)
    return [
        tall,
        *([plain] if with_right else []),
        vmem(parts, n + 1, rows, lanes),
        plain,
        plain,
        plain,
        tall,
        plain,
    ]


def per_device_two_rounds(right_side, coefficient):
    bx, by, bz = right_side.shape
    rows = by // 2
    at_x, at_y, at_z = (lax.axis_index(name) for name in ("gx", "gy", "gz"))
    core = at_z % 2
    middle_y, middle_z = ((at == 1) | (at == 2) for at in (at_y, at_z))
    pos = jnp.stack([core, at_y % 2, at_y // 2, at_x, middle_z, middle_y, middle_y]).astype(jnp.int32)
    in_smem = pl.BlockSpec(memory_space=pltpu.SMEM)
    in_vmem = pl.BlockSpec(memory_space=pltpu.VMEM)
    params = pltpu.CompilerParams(vmem_limit_bytes=24 * 2**20)
    shape = lambda *sizes: jax.ShapeDtypeStruct(sizes, jnp.float32)

    mine = pl.pallas_call(
        split_kernel,
        out_shape=shape(2, 2, bx, rows, bz),
        in_specs=[in_vmem] * 2,
        out_specs=in_vmem,
        scratch_shapes=[vmem(bx * by, bz)],
        compiler_params=params,
        name="split",
    )(right_side, coefficient)

    pairs = [1, 0, 3, 2]
    inner = [0, 2, 1, 3]
    across = [(0, 1), (1, 0)]

    def both(partner):
        return [(4 * x + y, 4 * (1 - x) + partner[y]) for x in (0, 1) for y in range(4)]

    blocks = jnp.stack(
        [
            mine,
            lax.ppermute(mine, "gx", across),
            lax.ppermute(mine, "gy", list(enumerate(pairs))),
            lax.ppermute(mine, "gy", list(enumerate(inner))),
            lax.ppermute(mine, ("gx", "gy"), both(pairs)),
            lax.ppermute(mine, ("gx", "gy"), both(inner)),
        ]
    )
    quarter = bz // 4
    low_quarter = jnp.arange(bz) % (bz // 2) < quarter
    right_blocks, coef_blocks = blocks[:, 0], blocks[:, 1]
    packed = jnp.where(
        core == 0,
        jnp.where(low_quarter, right_blocks, jnp.roll(coef_blocks, quarter, axis=-1)),
        jnp.where(low_quarter, jnp.roll(coef_blocks, -quarter, axis=-1), right_blocks),
    )
    mid = lax.ppermute(packed, "gz", list(enumerate(inner)))
    sib = lax.ppermute(blocks, "gz", list(enumerate(pairs)))

    nx = 2 * bx
    window = shape(4, nx, 2 * rows, bz)
    start, right_wide, coef_wide, pay, edge = pl.pallas_call(
        down_kernel,
        out_shape=(window, window, window, shape(2, 2, bx, rows, bz), shape(2, bx, rows, bz)),
        in_specs=[in_smem] + [in_vmem] * 3,
        out_specs=(in_vmem,) * 5,
        scratch_shapes=[
            *level_scratch(4, nx, 3 * rows, bz, True),
            vmem(nx, 3 * rows, bz),
            vmem(nx, 3 * rows, bz),
        ],
        compiler_params=params,
        name="down",
    )(pos, blocks, sib, mid)
    far = lax.ppermute(pay, "gy", [(0, 2), (2, 0), (1, 3), (3, 1)])
    near = lax.ppermute(edge, "gy", list(enumerate(pairs)))
    return pl.pallas_call(
        up_kernel,
        out_shape=(shape(bx, by, bz),) * 2,
        in_specs=[in_smem] + [in_vmem] * 6,
        out_specs=(in_vmem,) * 2,
        scratch_shapes=[
            *level_scratch(2, bx, 3 * rows, bz, True),
            *level_scratch(1, bx // 2, 3 * rows, bz, True),
            *level_scratch(4, nx, 2 * rows, bz, False),
            vmem(bx, 2 * rows, bz),
            vmem(2, bx, by, bz),
        ],
        compiler_params=params,
        name="up",
    )(pos, pay, far, near, start, right_wide, coef_wide)


def two_rounds_fit(mesh, shape):
    counts = tuple(mesh.shape[name] for name in ("gx", "gy", "gz"))
    bx, by, bz = (size // count for size, count in zip(shape, counts))
    edge = by // 4
    reach_coarse = 4 * DEGREE + 2
    return (
        counts == (2, 4, 4)
        and LEVELS == 3
        and bx % 4 == 0
        and by == 16
        and bz == 128
        and 2 * edge + DEGREE + 1 <= by
        and by // 2 + reach_coarse <= 2 * by - edge
        and 2 * reach_coarse + DEGREE + 1 <= bz // 2
    )


def solution(mesh):
    in_specs = (P("gx", "gy", "gz"), P("gx", "gy", "gz"))
    out_specs = (P("gx", "gy", "gz"), P("gx", "gy", "gz"))

    def whole(right_side, coefficient):
        fits = two_rounds_fit(mesh, right_side.shape)
        return jax.shard_map(
            per_device_two_rounds if fits else per_device,
            mesh=mesh,
            in_specs=in_specs,
            out_specs=out_specs,
            check_vma=False,
        )(right_side, coefficient)

    return whole
```

```python
import jax
import jax.numpy as jnp
from jax import lax
from jax.experimental import pallas as pl
from jax.experimental.pallas import tpu as pltpu
from jax.sharding import PartitionSpec as P

LEVELS = 3
DEGREE = 4


cheb_low = 0.3
cheb_high = 2.0


def extended(block, sides, width):
    for axis, dim in sides:
        count = lax.axis_size(axis)
        forward = [(i, i + 1) for i in range(count - 1)]
        backward = [(target, source) for source, target in forward]
        low = lax.ppermute(
            lax.slice_in_dim(block, block.shape[dim] - width, None, axis=dim), axis, forward
        )
        high = lax.ppermute(lax.slice_in_dim(block, 0, width, axis=dim), axis, backward)
        block = jnp.concatenate([low, block, high], axis=dim)
    return block


def face_terms(padded):
    face_x = 0.5 * (padded[1:, 1:-1, 1:-1] + padded[:-1, 1:-1, 1:-1])
    face_y = 0.5 * (padded[1:-1, 1:, 1:-1] + padded[1:-1, :-1, 1:-1])
    face_z = 0.5 * (padded[1:-1, 1:-1, 1:] + padded[1:-1, 1:-1, :-1])
    diagonal = (
        face_x[1:]
        + face_x[:-1]
        + face_y[:, 1:]
        + face_y[:, :-1]
        + face_z[:, :, 1:]
        + face_z[:, :, :-1]
    )
    return (face_x, face_y, face_z, diagonal)


def apply_padded(padded, face_set, factor):
    face_x, face_y, face_z, diagonal = face_set
    flux_x = face_x * (padded[1:, 1:-1, 1:-1] - padded[:-1, 1:-1, 1:-1])
    flux_y = face_y * (padded[1:-1, 1:, 1:-1] - padded[1:-1, :-1, 1:-1])
    flux_z = face_z * (padded[1:-1, 1:-1, 1:] - padded[1:-1, 1:-1, :-1])
    result = (
        flux_x[:-1]
        - flux_x[1:]
        + (flux_y[:, :-1] - flux_y[:, 1:])
        + (flux_z[:, :, :-1] - flux_z[:, :, 1:])
    )
    return factor * result


def fine_halo(values):
    return extended(values, (("gx", 0), ("gy", 1), ("gz", 2)), 1)


def spread_halo(values):
    return extended(values, (("gx", 0), ("gy", 1), ("gz", 2)), 1)


def restrict(values):
    size_x, size_y, size_z = values.shape
    blocks = values.reshape(size_x // 2, 2, size_y // 2, 2, size_z // 2, 2)
    return jnp.mean(blocks, axis=(1, 3, 5))


def prolong(values):
    size_x, size_y, size_z = values.shape
    spread = jnp.broadcast_to(values[:, None, :, None, :, None], (size_x, 2, size_y, 2, size_z, 2))
    return spread.reshape(2 * size_x, 2 * size_y, 2 * size_z)


def trim_cells(values, layers):
    return values[
        layers : values.shape[0] - layers,
        layers : values.shape[1] - layers,
        layers : values.shape[2] - layers,
    ]


def trim_faces(face_set, layers):
    return tuple((trim_cells(member, layers) for member in face_set))


def inside_mask(shape, margin):
    count_x = shape[0]
    count_y = shape[1]
    count_z = shape[2]
    along_x = lax.axis_index("gx") * count_x + jnp.arange(
        -margin, count_x + margin, dtype=jnp.int32
    )
    along_y = lax.axis_index("gy") * count_y + jnp.arange(
        -margin, count_y + margin, dtype=jnp.int32
    )
    along_z = lax.axis_index("gz") * count_z + jnp.arange(
        -margin, count_z + margin, dtype=jnp.int32
    )
    valid_x = (along_x >= 0) & (along_x < count_x * lax.axis_size("gx"))
    valid_y = (along_y >= 0) & (along_y < count_y * lax.axis_size("gy"))
    valid_z = (along_z >= 0) & (along_z < count_z * lax.axis_size("gz"))
    return valid_x[:, None, None] & valid_y[None, :, None] & valid_z[None, None, :]


def deep_smooth(right_wide, start_wide, face_wide, valid_wide):
    centre = 0.5 * (cheb_high + cheb_low)
    half_width = 0.5 * (cheb_high - cheb_low)
    sigma_val = centre / half_width
    rho_now = 1.0 / sigma_val
    safe_diag = jnp.where(valid_wide, face_wide[3], 1.0)
    if start_wide is None:
        update = jnp.where(valid_wide, right_wide / (1.0 * safe_diag) / centre, 0.0)
        iterate = update
        lost = 0
    else:
        leftover = trim_cells(right_wide, 1) - apply_padded(
            start_wide, trim_faces(face_wide, 1), 1.0
        )
        update = jnp.where(
            trim_cells(valid_wide, 1), leftover / (1.0 * trim_cells(safe_diag, 1)) / centre, 0.0
        )
        iterate = trim_cells(start_wide, 1) + update
        lost = 1
    for sweep_no in range(DEGREE - 1):
        lost = lost + 1
        leftover = trim_cells(right_wide, lost) - apply_padded(
            iterate, trim_faces(face_wide, lost), 1.0
        )
        rho_next = 1.0 / (2.0 * sigma_val - rho_now)
        fresh = rho_next * rho_now * trim_cells(update, 1) + 2.0 * rho_next / half_width * (
            leftover / (1.0 * trim_cells(safe_diag, lost))
        )
        update = jnp.where(trim_cells(valid_wide, lost), fresh, 0.0)
        iterate = trim_cells(iterate, 1) + update
        rho_now = rho_next
    return (iterate, lost)


def smooth(right, initial, face_set, factor, padder):
    diagonal = face_set[3]
    centre = 0.5 * (cheb_high + cheb_low)
    half_width = 0.5 * (cheb_high - cheb_low)
    sigma_val = centre / half_width
    rho_now = 1.0 / sigma_val
    if initial is None:
        iterate = jnp.zeros_like(right)
        leftover = right
    else:
        iterate = initial
        leftover = right - apply_padded(padder(initial), face_set, factor)
    update = leftover / (factor * diagonal) / centre
    iterate = iterate + update
    for sweep_no in range(DEGREE - 1):
        leftover = right - apply_padded(padder(iterate), face_set, factor)
        rho_next = 1.0 / (2.0 * sigma_val - rho_now)
        update = rho_next * rho_now * update + 2.0 * rho_next / half_width * (
            leftover / (factor * diagonal)
        )
        iterate = iterate + update
        rho_now = rho_next
    return iterate


def per_device(right_side, coefficient):
    depth = DEGREE
    stacked = jnp.stack([right_side, coefficient])
    widened = extended(stacked, (("gx", 1), ("gy", 2), ("gz", 3)), depth + 1)
    right_wide = trim_cells(widened[0], 1)
    face_wide = face_terms(widened[1])
    valid_wide = inside_mask(right_side.shape, depth)
    fine_set = trim_faces(face_wide, depth)
    partial_value, lost = deep_smooth(right_wide, None, face_wide, valid_wide)
    leftover = right_side - apply_padded(partial_value, trim_faces(face_wide, depth), 1.0)
    iterate = trim_cells(partial_value, 1)
    coarse_right = restrict(leftover)
    coarse_coef = restrict(coefficient)
    rights = [coarse_right]
    face_sets = []
    iterates = []
    for level_no in range(1, LEVELS):
        factor = 0.25**level_no
        face_set = face_terms(spread_halo(coarse_coef))
        face_sets.append(face_set)
        current = smooth(rights[-1], None, face_set, factor, spread_halo)
        iterates.append(current)
        if level_no < LEVELS - 1:
            remains = rights[-1] - apply_padded(spread_halo(current), face_set, factor)
            rights.append(restrict(remains))
            coarse_coef = restrict(coarse_coef)
    level_no = 1
    slot_no = level_no - 1
    iterates[slot_no] = smooth(
        rights[slot_no],
        iterates[slot_no] + prolong(iterates[slot_no + 1]),
        face_sets[slot_no],
        0.25**level_no,
        spread_halo,
    )
    correction = iterates[0]
    start = iterate + prolong(correction)
    start_wide = extended(start, (("gx", 0), ("gy", 1), ("gz", 2)), depth)
    solution, lost = deep_smooth(right_wide, start_wide, face_wide, valid_wide)
    residual = right_side - apply_padded(fine_halo(solution), fine_set, 1.0)
    return (solution, residual)


ORDER = (0, 1, 3, 5, 2, 4)
UNROLL_FINE = 4
UNROLL_COARSE = 16


def place():
    at_x, at_y, at_z = (lax.axis_index(name) for name in ("gx", "gy", "gz"))
    return at_x, at_y, at_z, lax.rem(at_z, 2), lax.rem(at_y, 2)


def in_the_middle(at):
    return (at == 1) | (at == 2)


def smoothing_weights():
    centre = 0.5 * (cheb_high + cheb_low)
    half_width = 0.5 * (cheb_high - cheb_low)
    sigma_val = centre / half_width
    rho_now = 1.0 / sigma_val
    weights = [(0.0, 1.0 / centre)]
    for _ in range(DEGREE - 1):
        rho_next = 1.0 / (2.0 * sigma_val - rho_now)
        weights.append((rho_next * rho_now, 2.0 * rho_next / half_width))
        rho_now = rho_next
    return weights


def turn(values, shift, axis):
    return pltpu.roll(values, shift % values.shape[axis], axis)


def run(low, count, body, carry, unroll):
    unroll = min(unroll, count)

    def several(step, state):
        for k in range(unroll):
            state = body(low + step * unroll + k, state)
        return state

    if count // unroll == 1:
        carry = several(0, carry)
    else:
        carry = lax.fori_loop(0, count // unroll, several, carry)
    for k in range(count // unroll * unroll, count):
        carry = body(low + k, carry)
    return carry


class Level:
    def __init__(self, refs, split_y, split_z, step, scale, unroll):
        self.coef, self.right, self.face_x, self.face_y, self.face_z, self.inverse, self.values, self.update = refs
        self.count = self.face_y.shape[1]
        self.parts = self.face_y.shape[0]
        self.split_y, self.split_z, self.step = split_y, split_z, step
        self.half, self.unroll = 0.5 * scale, unroll
        self.pairs_z = 2 if split_z else 1

    def read(self, ref, i):
        return [ref[part, i] for part in range(self.parts)]

    def write(self, ref, i, values):
        for part in range(self.parts):
            ref[part, i] = values[part]

    def clear_ends(self):
        zero = jnp.zeros(self.coef.shape[2:], jnp.float32)
        for part in range(self.parts):
            for ref in (self.coef, self.values):
                ref[part, 0] = zero
                ref[part, self.count + 1] = zero

    def next_y(self, v, part):
        if not self.split_y:
            return turn(v[part], -1, 0)
        if part < self.pairs_z:
            return v[part + self.pairs_z]
        return turn(v[part - self.pairs_z], -1, 0)

    def last_y(self, v, part):
        if not self.split_y:
            return turn(v[part], 1, 0)
        if part < self.pairs_z:
            return turn(v[part + self.pairs_z], 1, 0)
        return v[part - self.pairs_z]

    def next_z(self, v, part):
        if not self.split_z:
            return turn(v[part], -self.step, 1)
        if part % 2 == 0:
            return v[part + 1]
        return turn(v[part - 1], -1, 1)

    def last_z(self, v, part):
        if not self.split_z:
            return turn(v[part], self.step, 1)
        if part % 2 == 0:
            return turn(v[part + 1], 1, 1)
        return v[part - 1]

    def set_faces(self, use):
        half = self.half
        parts = range(self.parts)

        def body(i, carry):
            here, below = carry
            above = self.read(self.coef, i + 2)
            upper = [half * (here[p] + above[p]) for p in parts]
            along_y = [half * (here[p] + self.next_y(here, p)) for p in parts]
            along_z = [half * (here[p] + self.next_z(here, p)) for p in parts]
            inverse = []
            for p in parts:
                diagonal = (
                    (below[p] + upper[p])
                    + (along_y[p] + self.last_y(along_y, p))
                    + (along_z[p] + self.last_z(along_z, p))
                )
                inside = here[p] > 0.0
                inverse.append(jnp.where(inside, 1.0 / jnp.where(inside, diagonal, 1.0), 0.0))
            self.write(self.face_x, i + 1, upper)
            self.write(self.face_y, i, along_y)
            self.write(self.face_z, i, along_z)
            self.write(self.inverse, i, inverse)
            use(i, here, inverse)
            return above, upper

        here = self.read(self.coef, 1)
        first = [half * here[p] for p in parts]
        self.write(self.face_x, 0, first)
        run(0, self.count, body, (here, first), self.unroll)

    def sweep(self, low, count, use):
        parts = range(self.parts)

        def body(i, carry):
            here, flux_low = carry
            above = self.read(self.values, i + 2)
            face_x, face_y, face_z = (self.read(ref, at) for ref, at in ((self.face_x, i + 1), (self.face_y, i), (self.face_z, i)))
            flux_high = [face_x[p] * (above[p] - here[p]) for p in parts]
            flux_y = [face_y[p] * (self.next_y(here, p) - here[p]) for p in parts]
            flux_z = [face_z[p] * (self.next_z(here, p) - here[p]) for p in parts]
            applied = [
                (flux_low[p] - flux_high[p])
                + (self.last_y(flux_y, p) - flux_y[p])
                + (self.last_z(flux_z, p) - flux_z[p])
                for p in parts
            ]
            use(i, applied, here)
            return above, flux_high

        here = self.read(self.values, low + 1)
        before = self.read(self.values, low)
        face = self.read(self.face_x, low)
        run(low, count, body, (here, [face[p] * (here[p] - before[p]) for p in parts]), self.unroll)

    def from_zero(self, i, inverse):
        first = smoothing_weights()[0][1]
        right = self.read(self.right, i)
        step = [right[p] * (inverse[p] * first) for p in range(self.parts)]
        self.write(self.update, i, step)
        self.write(self.values, i + 1, step)

    def smooth(self, low, count, weight):
        keep, gain = weight

        def use(i, applied, here):
            right = self.read(self.right, i)
            inverse = self.read(self.inverse, i)
            step = [(right[p] - applied[p]) * (inverse[p] * gain) for p in range(self.parts)]
            if keep:
                update = self.read(self.update, i)
                step = [keep * update[p] + step[p] for p in range(self.parts)]
            self.write(self.update, i, step)
            self.write(self.values, i + 1, [here[p] + step[p] for p in range(self.parts)])

        self.sweep(low, count, use)


def total(items):
    items = list(items)
    while len(items) > 1:
        items = [sum(items[k : k + 2][1:], items[k]) for k in range(0, len(items), 2)]
    return items[0]


def exact_dot(left, right):
    return jnp.dot(left, right, precision=lax.Precision.HIGHEST, preferred_element_type=jnp.float32)


def parity_matrix(size, back):
    row = lax.broadcasted_iota(jnp.int32, (size, size), 0)
    column = lax.broadcasted_iota(jnp.int32, (size, size), 1)
    if back:
        row, column = column, row
    hit = column == row // 2 + (row % 2) * (size // 2)
    return jnp.where(hit, 1.0, 0.0).astype(jnp.float32)


def split_kernel(fields, out, rows):
    _, bx, by, bz = fields.shape
    matrix = parity_matrix(bz, False)
    for which in (0, 1):
        rows[which] = exact_dot(fields[which].reshape(bx * by, bz), matrix)
        for odd in (0, 1):
            out[which, odd] = rows[which, pl.ds(odd, bx * by // 2, stride=2), :].reshape(bx, by // 2, bz)


def pack_kernel(*refs):
    *blocks, across_out, beside_out = refs
    bx, rows, bz = blocks[0].shape[2:]
    _, _, _, core, _ = place()
    quarter = bz // 4
    low = lax.broadcasted_iota(jnp.int32, (rows, bz), 1) % (bz // 2) < quarter

    def body(x, carry):
        for number, block in enumerate(blocks):
            for odd_y in (0, 1):
                right, coef = block[0, odd_y, x], block[1, odd_y, x]
                first = jnp.where(low, right, turn(coef, quarter, 1))
                last = jnp.where(low, turn(coef, -quarter, 1), right)
                across_out[number, odd_y, x] = jnp.where(core == 0, first, last)
                beside_out[number, odd_y, x] = jnp.where(core == 0, last, first)
        return carry

    lax.fori_loop(0, bx, body, 0, unroll=4)


def down_kernel(own, mid, sib, start_out, right_out, coef_out, pay_out, edge_out, *refs):
    level = Level(refs[:8], True, True, 1, 1.0, UNROLL_FINE)
    sums, coefs = refs[8:]
    bx, rows, bz = own.shape[3:]
    at_x, at_y, at_z, core, odd = place()
    lane = lax.broadcasted_iota(jnp.int32, (rows, bz), 1)
    quarter = bz // 4
    is_own = lane < bz // 2
    low = lane % (bz // 2) < quarter
    outside = (low == (core == 1)) & ~in_the_middle(at_z)
    level.clear_ends()

    for block, kind in enumerate(ORDER):
        at = at_x * bx if kind in (0, 2, 3) else (1 - at_x) * bx
        row = {0: 1, 1: 1, 2: 2 * (1 - odd), 4: 2 * (1 - odd), 3: 2 * odd, 5: 2 * odd}[kind] * rows
        if kind > 1:
            row = pl.multiple_of(row, rows)
        window = pl.ds(row, rows)

        def assemble(x, carry, block=block, kind=kind, at=at, window=window):
            for odd_y in (0, 1):
                over, beside = mid[block, odd_y, x], sib[block, odd_y, x]
                first = jnp.where(core == 1, over, beside)
                last = jnp.where(core == 1, beside, over)
                side = jnp.where(low, first, last)
                mine = own[block, 0, odd_y, x]
                level.right[2 * odd_y, at + x, window, :] = jnp.where(is_own, mine, turn(side, bz // 2, 1))
                level.right[2 * odd_y + 1, at + x, window, :] = jnp.where(is_own, turn(mine, bz // 2, 1), side)
                side = jnp.where(low, last, first)
                up, down = turn(side, quarter, 1), turn(side, -quarter, 1)
                mine = own[block, 1, odd_y, x]
                for odd_z in (0, 1):
                    near = jnp.where(low, down, up) if odd_z else jnp.where(low, up, down)
                    value = jnp.where(
                        is_own,
                        turn(mine, bz // 2, 1) if odd_z else mine,
                        jnp.where(outside, 0.0, near),
                    )
                    if kind in (3, 5):
                        value = jnp.where(in_the_middle(at_y), value, 0.0)
                    level.coef[2 * odd_y + odd_z, at + x + 1, window, :] = value
            return carry

        lax.fori_loop(0, bx, assemble, 0, unroll=2)

    def begin(i, here, inverse):
        level.from_zero(i, inverse)
        coefs[i] = total(here)

    level.set_faces(begin)
    for weight in smoothing_weights()[1:]:
        level.smooth(0, level.count, weight)

    def leftover(i, applied, here):
        right = level.read(level.right, i)
        sums[i] = total(right[p] - applied[p] for p in range(level.parts))

    level.sweep(0, level.count, leftover)

    edge = rows // 2
    upper_half = lax.broadcasted_iota(jnp.int32, (rows, bz), 0) < edge
    for which, ref in enumerate((sums, coefs)):
        for x in range(bx):
            ref[x] = 0.125 * (ref[2 * x] + ref[2 * x + 1])
            halves = [ref[x, pl.ds(edge + parity, rows, stride=2), :] for parity in (0, 1)]
            for parity in (0, 1):
                pay_out[which, parity, x] = halves[parity]
            edge_out[which, x] = jnp.where(
                upper_half,
                jnp.where(odd == 1, turn(halves[0], edge, 0), halves[0]),
                jnp.where(odd == 1, halves[1], turn(halves[1], edge, 0)),
            )

    window = pl.ds(edge, 2 * rows)

    def copy_out(i, carry):
        for part in range(level.parts):
            start_out[part, i] = turn(level.values[part, i + 1, window, :], -edge, 0)
            right_out[part, i] = turn(level.right[part, i, window, :], -edge, 0)
            coef_out[part, i] = turn(level.coef[part, i + 1, window, :], -edge, 0)
        return carry

    lax.fori_loop(0, level.count, copy_out, 0)


def up_kernel(pay, far, near, start, right, coef_in, solution_out, residual_out, *refs):
    level1 = Level(refs[:8], True, False, 1, 0.25, UNROLL_COARSE)
    level2 = Level(refs[8:16], False, False, 2, 0.0625, UNROLL_COARSE)
    fine = Level((refs[16], right, *refs[17:23]), True, True, 1, 1.0, UNROLL_FINE)
    window, rows_out = refs[23:]
    n1, rows, bz = pay.shape[2:]
    edge = rows // 2
    at_x, at_y, _, _, odd = place()
    upper = at_y // 2
    weights = smoothing_weights()
    for level in (level1, level2, fine):
        level.clear_ends()

    top = lax.broadcasted_iota(jnp.int32, (rows, bz), 0) < edge
    near_here = (top == (odd == 0)) & in_the_middle(at_y)
    for j in range(n1):
        for which, (ref, shift) in enumerate(((level1.right, 0), (level1.coef, 1))):
            piece = near[which, j]
            other = turn(piece, edge, 0)
            for parity in (0, 1):
                mine, theirs = pay[which, parity, j], far[which, parity, j]
                ref[parity, j + shift, :rows] = jnp.where(upper == 1, theirs, mine)
                ref[parity, j + shift, rows : 2 * rows] = jnp.where(upper == 1, mine, theirs)
                if parity == 0:
                    side = jnp.where(odd == 0, piece, other)
                else:
                    side = jnp.where(odd == 0, other, piece)
                ref[parity, j + shift, 2 * rows :] = jnp.where(near_here, side, 0.0)

    even_lane = lax.broadcasted_iota(jnp.int32, (3 * rows, bz), 1) % 2 == 0

    def pair_lanes(values):
        return values + jnp.where(even_lane, turn(values, -1, 1), turn(values, 1, 1))

    coefs, sums = [], []

    def begin1(i, here, inverse):
        level1.from_zero(i, inverse)
        coefs.append(total(here))

    level1.set_faces(begin1)
    for weight in weights[1:]:
        level1.smooth(0, n1, weight)

    def leftover1(i, applied, here):
        values = level1.read(level1.right, i)
        sums.append(total(values[p] - applied[p] for p in range(level1.parts)))

    level1.sweep(0, n1, leftover1)
    for j in range(n1 // 2):
        level2.right[0, j] = 0.125 * pair_lanes(sums[2 * j] + sums[2 * j + 1])
        level2.coef[0, j + 1] = 0.125 * pair_lanes(coefs[2 * j] + coefs[2 * j + 1])

    level2.set_faces(lambda i, here, inverse: level2.from_zero(i, inverse))
    for weight in weights[1:]:
        level2.smooth(0, n1 // 2, weight)

    for j in range(n1):
        for parity in (0, 1):
            level1.values[parity, j + 1] = level1.values[parity, j + 1] + level2.values[0, j // 2 + 1]
    for weight in weights:
        level1.smooth(0, n1, weight)

    def copy_in(i, carry):
        for part in range(fine.parts):
            fine.coef[part, i + 1] = coef_in[part, i]
        return carry

    lax.fori_loop(0, fine.count, copy_in, 0)
    fine.set_faces(lambda i, here, inverse: None)
    for j in range(n1):
        for parity in (0, 1):
            rows_of = level1.values[parity, j + 1, :rows], level1.values[parity, j + 1, rows : 2 * rows]
            window[j, pl.ds(parity, rows, stride=2), :] = jnp.where(upper == 1, rows_of[1], rows_of[0])
        spread = turn(window[j], -edge, 0)
        for i in (2 * j, 2 * j + 1):
            for part in range(fine.parts):
                fine.values[part, i + 1] = start[part, i] + spread
    bx = fine.count // 2
    for number, weight in enumerate(weights):
        reach = DEGREE - number
        fine.smooth(jnp.where(at_x == 0, 0, bx - reach), bx + reach, weight)

    base = at_x * bx
    own_lane = lax.broadcasted_iota(jnp.int32, (rows, bz), 1) < bz // 2

    def finish(i, applied, here):
        values = fine.read(right, i)
        for slot, field in enumerate((here, [values[p] - applied[p] for p in range(fine.parts)])):
            for odd_y in (0, 1):
                even, other = field[2 * odd_y][:rows], field[2 * odd_y + 1][:rows]
                rows_out[slot, i - base, pl.ds(odd_y, rows, stride=2), :] = jnp.where(
                    own_lane, even, turn(other, bz // 2, 1)
                )

    fine.sweep(base, bx, finish)
    matrix = parity_matrix(bz, True)
    for slot, ref in enumerate((solution_out, residual_out)):
        ref[...] = exact_dot(rows_out[slot].reshape(bx * 2 * rows, bz), matrix).reshape(ref.shape)


def vmem(*shape):
    return pltpu.VMEM(shape, jnp.float32)


def level_scratch(parts, n, rows, lanes, with_right):
    tall, plain = vmem(parts, n + 2, rows, lanes), vmem(parts, n, rows, lanes)
    return [
        tall,
        *([plain] if with_right else []),
        vmem(parts, n + 1, rows, lanes),
        plain,
        plain,
        plain,
        tall,
        plain,
    ]


def per_device_two_rounds(right_side, coefficient):
    bx, by, bz = right_side.shape
    rows = by // 2
    in_vmem = pl.BlockSpec(memory_space=pltpu.VMEM)
    params = pltpu.CompilerParams(vmem_limit_bytes=24 * 2**20)
    shape = lambda *sizes: jax.ShapeDtypeStruct(sizes, jnp.float32)

    mine = pl.pallas_call(
        split_kernel,
        out_shape=shape(2, 2, bx, rows, bz),
        in_specs=[in_vmem],
        out_specs=in_vmem,
        scratch_shapes=[vmem(2, bx * by, bz)],
        compiler_params=params,
        name="split",
    )(jnp.stack([right_side, coefficient]))

    pairs = [1, 0, 3, 2]
    inner = [0, 2, 1, 3]
    across = [(0, 1), (1, 0)]

    def both(partner):
        return [(4 * x + y, 4 * (1 - x) + partner[y]) for x in (0, 1) for y in range(4)]

    swap_pairs, swap_inner = list(enumerate(pairs)), list(enumerate(inner))
    other = lax.ppermute(mine, "gx", across)
    by_pairs = lax.ppermute(mine, "gy", swap_pairs)
    by_inner = lax.ppermute(mine, "gy", swap_inner)
    other_pairs = lax.ppermute(mine, ("gx", "gy"), both(pairs))
    other_inner = lax.ppermute(mine, ("gx", "gy"), both(inner))
    blocks = (mine, other, by_pairs, by_inner, other_pairs, other_inner)
    blocks = [blocks[kind] for kind in ORDER]
    edges = shape(6, 2, bx, rows, bz)
    to_mid, to_sib = pl.pallas_call(
        pack_kernel,
        out_shape=(edges, edges),
        in_specs=[in_vmem] * 6,
        out_specs=(in_vmem,) * 2,
        compiler_params=params,
        name="pack",
    )(*blocks)
    mid = lax.ppermute(to_mid, "gz", swap_inner)
    sib = lax.ppermute(to_sib, "gz", swap_pairs)

    nx = 2 * bx
    window = shape(4, nx, 2 * rows, bz)
    start, right_wide, coef_wide, pay, edge = pl.pallas_call(
        down_kernel,
        out_shape=(window, window, window, shape(2, 2, bx, rows, bz), shape(2, bx, rows, bz)),
        in_specs=[in_vmem] * 3,
        out_specs=(in_vmem,) * 5,
        scratch_shapes=[
            *level_scratch(4, nx, 3 * rows, bz, True),
            vmem(nx, 3 * rows, bz),
            vmem(nx, 3 * rows, bz),
        ],
        compiler_params=params,
        name="down",
    )(jnp.stack(blocks), mid, sib)
    far = lax.ppermute(pay, "gy", [(0, 2), (2, 0), (1, 3), (3, 1)])
    near = lax.ppermute(edge, "gy", list(enumerate(pairs)))
    return pl.pallas_call(
        up_kernel,
        out_shape=(shape(bx, by, bz),) * 2,
        in_specs=[in_vmem] * 6,
        out_specs=(in_vmem,) * 2,
        scratch_shapes=[
            *level_scratch(2, bx, 3 * rows, bz, True),
            *level_scratch(1, bx // 2, 3 * rows, bz, True),
            *level_scratch(4, nx, 2 * rows, bz, False),
            vmem(bx, 2 * rows, bz),
            vmem(2, bx, by, bz),
        ],
        compiler_params=params,
        name="up",
    )(pay, far, near, start, right_wide, coef_wide)


def two_rounds_fit(mesh, shape):
    counts = tuple(mesh.shape[name] for name in ("gx", "gy", "gz"))
    bx, by, bz = (size // count for size, count in zip(shape, counts))
    edge = by // 4
    reach_coarse = 4 * DEGREE + 2
    return (
        counts == (2, 4, 4)
        and LEVELS == 3
        and bx % 4 == 0
        and by == 16
        and bz == 128
        and 2 * edge + DEGREE + 1 <= by
        and by // 2 + reach_coarse <= 2 * by - edge
        and 2 * reach_coarse + DEGREE + 1 <= bz // 2
    )


def solution(mesh):
    in_specs = (P("gx", "gy", "gz"), P("gx", "gy", "gz"))
    out_specs = (P("gx", "gy", "gz"), P("gx", "gy", "gz"))

    def whole(right_side, coefficient):
        fits = two_rounds_fit(mesh, right_side.shape)
        return jax.shard_map(
            per_device_two_rounds if fits else per_device,
            mesh=mesh,
            in_specs=in_specs,
            out_specs=out_specs,
            check_vma=False,
        )(right_side, coefficient)

    return whole
```

```python
import jax
import jax.numpy as jnp
from jax import lax
from jax.experimental import pallas as pl
from jax.experimental.pallas import tpu as pltpu
from jax.sharding import PartitionSpec as P

LEVELS = 3
DEGREE = 4


cheb_low = 0.3
cheb_high = 2.0


def extended(block, sides, width):
    for axis, dim in sides:
        count = lax.axis_size(axis)
        forward = [(i, i + 1) for i in range(count - 1)]
        backward = [(target, source) for source, target in forward]
        low = lax.ppermute(
            lax.slice_in_dim(block, block.shape[dim] - width, None, axis=dim), axis, forward
        )
        high = lax.ppermute(lax.slice_in_dim(block, 0, width, axis=dim), axis, backward)
        block = jnp.concatenate([low, block, high], axis=dim)
    return block


def face_terms(padded):
    face_x = 0.5 * (padded[1:, 1:-1, 1:-1] + padded[:-1, 1:-1, 1:-1])
    face_y = 0.5 * (padded[1:-1, 1:, 1:-1] + padded[1:-1, :-1, 1:-1])
    face_z = 0.5 * (padded[1:-1, 1:-1, 1:] + padded[1:-1, 1:-1, :-1])
    diagonal = (
        face_x[1:]
        + face_x[:-1]
        + face_y[:, 1:]
        + face_y[:, :-1]
        + face_z[:, :, 1:]
        + face_z[:, :, :-1]
    )
    return (face_x, face_y, face_z, diagonal)


def apply_padded(padded, face_set, factor):
    face_x, face_y, face_z, diagonal = face_set
    flux_x = face_x * (padded[1:, 1:-1, 1:-1] - padded[:-1, 1:-1, 1:-1])
    flux_y = face_y * (padded[1:-1, 1:, 1:-1] - padded[1:-1, :-1, 1:-1])
    flux_z = face_z * (padded[1:-1, 1:-1, 1:] - padded[1:-1, 1:-1, :-1])
    result = (
        flux_x[:-1]
        - flux_x[1:]
        + (flux_y[:, :-1] - flux_y[:, 1:])
        + (flux_z[:, :, :-1] - flux_z[:, :, 1:])
    )
    return factor * result


def fine_halo(values):
    return extended(values, (("gx", 0), ("gy", 1), ("gz", 2)), 1)


def spread_halo(values):
    return extended(values, (("gx", 0), ("gy", 1), ("gz", 2)), 1)


def restrict(values):
    size_x, size_y, size_z = values.shape
    blocks = values.reshape(size_x // 2, 2, size_y // 2, 2, size_z // 2, 2)
    return jnp.mean(blocks, axis=(1, 3, 5))


def prolong(values):
    size_x, size_y, size_z = values.shape
    spread = jnp.broadcast_to(values[:, None, :, None, :, None], (size_x, 2, size_y, 2, size_z, 2))
    return spread.reshape(2 * size_x, 2 * size_y, 2 * size_z)


def trim_cells(values, layers):
    return values[
        layers : values.shape[0] - layers,
        layers : values.shape[1] - layers,
        layers : values.shape[2] - layers,
    ]


def trim_faces(face_set, layers):
    return tuple((trim_cells(member, layers) for member in face_set))


def inside_mask(shape, margin):
    count_x = shape[0]
    count_y = shape[1]
    count_z = shape[2]
    along_x = lax.axis_index("gx") * count_x + jnp.arange(
        -margin, count_x + margin, dtype=jnp.int32
    )
    along_y = lax.axis_index("gy") * count_y + jnp.arange(
        -margin, count_y + margin, dtype=jnp.int32
    )
    along_z = lax.axis_index("gz") * count_z + jnp.arange(
        -margin, count_z + margin, dtype=jnp.int32
    )
    valid_x = (along_x >= 0) & (along_x < count_x * lax.axis_size("gx"))
    valid_y = (along_y >= 0) & (along_y < count_y * lax.axis_size("gy"))
    valid_z = (along_z >= 0) & (along_z < count_z * lax.axis_size("gz"))
    return valid_x[:, None, None] & valid_y[None, :, None] & valid_z[None, None, :]


def deep_smooth(right_wide, start_wide, face_wide, valid_wide):
    centre = 0.5 * (cheb_high + cheb_low)
    half_width = 0.5 * (cheb_high - cheb_low)
    sigma_val = centre / half_width
    rho_now = 1.0 / sigma_val
    safe_diag = jnp.where(valid_wide, face_wide[3], 1.0)
    if start_wide is None:
        update = jnp.where(valid_wide, right_wide / (1.0 * safe_diag) / centre, 0.0)
        iterate = update
        lost = 0
    else:
        leftover = trim_cells(right_wide, 1) - apply_padded(
            start_wide, trim_faces(face_wide, 1), 1.0
        )
        update = jnp.where(
            trim_cells(valid_wide, 1), leftover / (1.0 * trim_cells(safe_diag, 1)) / centre, 0.0
        )
        iterate = trim_cells(start_wide, 1) + update
        lost = 1
    for sweep_no in range(DEGREE - 1):
        lost = lost + 1
        leftover = trim_cells(right_wide, lost) - apply_padded(
            iterate, trim_faces(face_wide, lost), 1.0
        )
        rho_next = 1.0 / (2.0 * sigma_val - rho_now)
        fresh = rho_next * rho_now * trim_cells(update, 1) + 2.0 * rho_next / half_width * (
            leftover / (1.0 * trim_cells(safe_diag, lost))
        )
        update = jnp.where(trim_cells(valid_wide, lost), fresh, 0.0)
        iterate = trim_cells(iterate, 1) + update
        rho_now = rho_next
    return (iterate, lost)


def smooth(right, initial, face_set, factor, padder):
    diagonal = face_set[3]
    centre = 0.5 * (cheb_high + cheb_low)
    half_width = 0.5 * (cheb_high - cheb_low)
    sigma_val = centre / half_width
    rho_now = 1.0 / sigma_val
    if initial is None:
        iterate = jnp.zeros_like(right)
        leftover = right
    else:
        iterate = initial
        leftover = right - apply_padded(padder(initial), face_set, factor)
    update = leftover / (factor * diagonal) / centre
    iterate = iterate + update
    for sweep_no in range(DEGREE - 1):
        leftover = right - apply_padded(padder(iterate), face_set, factor)
        rho_next = 1.0 / (2.0 * sigma_val - rho_now)
        update = rho_next * rho_now * update + 2.0 * rho_next / half_width * (
            leftover / (factor * diagonal)
        )
        iterate = iterate + update
        rho_now = rho_next
    return iterate


def per_device(right_side, coefficient):
    depth = DEGREE
    stacked = jnp.stack([right_side, coefficient])
    widened = extended(stacked, (("gx", 1), ("gy", 2), ("gz", 3)), depth + 1)
    right_wide = trim_cells(widened[0], 1)
    face_wide = face_terms(widened[1])
    valid_wide = inside_mask(right_side.shape, depth)
    fine_set = trim_faces(face_wide, depth)
    partial_value, lost = deep_smooth(right_wide, None, face_wide, valid_wide)
    leftover = right_side - apply_padded(partial_value, trim_faces(face_wide, depth), 1.0)
    iterate = trim_cells(partial_value, 1)
    coarse_right = restrict(leftover)
    coarse_coef = restrict(coefficient)
    rights = [coarse_right]
    face_sets = []
    iterates = []
    for level_no in range(1, LEVELS):
        factor = 0.25**level_no
        face_set = face_terms(spread_halo(coarse_coef))
        face_sets.append(face_set)
        current = smooth(rights[-1], None, face_set, factor, spread_halo)
        iterates.append(current)
        if level_no < LEVELS - 1:
            remains = rights[-1] - apply_padded(spread_halo(current), face_set, factor)
            rights.append(restrict(remains))
            coarse_coef = restrict(coarse_coef)
    level_no = 1
    slot_no = level_no - 1
    iterates[slot_no] = smooth(
        rights[slot_no],
        iterates[slot_no] + prolong(iterates[slot_no + 1]),
        face_sets[slot_no],
        0.25**level_no,
        spread_halo,
    )
    correction = iterates[0]
    start = iterate + prolong(correction)
    start_wide = extended(start, (("gx", 0), ("gy", 1), ("gz", 2)), depth)
    solution, lost = deep_smooth(right_wide, start_wide, face_wide, valid_wide)
    residual = right_side - apply_padded(fine_halo(solution), fine_set, 1.0)
    return (solution, residual)


UNROLL_FINE = 20
UNROLL_COARSE = 64


def place():
    at_x, at_y, at_z = (lax.axis_index(name) for name in ("gx", "gy", "gz"))
    return at_x, at_y, at_z, lax.rem(at_z, 2), lax.rem(at_y, 2)


def in_the_middle(at):
    return (at == 1) | (at == 2)


def smoothing_weights():
    centre = 0.5 * (cheb_high + cheb_low)
    half_width = 0.5 * (cheb_high - cheb_low)
    sigma_val = centre / half_width
    rho_now = 1.0 / sigma_val
    weights = [(0.0, 1.0 / centre)]
    for _ in range(DEGREE - 1):
        rho_next = 1.0 / (2.0 * sigma_val - rho_now)
        weights.append((rho_next * rho_now, 2.0 * rho_next / half_width))
        rho_now = rho_next
    return weights


def turn(values, shift, axis):
    return pltpu.roll(values, shift % values.shape[axis], axis)


def run(low, high, body, carry, unroll):
    count = high - low
    steps = -(-count // unroll)
    unroll = -(-count // steps)

    def several(start, state, rows):
        pending = []
        for k in range(rows):
            state, stores = body(start + k, state)
            pending += stores
        for ref, i, values in pending:
            for part, value in enumerate(values):
                ref[part, i] = value
        return state

    whole = count // unroll
    if whole == 1:
        carry = several(low, carry, unroll)
    else:
        carry = lax.fori_loop(0, whole, lambda step, state: several(low + step * unroll, state, unroll), carry)
    if count > whole * unroll:
        carry = several(low + whole * unroll, carry, count - whole * unroll)
    return carry


def tile_place(shape, axis):
    return lax.broadcasted_iota(jnp.int32, shape, axis)


class Level:
    def __init__(self, refs, split, step, scale, unroll):
        self.coef, self.right, self.face_x, self.face_y, self.face_z, self.edge_x, self.inverse, self.values, self.update = refs
        self.parts, self.rows = self.inverse.shape[:2]
        self.tile = self.inverse.shape[2:]
        self.split, self.step, self.half, self.unroll = split, step, 0.5 * scale, unroll
        self.first = tile_place(self.tile, 0) < step
        self.last = tile_place(self.tile, 0) >= self.tile[0] - step

    def read(self, ref, i):
        return [ref[part, i] for part in range(ref.shape[0])]

    def clear_ends(self):
        for ref in (self.coef, self.values):
            for part in range(self.parts):
                for i in (0, self.rows - 1):
                    ref[part, i] = jnp.zeros(self.tile, jnp.float32)

    def next_x(self, v, part):
        if self.split and part < 2:
            return v[part + 2]
        return jnp.where(self.last, 0.0, turn(v[part - 2 if self.split else part], -self.step, 0))

    def last_x(self, v, part, at_edge):
        if self.split and part >= 2:
            return v[part - 2]
        return jnp.where(self.first, at_edge[part], turn(v[part + 2 if self.split else part], self.step, 0))

    def next_z(self, v, part):
        if self.split and part % 2 == 0:
            return v[part + 1]
        return turn(v[part - 1 if self.split else part], -self.step, 1)

    def last_z(self, v, part):
        if self.split and part % 2 == 1:
            return v[part - 1]
        return turn(v[part + 1 if self.split else part], self.step, 1)

    def set_faces(self, use):
        half = self.half
        parts = range(self.parts)

        def body(i, carry):
            here, below = carry
            above = self.read(self.coef, i + 1)
            upper = [half * (here[p] + above[p]) for p in parts]
            along_x = [half * (here[p] + self.next_x(here, p)) for p in parts]
            along_z = [half * (here[p] + self.next_z(here, p)) for p in parts]
            edge = [half * here[p] for p in range(self.edge_x.shape[0])]
            inverse = []
            for p in parts:
                diagonal = (
                    (below[p] + upper[p])
                    + (along_x[p] + self.last_x(along_x, p, edge))
                    + (along_z[p] + self.last_z(along_z, p))
                )
                inside = here[p] > 0.0
                inverse.append(jnp.where(inside, 1.0 / jnp.where(inside, diagonal, 1.0), 0.0))
            stores = [
                (self.face_y, i, upper),
                (self.face_x, i, along_x),
                (self.face_z, i, along_z),
                (self.edge_x, i, edge),
                (self.inverse, i, inverse),
            ]
            return (above, upper), stores + use(i, here, inverse)

        here, before = self.read(self.coef, 1), self.read(self.coef, 0)
        face = [half * (here[p] + before[p]) for p in parts]
        for p in parts:
            self.face_y[p, 0] = face[p]
        run(1, self.rows - 1, body, (here, face), self.unroll)

    def sweep(self, low, high, use):
        parts = range(self.parts)

        def body(i, carry):
            here, flux_low = carry
            above = self.read(self.values, i + 1)
            face_x, face_y, face_z, edge_x = (
                self.read(ref, i) for ref in (self.face_x, self.face_y, self.face_z, self.edge_x)
            )
            flux_high = [face_y[p] * (above[p] - here[p]) for p in parts]
            flux_x = [face_x[p] * (self.next_x(here, p) - here[p]) for p in parts]
            flux_z = [face_z[p] * (self.next_z(here, p) - here[p]) for p in parts]
            at_edge = [face * value for face, value in zip(edge_x, here)]
            applied = [
                (flux_low[p] - flux_high[p])
                + (self.last_x(flux_x, p, at_edge) - flux_x[p])
                + (self.last_z(flux_z, p) - flux_z[p])
                for p in parts
            ]
            return (above, flux_high), use(i, applied, here)

        here, before = self.read(self.values, low), self.read(self.values, low - 1)
        face = self.read(self.face_y, low - 1)
        run(low, high, body, (here, [face[p] * (here[p] - before[p]) for p in parts]), self.unroll)

    def from_zero(self, i, inverse):
        first = smoothing_weights()[0][1]
        right = self.read(self.right, i)
        step = [right[p] * (inverse[p] * first) for p in range(self.parts)]
        return [(self.update, i, step), (self.values, i, step)]

    def smooth(self, low, high, weight):
        keep, gain = weight

        def use(i, applied, here):
            right = self.read(self.right, i)
            inverse = self.read(self.inverse, i)
            step = [(right[p] - applied[p]) * (inverse[p] * gain) for p in range(self.parts)]
            if keep:
                update = self.read(self.update, i)
                step = [keep * update[p] + step[p] for p in range(self.parts)]
            return [(self.update, i, step), (self.values, i, [here[p] + step[p] for p in range(self.parts)])]

        self.sweep(low, high, use)


def total(items):
    items = list(items)
    while len(items) > 1:
        items = [sum(items[k : k + 2][1:], items[k]) for k in range(0, len(items), 2)]
    return items[0]


def exact_dot(left, right):
    return jnp.dot(left, right, precision=lax.Precision.HIGHEST, preferred_element_type=jnp.float32)


def parity_matrix(size, back):
    row, column = tile_place((size, size), 0), tile_place((size, size), 1)
    if back:
        row, column = column, row
    hit = column == row // 2 + (row % 2) * (size // 2)
    return jnp.where(hit, 1.0, 0.0).astype(jnp.float32)


def parity_place(x, count):
    return x // 2 + (x % 2) * (count // 2)


def halo_rows(by):
    return 2 * (by // 4) + DEGREE + 1


def split_kernel(fields, out, pair_out, inner_out, rows):
    _, bx, by, bz = fields.shape
    _, _, _, _, odd = place()
    halo = halo_rows(by)
    matrix = parity_matrix(bz, False)
    for which in (0, 1):
        moved = exact_dot(fields[which].reshape(bx * by, bz), matrix)
        for x in range(bx):
            at = parity_place(x, bx) * by
            rows[which, at : at + by] = moved[x * by : (x + 1) * by]
        for y in range(by):
            out[which, y] = rows[which, pl.ds(y, bx, stride=by), :]
    for which in (0, 1):
        pair_out[which] = out[which, pl.ds((1 - odd) * (by - halo), halo)]
        inner_out[which] = out[which, pl.ds(odd * (by - halo), halo)]


def pack_kernel(*refs):
    *blocks, across_out, beside_out = refs
    _, _, _, core, _ = place()
    tile = across_out.shape[1:]
    quarter = tile[1] // 4
    low = tile_place(tile, 1) % (2 * quarter) < quarter
    at = 0
    for block in blocks:
        for y in range(block.shape[1]):
            right, coef = block[0, y], block[1, y]
            first = jnp.where(low, right, turn(coef, quarter, 1))
            last = jnp.where(low, turn(coef, -quarter, 1), right)
            across_out[at] = jnp.where(core == 0, first, last)
            beside_out[at] = jnp.where(core == 0, last, first)
            at += 1


def down_kernel(mine, other, pair, pair_other, inner, inner_other, mid, sib, *refs):
    right, face_x, face_y, face_z, edge_x, inverse, values, pay_out, near_out, coef, update, sums, coefs = refs
    level = Level((coef, right, face_x, face_y, face_z, edge_x, inverse, values, update), True, 1, 1.0, UNROLL_FINE)
    by, bx, bz = mine.shape[1:]
    halo = pair.shape[1]
    at_x, at_y, at_z, core, odd = place()
    tile = (bx, bz)
    lane = tile_place(tile, 1)
    quarter = bz // 4
    is_own = lane < bz // 2
    low = lane % (bz // 2) < quarter
    outside = (low == (core == 1)) & ~in_the_middle(at_z)
    top = tile_place(tile, 0) < bx // 2

    def columns(block, y, at):
        over, beside = mid[at], sib[at]
        first = jnp.where(core == 1, over, beside)
        last = jnp.where(core == 1, beside, over)
        side, own = jnp.where(low, first, last), block[0, y]
        right_cells = [
            jnp.where(is_own, own, turn(side, bz // 2, 1)),
            jnp.where(is_own, turn(own, bz // 2, 1), side),
        ]
        side, own = jnp.where(low, last, first), block[1, y]
        up, down = turn(side, quarter, 1), turn(side, -quarter, 1)
        coef_cells = [
            jnp.where(is_own, own, jnp.where(outside, 0.0, jnp.where(low, up, down))),
            jnp.where(is_own, turn(own, bz // 2, 1), jnp.where(outside, 0.0, jnp.where(low, down, up))),
        ]
        return right_cells, coef_cells

    at = 0
    for near, far, row in (
        (mine, other, halo),
        (pair, pair_other, (1 - odd) * (halo + by)),
        (inner, inner_other, odd * (halo + by)),
    ):
        count = near.shape[1]

        def assemble(y, carry, near=near, far=far, row=row, at=at, count=count):
            both = zip(columns(near, y, at + y), columns(far, y, at + count + y))
            stores = []
            for ref, (here, there) in zip((right, coef), both):
                for odd_z in (0, 1):
                    one = jnp.where(at_x == 0, here[odd_z], there[odd_z])
                    two = jnp.where(at_x == 0, there[odd_z], here[odd_z])
                    cells = jnp.where(top, one, turn(two, bx // 2, 0)), jnp.where(top, turn(one, bx // 2, 0), two)
                    for odd_x in (0, 1):
                        value = cells[odd_x]
                        if ref is coef and near is inner:
                            value = jnp.where(in_the_middle(at_y), value, 0.0)
                        stores.append((ref.at[pl.ds(2 * odd_x + odd_z, 1)], row + y, [value]))
            return carry, stores

        run(0, count, assemble, 0, 4)
        at += 2 * count

    def begin(i, here, inverse):
        return level.from_zero(i, inverse) + [(coefs, i, [total(here)])]

    level.set_faces(begin)
    edge = 1
    for weight in smoothing_weights()[1:]:
        edge += 1
        level.smooth(edge, level.rows - edge, weight)

    def leftover(i, applied, here):
        right = level.read(level.right, i)
        return [(sums, i, [total(right[p] - applied[p] for p in range(level.parts))])]

    edge += 1
    level.sweep(edge, level.rows - edge, leftover)
    for which, ref in enumerate((sums, coefs)):
        for y in range(by):
            pay_out[which, y] = 0.125 * (ref[0, edge + 2 * y] + ref[0, edge + 2 * y + 1])
        shared = by // 4
        near_out[which] = pay_out[which, pl.ds(shared + odd * (by - 3 * shared), shared)]


def up_kernel(pay, far, near, right, face_x, face_y, face_z, edge_x, inverse, start, solution_out, residual_out, *refs):
    level1 = Level(refs[:9], False, 1, 0.25, UNROLL_COARSE)
    level2 = Level(refs[9:18], False, 2, 0.0625, UNROLL_COARSE)
    values, update, sums, moved, rows_out = refs[18:]
    fine = Level((None, right, face_x, face_y, face_z, edge_x, inverse, values, update), True, 1, 1.0, UNROLL_FINE)
    by, bx, bz = pay.shape[1:]
    shared = near.shape[1]
    at_x, at_y, _, _, odd = place()
    upper = at_y // 2
    weights = smoothing_weights()
    tile = (bx, bz)
    level1.clear_ends()
    level2.clear_ends()

    for which, ref in enumerate((level1.right, level1.coef)):
        for y in range(by):
            one, two = pay[which, y], far[which, y]
            ref[0, 1 + shared * odd + y] = jnp.where(upper == 1, two, one)
            ref[0, 1 + by + shared * odd + y] = jnp.where(upper == 1, one, two)
        for y in range(shared):
            ref[0, 1 + 2 * by * (1 - odd) + y] = jnp.where(in_the_middle(at_y), near[which, y], 0.0)

    n1 = level1.rows - 1
    n2 = level2.rows - 1
    even_lane = tile_place(tile, 1) % 2 == 0
    even_row = tile_place(tile, 0) % 2 == 0

    def pair_cells(values):
        values = values + jnp.where(even_lane, turn(values, -1, 1), turn(values, 1, 1))
        return 0.125 * (values + jnp.where(even_row, turn(values, -1, 0), turn(values, 1, 0)))

    level1.set_faces(lambda i, here, inverse: level1.from_zero(i, inverse))
    for weight in weights[1:]:
        level1.smooth(1, n1, weight)

    def leftover1(i, applied, here):
        return [(sums, i, [level1.right[0, i] - applied[0]])]

    level1.sweep(1, n1, leftover1)
    for j in range(1, n2):
        level2.right[0, j] = pair_cells(sums[0, 2 * j - 1] + sums[0, 2 * j])
        level2.coef[0, j] = pair_cells(level1.coef[0, 2 * j - 1] + level1.coef[0, 2 * j])

    level2.set_faces(lambda i, here, inverse: level2.from_zero(i, inverse))
    for weight in weights[1:]:
        level2.smooth(1, n2, weight)

    for j in range(1, n1):
        level1.values[0, j] = level1.values[0, j] + level2.values[0, (j + 1) // 2]
    for weight in weights:
        level1.smooth(1, n1, weight)

    halo = (fine.rows - by) // 2
    reach = DEGREE + 1
    base = 1 + (by // 2) * at_y + shared * (1 - odd)
    for y in range(-reach, by + reach):
        coarse = level1.values[0, base + y // 2]
        for part in range(fine.parts):
            values[part, halo + y] = start[part, halo + y] + coarse
    for weight in weights:
        reach -= 1
        fine.smooth(halo - reach, halo + by + reach, weight)

    own_lane = tile_place(tile, 1) < bz // 2
    top = tile_place(tile, 0) < bx // 2

    def finish(i, applied, here):
        right_row = fine.read(right, i)
        stores = []
        for slot, field in enumerate((here, [right_row[p] - applied[p] for p in range(fine.parts)])):
            cells = []
            for odd_z in (0, 1):
                one, two = field[odd_z], field[2 + odd_z]
                cells.append(
                    jnp.where(
                        top,
                        jnp.where(at_x == 0, one, turn(one, bx // 2, 0)),
                        jnp.where(at_x == 0, turn(two, bx // 2, 0), two),
                    )
                )
            stores.append((rows_out.at[pl.ds(slot, 1)], i - halo, [jnp.where(own_lane, cells[0], turn(cells[1], bz // 2, 1))]))
        return stores

    fine.sweep(halo, halo + by, finish)
    matrix = parity_matrix(bz, True)
    for slot, ref in enumerate((solution_out, residual_out)):
        moved[slot] = exact_dot(rows_out[slot].reshape(by * bx, bz), matrix)
        for x in range(bx):
            ref[x] = moved[slot, pl.ds(parity_place(x, bx), by, stride=bx), :]


def vmem(*shape):
    return pltpu.VMEM(shape, jnp.float32)


def per_device_two_rounds(right_side, coefficient):
    bx, by, bz = right_side.shape
    halo = halo_rows(by)
    shared = by // 4
    in_vmem = pl.BlockSpec(memory_space=pltpu.VMEM)
    params = pltpu.CompilerParams(vmem_limit_bytes=24 * 2**20)
    shape = lambda *sizes: jax.ShapeDtypeStruct(sizes, jnp.float32)

    mine, for_pair, for_inner = pl.pallas_call(
        split_kernel,
        out_shape=(shape(2, by, bx, bz), shape(2, halo, bx, bz), shape(2, halo, bx, bz)),
        in_specs=[in_vmem],
        out_specs=(in_vmem,) * 3,
        scratch_shapes=[vmem(2, bx * by, bz)],
        compiler_params=params,
        name="split",
    )(jnp.stack([right_side, coefficient]))

    pairs = [1, 0, 3, 2]
    inner = [0, 2, 1, 3]
    swap_pairs, swap_inner = list(enumerate(pairs)), list(enumerate(inner))

    def across_x(partner):
        return [(4 * x + y, 4 * (1 - x) + partner[y]) for x in (0, 1) for y in range(4)]

    blocks = {
        "mine": mine,
        "other": lax.ppermute(mine, "gx", [(0, 1), (1, 0)]),
        "pair": lax.ppermute(for_pair, "gy", swap_pairs),
        "pair_other": lax.ppermute(for_pair, ("gx", "gy"), across_x(pairs)),
        "inner": lax.ppermute(for_inner, "gy", swap_inner),
        "inner_other": lax.ppermute(for_inner, ("gx", "gy"), across_x(inner)),
    }
    blocks = list(blocks.values())
    edges = shape(2 * by + 4 * halo, bx, bz)
    to_mid, to_sib = pl.pallas_call(
        pack_kernel,
        out_shape=(edges, edges),
        in_specs=[in_vmem] * 6,
        out_specs=(in_vmem,) * 2,
        compiler_params=params,
        name="pack",
    )(*blocks)
    mid = lax.ppermute(to_mid, "gz", swap_inner)
    sib = lax.ppermute(to_sib, "gz", swap_pairs)

    rows = by + 2 * halo
    field, half_field = (4, rows, bx, bz), (2, rows, bx, bz)
    *fine, pay, near = pl.pallas_call(
        down_kernel,
        out_shape=(
            *(shape(*(half_field if number == 4 else field)) for number in range(7)),
            shape(2, by, bx, bz),
            shape(2, shared, bx, bz),
        ),
        in_specs=[in_vmem] * 8,
        out_specs=(in_vmem,) * 9,
        scratch_shapes=[vmem(*field), vmem(*field), vmem(1, rows, bx, bz), vmem(1, rows, bx, bz)],
        compiler_params=params,
        name="down",
    )(*blocks, mid, sib)
    far = lax.ppermute(pay, "gy", [(0, 2), (2, 0), (1, 3), (3, 1)])
    near = lax.ppermute(near, "gy", swap_pairs)
    rows1 = 2 * by + shared + 2
    return pl.pallas_call(
        up_kernel,
        out_shape=(shape(bx, by, bz),) * 2,
        in_specs=[in_vmem] * 10,
        out_specs=(in_vmem,) * 2,
        scratch_shapes=[
            *[vmem(1, rows1, bx, bz)] * 9,
            *[vmem(1, rows1 // 2 + 1, bx, bz)] * 9,
            vmem(*field),
            vmem(*field),
            vmem(1, rows1, bx, bz),
            vmem(2, bx * by, bz),
            vmem(2, by, bx, bz),
        ],
        compiler_params=params,
        name="up",
    )(pay, far, near, *fine)


def two_rounds_fit(mesh, shape):
    counts = tuple(mesh.shape[name] for name in ("gx", "gy", "gz"))
    bx, by, bz = (size // count for size, count in zip(shape, counts))
    shared = by // 4
    reach_coarse = 4 * DEGREE + 2
    return (
        counts == (2, 4, 4)
        and LEVELS == 3
        and bx == 8
        and by % 8 == 0
        and bz == 128
        and halo_rows(by) <= by
        and by // 2 + reach_coarse <= 2 * by - shared
        and 2 * reach_coarse + DEGREE + 1 <= bz // 2
    )


def solution(mesh):
    in_specs = (P("gx", "gy", "gz"), P("gx", "gy", "gz"))
    out_specs = (P("gx", "gy", "gz"), P("gx", "gy", "gz"))

    def whole(right_side, coefficient):
        fits = two_rounds_fit(mesh, right_side.shape)
        return jax.shard_map(
            per_device_two_rounds if fits else per_device,
            mesh=mesh,
            in_specs=in_specs,
            out_specs=out_specs,
            check_vma=False,
        )(right_side, coefficient)

    return whole
```

```python
import jax
import jax.numpy as jnp
from jax import lax
from jax.experimental import pallas as pl
from jax.experimental.pallas import tpu as pltpu
from jax.sharding import PartitionSpec as P

LEVELS = 3
DEGREE = 4


cheb_low = 0.3
cheb_high = 2.0


def extended(block, sides, width):
    for axis, dim in sides:
        count = lax.axis_size(axis)
        forward = [(i, i + 1) for i in range(count - 1)]
        backward = [(target, source) for source, target in forward]
        low = lax.ppermute(
            lax.slice_in_dim(block, block.shape[dim] - width, None, axis=dim), axis, forward
        )
        high = lax.ppermute(lax.slice_in_dim(block, 0, width, axis=dim), axis, backward)
        block = jnp.concatenate([low, block, high], axis=dim)
    return block


def face_terms(padded):
    face_x = 0.5 * (padded[1:, 1:-1, 1:-1] + padded[:-1, 1:-1, 1:-1])
    face_y = 0.5 * (padded[1:-1, 1:, 1:-1] + padded[1:-1, :-1, 1:-1])
    face_z = 0.5 * (padded[1:-1, 1:-1, 1:] + padded[1:-1, 1:-1, :-1])
    diagonal = (
        face_x[1:]
        + face_x[:-1]
        + face_y[:, 1:]
        + face_y[:, :-1]
        + face_z[:, :, 1:]
        + face_z[:, :, :-1]
    )
    return (face_x, face_y, face_z, diagonal)


def apply_padded(padded, face_set, factor):
    face_x, face_y, face_z, diagonal = face_set
    flux_x = face_x * (padded[1:, 1:-1, 1:-1] - padded[:-1, 1:-1, 1:-1])
    flux_y = face_y * (padded[1:-1, 1:, 1:-1] - padded[1:-1, :-1, 1:-1])
    flux_z = face_z * (padded[1:-1, 1:-1, 1:] - padded[1:-1, 1:-1, :-1])
    result = (
        flux_x[:-1]
        - flux_x[1:]
        + (flux_y[:, :-1] - flux_y[:, 1:])
        + (flux_z[:, :, :-1] - flux_z[:, :, 1:])
    )
    return factor * result


def fine_halo(values):
    return extended(values, (("gx", 0), ("gy", 1), ("gz", 2)), 1)


def spread_halo(values):
    return extended(values, (("gx", 0), ("gy", 1), ("gz", 2)), 1)


def restrict(values):
    size_x, size_y, size_z = values.shape
    blocks = values.reshape(size_x // 2, 2, size_y // 2, 2, size_z // 2, 2)
    return jnp.mean(blocks, axis=(1, 3, 5))


def prolong(values):
    size_x, size_y, size_z = values.shape
    spread = jnp.broadcast_to(values[:, None, :, None, :, None], (size_x, 2, size_y, 2, size_z, 2))
    return spread.reshape(2 * size_x, 2 * size_y, 2 * size_z)


def trim_cells(values, layers):
    return values[
        layers : values.shape[0] - layers,
        layers : values.shape[1] - layers,
        layers : values.shape[2] - layers,
    ]


def trim_faces(face_set, layers):
    return tuple((trim_cells(member, layers) for member in face_set))


def inside_mask(shape, margin):
    count_x = shape[0]
    count_y = shape[1]
    count_z = shape[2]
    along_x = lax.axis_index("gx") * count_x + jnp.arange(
        -margin, count_x + margin, dtype=jnp.int32
    )
    along_y = lax.axis_index("gy") * count_y + jnp.arange(
        -margin, count_y + margin, dtype=jnp.int32
    )
    along_z = lax.axis_index("gz") * count_z + jnp.arange(
        -margin, count_z + margin, dtype=jnp.int32
    )
    valid_x = (along_x >= 0) & (along_x < count_x * lax.axis_size("gx"))
    valid_y = (along_y >= 0) & (along_y < count_y * lax.axis_size("gy"))
    valid_z = (along_z >= 0) & (along_z < count_z * lax.axis_size("gz"))
    return valid_x[:, None, None] & valid_y[None, :, None] & valid_z[None, None, :]


def deep_smooth(right_wide, start_wide, face_wide, valid_wide):
    centre = 0.5 * (cheb_high + cheb_low)
    half_width = 0.5 * (cheb_high - cheb_low)
    sigma_val = centre / half_width
    rho_now = 1.0 / sigma_val
    safe_diag = jnp.where(valid_wide, face_wide[3], 1.0)
    if start_wide is None:
        update = jnp.where(valid_wide, right_wide / (1.0 * safe_diag) / centre, 0.0)
        iterate = update
        lost = 0
    else:
        leftover = trim_cells(right_wide, 1) - apply_padded(
            start_wide, trim_faces(face_wide, 1), 1.0
        )
        update = jnp.where(
            trim_cells(valid_wide, 1), leftover / (1.0 * trim_cells(safe_diag, 1)) / centre, 0.0
        )
        iterate = trim_cells(start_wide, 1) + update
        lost = 1
    for sweep_no in range(DEGREE - 1):
        lost = lost + 1
        leftover = trim_cells(right_wide, lost) - apply_padded(
            iterate, trim_faces(face_wide, lost), 1.0
        )
        rho_next = 1.0 / (2.0 * sigma_val - rho_now)
        fresh = rho_next * rho_now * trim_cells(update, 1) + 2.0 * rho_next / half_width * (
            leftover / (1.0 * trim_cells(safe_diag, lost))
        )
        update = jnp.where(trim_cells(valid_wide, lost), fresh, 0.0)
        iterate = trim_cells(iterate, 1) + update
        rho_now = rho_next
    return (iterate, lost)


def smooth(right, initial, face_set, factor, padder):
    diagonal = face_set[3]
    centre = 0.5 * (cheb_high + cheb_low)
    half_width = 0.5 * (cheb_high - cheb_low)
    sigma_val = centre / half_width
    rho_now = 1.0 / sigma_val
    if initial is None:
        iterate = jnp.zeros_like(right)
        leftover = right
    else:
        iterate = initial
        leftover = right - apply_padded(padder(initial), face_set, factor)
    update = leftover / (factor * diagonal) / centre
    iterate = iterate + update
    for sweep_no in range(DEGREE - 1):
        leftover = right - apply_padded(padder(iterate), face_set, factor)
        rho_next = 1.0 / (2.0 * sigma_val - rho_now)
        update = rho_next * rho_now * update + 2.0 * rho_next / half_width * (
            leftover / (factor * diagonal)
        )
        iterate = iterate + update
        rho_now = rho_next
    return iterate


def per_device(right_side, coefficient):
    depth = DEGREE
    stacked = jnp.stack([right_side, coefficient])
    widened = extended(stacked, (("gx", 1), ("gy", 2), ("gz", 3)), depth + 1)
    right_wide = trim_cells(widened[0], 1)
    face_wide = face_terms(widened[1])
    valid_wide = inside_mask(right_side.shape, depth)
    fine_set = trim_faces(face_wide, depth)
    partial_value, lost = deep_smooth(right_wide, None, face_wide, valid_wide)
    leftover = right_side - apply_padded(partial_value, trim_faces(face_wide, depth), 1.0)
    iterate = trim_cells(partial_value, 1)
    coarse_right = restrict(leftover)
    coarse_coef = restrict(coefficient)
    rights = [coarse_right]
    face_sets = []
    iterates = []
    for level_no in range(1, LEVELS):
        factor = 0.25**level_no
        face_set = face_terms(spread_halo(coarse_coef))
        face_sets.append(face_set)
        current = smooth(rights[-1], None, face_set, factor, spread_halo)
        iterates.append(current)
        if level_no < LEVELS - 1:
            remains = rights[-1] - apply_padded(spread_halo(current), face_set, factor)
            rights.append(restrict(remains))
            coarse_coef = restrict(coarse_coef)
    level_no = 1
    slot_no = level_no - 1
    iterates[slot_no] = smooth(
        rights[slot_no],
        iterates[slot_no] + prolong(iterates[slot_no + 1]),
        face_sets[slot_no],
        0.25**level_no,
        spread_halo,
    )
    correction = iterates[0]
    start = iterate + prolong(correction)
    start_wide = extended(start, (("gx", 0), ("gy", 1), ("gz", 2)), depth)
    solution, lost = deep_smooth(right_wide, start_wide, face_wide, valid_wide)
    residual = right_side - apply_padded(fine_halo(solution), fine_set, 1.0)
    return (solution, residual)


UNROLL_FINE = 20
GROUPS = ((0, 1, 2), (4, 5, 3))
UNROLL_COARSE = 64


def place():
    at_x, at_y, at_z = (lax.axis_index(name) for name in ("gx", "gy", "gz"))
    return at_x, at_y, at_z, lax.rem(at_z, 2), lax.rem(at_y, 2)


def in_the_middle(at):
    return (at == 1) | (at == 2)


def smoothing_weights():
    centre = 0.5 * (cheb_high + cheb_low)
    half_width = 0.5 * (cheb_high - cheb_low)
    sigma_val = centre / half_width
    rho_now = 1.0 / sigma_val
    weights = [(0.0, 1.0 / centre)]
    for _ in range(DEGREE - 1):
        rho_next = 1.0 / (2.0 * sigma_val - rho_now)
        weights.append((rho_next * rho_now, 2.0 * rho_next / half_width))
        rho_now = rho_next
    return weights


def turn(values, shift, axis):
    return pltpu.roll(values, shift % values.shape[axis], axis)


def run(low, count, body, carry, unroll):
    steps = -(-count // unroll)
    unroll = -(-count // steps)

    def several(start, state, rows):
        pending = []
        for k in range(rows):
            state, stores = body(start + k, state)
            pending += stores
        for ref, i, values in pending:
            for part, value in enumerate(values):
                ref[part, i] = value
        return state

    whole = count // unroll
    if whole == 1:
        carry = several(low, carry, unroll)
    else:
        carry = lax.fori_loop(0, whole, lambda step, state: several(low + step * unroll, state, unroll), carry)
    if count > whole * unroll:
        carry = several(low + whole * unroll, carry, count - whole * unroll)
    return carry


def tile_place(shape, axis):
    return lax.broadcasted_iota(jnp.int32, shape, axis)


class Level:
    def __init__(self, refs, split, step, scale, unroll, pad=1):
        self.coef, self.right, self.face_x, self.face_y, self.face_z, self.edge_x, self.inverse, self.values, self.update = refs
        self.parts, self.rows = self.inverse.shape[:2]
        self.tile = self.inverse.shape[2:]
        self.split, self.step, self.half, self.unroll, self.pad = split, step, 0.5 * scale, unroll, pad
        self.first = tile_place(self.tile, 0) < step
        self.last = tile_place(self.tile, 0) >= self.tile[0] - step

    def read(self, ref, i):
        return [ref[part, i] for part in range(ref.shape[0])]

    def clear(self):
        for i in range(self.rows):
            self.coef[0, i] = self.values[0, i] = self.right[0, i] = jnp.zeros(self.tile, jnp.float32)

    def next_x(self, v, part):
        if self.split and part < 2:
            return v[part + 2]
        return jnp.where(self.last, 0.0, turn(v[part - 2 if self.split else part], -self.step, 0))

    def last_x(self, v, part, at_edge):
        if self.split and part >= 2:
            return v[part - 2]
        return jnp.where(self.first, at_edge[part], turn(v[part + 2 if self.split else part], self.step, 0))

    def next_z(self, v, part):
        if self.split and part % 2 == 0:
            return v[part + 1]
        return turn(v[part - 1 if self.split else part], -self.step, 1)

    def last_z(self, v, part):
        if self.split and part % 2 == 1:
            return v[part - 1]
        return turn(v[part + 1 if self.split else part], self.step, 1)

    def set_faces(self, use):
        half = self.half
        parts = range(self.parts)

        def body(i, carry):
            here, below = carry
            above = self.read(self.coef, i + 1)
            upper = [half * (here[p] + above[p]) for p in parts]
            along_x = [half * (here[p] + self.next_x(here, p)) for p in parts]
            along_z = [half * (here[p] + self.next_z(here, p)) for p in parts]
            edge = [half * here[p] for p in range(self.edge_x.shape[0])]
            inverse = []
            for p in parts:
                diagonal = (
                    (below[p] + upper[p])
                    + (along_x[p] + self.last_x(along_x, p, edge))
                    + (along_z[p] + self.last_z(along_z, p))
                )
                inside = here[p] > 0.0
                inverse.append(jnp.where(inside, 1.0 / diagonal, 0.0))
            stores = [
                (self.face_y, i, upper),
                (self.face_x, i, along_x),
                (self.face_z, i, along_z),
                (self.edge_x, i, edge),
                (self.inverse, i, inverse),
            ]
            return (above, upper), stores + use(i, here, inverse)

        low, high = self.pad, self.rows - self.pad
        here, before = self.read(self.coef, low), self.read(self.coef, low - 1)
        face = [half * (here[p] + before[p]) for p in parts]
        for p in parts:
            self.face_y[p, low - 1] = face[p]
        run(low, high - low, body, (here, face), self.unroll)

    def sweep(self, low, count, use):
        parts = range(self.parts)

        def body(i, carry):
            here, flux_low = carry
            above = self.read(self.values, i + 1)
            face_x, face_y, face_z, edge_x = (
                self.read(ref, i) for ref in (self.face_x, self.face_y, self.face_z, self.edge_x)
            )
            flux_high = [face_y[p] * (above[p] - here[p]) for p in parts]
            flux_x = [face_x[p] * (self.next_x(here, p) - here[p]) for p in parts]
            flux_z = [face_z[p] * (self.next_z(here, p) - here[p]) for p in parts]
            at_edge = [face * value for face, value in zip(edge_x, here)]
            applied = [
                (flux_low[p] - flux_high[p])
                + (self.last_x(flux_x, p, at_edge) - flux_x[p])
                + (self.last_z(flux_z, p) - flux_z[p])
                for p in parts
            ]
            return (above, flux_high), use(i, applied, here)

        here, before = self.read(self.values, low), self.read(self.values, low - 1)
        face = self.read(self.face_y, low - 1)
        run(low, count, body, (here, [face[p] * (here[p] - before[p]) for p in parts]), self.unroll)

    def from_zero(self, i, inverse):
        first = smoothing_weights()[0][1]
        right = self.read(self.right, i)
        step = [right[p] * (inverse[p] * first) for p in range(self.parts)]
        return [(self.update, i, step), (self.values, i, step)]

    def smooth(self, low, count, weight):
        keep, gain = weight

        def use(i, applied, here):
            right = self.read(self.right, i)
            inverse = self.read(self.inverse, i)
            step = [(right[p] - applied[p]) * (inverse[p] * gain) for p in range(self.parts)]
            if keep:
                update = self.read(self.update, i)
                step = [keep * update[p] + step[p] for p in range(self.parts)]
            return [(self.update, i, step), (self.values, i, [here[p] + step[p] for p in range(self.parts)])]

        self.sweep(low, count, use)


def total(items):
    items = list(items)
    while len(items) > 1:
        items = [sum(items[k : k + 2][1:], items[k]) for k in range(0, len(items), 2)]
    return items[0]


def exact_dot(left, right):
    return jnp.dot(left, right, precision=lax.Precision.HIGHEST, preferred_element_type=jnp.float32)


def parity_matrix(size, back):
    row, column = tile_place((size, size), 0), tile_place((size, size), 1)
    if back:
        row, column = column, row
    hit = column == row // 2 + (row % 2) * (size // 2)
    return jnp.where(hit, 1.0, 0.0).astype(jnp.float32)


def parity_place(x, count):
    return x // 2 + (x % 2) * (count // 2)


def halo_rows(by):
    return 2 * (by // 4) + DEGREE + 1


def split_kernel(fields, out, pair_out, inner_out, rows):
    _, bx, by, bz = fields.shape
    _, _, _, _, odd = place()
    halo = halo_rows(by)
    matrix = parity_matrix(bz, False)
    for which in (0, 1):
        moved = exact_dot(fields[which].reshape(bx * by, bz), matrix)
        for x in range(bx):
            at = parity_place(x, bx) * by
            rows[which, at : at + by] = moved[x * by : (x + 1) * by]
        for y in range(by):
            out[which, y] = rows[which, pl.ds(y, bx, stride=by), :]
    for which in (0, 1):
        pair_out[which] = out[which, pl.ds((1 - odd) * (by - halo), halo)]
        inner_out[which] = out[which, pl.ds(odd * (by - halo), halo)]


def pack_kernel(*refs):
    *blocks, across_out, beside_out = refs
    _, _, _, core, _ = place()
    tile = across_out.shape[1:]
    quarter = tile[1] // 4
    low = tile_place(tile, 1) % (2 * quarter) < quarter
    at = 0
    for block in blocks:
        for y in range(block.shape[1]):
            right, coef = block[0, y], block[1, y]
            first = jnp.where(low, right, turn(coef, quarter, 1))
            last = jnp.where(low, turn(coef, -quarter, 1), right)
            across_out[at] = jnp.where(core == 0, first, last)
            beside_out[at] = jnp.where(core == 0, last, first)
            at += 1


def down_kernel(mine, other, pair, pair_other, inner, inner_other, *refs):
    edges, refs = refs[: 2 * len(GROUPS)], refs[2 * len(GROUPS) :]
    right, face_x, face_y, face_z, edge_x, inverse, values, pay_out, far_out, near_out, coef, update, sums, coefs = refs
    level = Level((coef, right, face_x, face_y, face_z, edge_x, inverse, values, update), True, 1, 1.0, UNROLL_FINE)
    by, bx, bz = mine.shape[1:]
    halo = pair.shape[1]
    at_x, at_y, at_z, core, odd = place()
    tile = (bx, bz)
    lane = tile_place(tile, 1)
    quarter = bz // 4
    is_own = lane < bz // 2
    low = lane % (bz // 2) < quarter
    outside = (low == (core == 1)) & ~in_the_middle(at_z)
    top = tile_place(tile, 0) < bx // 2

    def columns(block, y, kind):
        blocks = (mine, other, pair, pair_other, inner, inner_other)
        number = next(number for number, group in enumerate(GROUPS) if kind in group)
        before = GROUPS[number][: GROUPS[number].index(kind)]
        at = y + sum(blocks[earlier].shape[1] for earlier in before)
        over, beside = edges[2 * number][at], edges[2 * number + 1][at]
        first = jnp.where(core == 1, over, beside)
        last = jnp.where(core == 1, beside, over)
        side, own = jnp.where(low, first, last), block[0, y]
        right_cells = [
            jnp.where(is_own, own, turn(side, bz // 2, 1)),
            jnp.where(is_own, turn(own, bz // 2, 1), side),
        ]
        side, own = jnp.where(low, last, first), block[1, y]
        up, down = turn(side, quarter, 1), turn(side, -quarter, 1)
        coef_cells = [
            jnp.where(is_own, own, jnp.where(outside, 0.0, jnp.where(low, up, down))),
            jnp.where(is_own, turn(own, bz // 2, 1), jnp.where(outside, 0.0, jnp.where(low, down, up))),
        ]
        return right_cells, coef_cells

    for kind, (near, far, row) in zip((0, 2, 4), (
        (mine, other, halo),
        (pair, pair_other, (1 - odd) * (halo + by)),
        (inner, inner_other, odd * (halo + by)),
    )):
        count = near.shape[1]

        def assemble(y, carry, near=near, far=far, row=row, kind=kind):
            both = zip(columns(near, y, kind), columns(far, y, kind + 1))
            stores = []
            for ref, (here, there) in zip((right, coef), both):
                for odd_z in (0, 1):
                    one = jnp.where(at_x == 0, here[odd_z], there[odd_z])
                    two = jnp.where(at_x == 0, there[odd_z], here[odd_z])
                    cells = jnp.where(top, one, turn(two, bx // 2, 0)), jnp.where(top, turn(one, bx // 2, 0), two)
                    for odd_x in (0, 1):
                        value = cells[odd_x]
                        if ref is coef and near is inner:
                            value = jnp.where(in_the_middle(at_y), value, 0.0)
                        stores.append((ref.at[pl.ds(2 * odd_x + odd_z, 1)], row + y, [value]))
            return carry, stores

        run(0, count, assemble, 0, 4)

    def begin(i, here, inverse):
        return level.from_zero(i, inverse) + [(coefs, i, [total(here)])]

    level.set_faces(begin)
    edge = 1
    for weight in smoothing_weights()[1:]:
        edge += 1
        level.smooth(edge, level.rows - 2 * edge, weight)

    def leftover(i, applied, here):
        right = level.read(level.right, i)
        return [(sums, i, [total(right[p] - applied[p] for p in range(level.parts))])]

    edge += 1
    level.sweep(edge, level.rows - 2 * edge, leftover)
    for which, ref in enumerate((sums, coefs)):
        for y in range(by):
            pay_out[which, y] = 0.125 * (ref[0, edge + 2 * y] + ref[0, edge + 2 * y + 1])
        shared = by // 4
        far_out[which] = pay_out[which, pl.ds(shared * (1 - odd), by - shared)]
        near_out[which] = pay_out[which, pl.ds(shared * (1 + odd), shared)]


def up_kernel(pay, far, near, right, face_x, face_y, face_z, edge_x, inverse, start, solution_out, residual_out, *refs):
    level1 = Level(refs[:9], False, 1, 0.25, UNROLL_COARSE, near.shape[1])
    level2 = Level(refs[9:18], False, 2, 0.0625, UNROLL_COARSE)
    values, update, sums, moved, rows_out = refs[18:]
    fine = Level((None, right, face_x, face_y, face_z, edge_x, inverse, values, update), True, 1, 1.0, UNROLL_FINE)
    by, bx, bz = pay.shape[1:]
    shared = near.shape[1]
    at_x, at_y, _, _, odd = place()
    weights = smoothing_weights()
    tile = (bx, bz)
    level1.clear()
    level2.clear()

    own1 = (by // 2) * at_y
    far1 = (by // 2) * (at_y + 2 - 4 * (at_y // 2)) + shared * (1 - odd)
    near1 = (by // 2) * (at_y + 1 - 2 * odd) + shared + shared * (1 - odd)
    for which, ref in enumerate((level1.right, level1.coef)):
        for piece, at in ((pay, own1), (far, far1), (near, near1)):
            for y in range(piece.shape[1]):
                ref[0, at + y] = piece[which, y]

    low1, high1 = level1.pad, level1.rows - level1.pad
    n2 = level2.rows - 1
    even_lane = tile_place(tile, 1) % 2 == 0
    even_row = tile_place(tile, 0) % 2 == 0

    def pair_cells(values):
        values = values + jnp.where(even_lane, turn(values, -1, 1), turn(values, 1, 1))
        return 0.125 * (values + jnp.where(even_row, turn(values, -1, 0), turn(values, 1, 0)))

    level1.set_faces(lambda i, here, inverse: level1.from_zero(i, inverse))
    for weight in weights[1:]:
        level1.smooth(low1, high1 - low1, weight)

    def leftover1(i, applied, here):
        return [(sums, i, [level1.right[0, i] - applied[0]])]

    level1.sweep(low1, high1 - low1, leftover1)
    for j in range(1, n2):
        level2.right[0, j] = pair_cells(sums[0, low1 + 2 * j - 2] + sums[0, low1 + 2 * j - 1])
        level2.coef[0, j] = pair_cells(level1.coef[0, low1 + 2 * j - 2] + level1.coef[0, low1 + 2 * j - 1])

    level2.set_faces(lambda i, here, inverse: level2.from_zero(i, inverse))
    for weight in weights[1:]:
        level2.smooth(1, n2 - 1, weight)

    for j in range(low1, high1):
        level1.values[0, j] = level1.values[0, j] + level2.values[0, 1 + (j - low1) // 2]
    reach = DEGREE + (DEGREE + 2) // 2
    for weight in weights:
        reach -= 1
        count = by // 2 + 2 * reach
        start1 = jnp.clip(shared + own1 - reach, low1, high1 - count)
        level1.smooth(start1, count, weight)

    halo = (fine.rows - by) // 2
    reach = DEGREE + 1
    base = shared + own1
    for y in range(-reach, by + reach):
        coarse = level1.values[0, base + y // 2]
        for part in range(fine.parts):
            values[part, halo + y] = start[part, halo + y] + coarse
    for weight in weights:
        reach -= 1
        fine.smooth(halo - reach, by + 2 * reach, weight)

    own_lane = tile_place(tile, 1) < bz // 2
    top = tile_place(tile, 0) < bx // 2

    def finish(i, applied, here):
        right_row = fine.read(right, i)
        stores = []
        for slot, field in enumerate((here, [right_row[p] - applied[p] for p in range(fine.parts)])):
            cells = []
            for odd_z in (0, 1):
                one, two = field[odd_z], field[2 + odd_z]
                cells.append(
                    jnp.where(
                        top,
                        jnp.where(at_x == 0, one, turn(one, bx // 2, 0)),
                        jnp.where(at_x == 0, turn(two, bx // 2, 0), two),
                    )
                )
            stores.append((rows_out.at[pl.ds(slot, 1)], i - halo, [jnp.where(own_lane, cells[0], turn(cells[1], bz // 2, 1))]))
        return stores

    fine.sweep(halo, by, finish)
    matrix = parity_matrix(bz, True)
    for slot, ref in enumerate((solution_out, residual_out)):
        moved[slot] = exact_dot(rows_out[slot].reshape(by * bx, bz), matrix)
        for x in range(bx):
            ref[x] = moved[slot, pl.ds(parity_place(x, bx), by, stride=bx), :]


def vmem(*shape):
    return pltpu.VMEM(shape, jnp.float32)


def per_device_two_rounds(right_side, coefficient):
    bx, by, bz = right_side.shape
    halo = halo_rows(by)
    shared = by // 4
    in_vmem = pl.BlockSpec(memory_space=pltpu.VMEM)
    params = pltpu.CompilerParams(vmem_limit_bytes=24 * 2**20)
    shape = lambda *sizes: jax.ShapeDtypeStruct(sizes, jnp.float32)

    mine, for_pair, for_inner = pl.pallas_call(
        split_kernel,
        out_shape=(shape(2, by, bx, bz), shape(2, halo, bx, bz), shape(2, halo, bx, bz)),
        in_specs=[in_vmem],
        out_specs=(in_vmem,) * 3,
        scratch_shapes=[vmem(2, bx * by, bz)],
        compiler_params=params,
        name="split",
    )(jnp.stack([right_side, coefficient]))

    pairs = [1, 0, 3, 2]
    inner = [0, 2, 1, 3]
    swap_pairs, swap_inner = list(enumerate(pairs)), list(enumerate(inner))

    def across_x(partner):
        return [(4 * x + y, 4 * (1 - x) + partner[y]) for x in (0, 1) for y in range(4)]

    blocks = {
        "mine": mine,
        "other": lax.ppermute(mine, "gx", [(0, 1), (1, 0)]),
        "pair": lax.ppermute(for_pair, "gy", swap_pairs),
        "pair_other": lax.ppermute(for_pair, ("gx", "gy"), across_x(pairs)),
        "inner": lax.ppermute(for_inner, "gy", swap_inner),
        "inner_other": lax.ppermute(for_inner, ("gx", "gy"), across_x(inner)),
    }
    blocks = list(blocks.values())
    def share(group):
        edges = shape(sum(block.shape[1] for block in group), bx, bz)
        to_mid, to_sib = pl.pallas_call(
            pack_kernel,
            out_shape=(edges, edges),
            in_specs=[in_vmem] * len(group),
            out_specs=(in_vmem,) * 2,
            compiler_params=params,
            name="pack",
        )(*group)
        return lax.ppermute(to_mid, "gz", swap_inner), lax.ppermute(to_sib, "gz", swap_pairs)

    edges = [part for group in GROUPS for part in share([blocks[kind] for kind in group])]

    rows = by + 2 * halo
    field, half_field = (4, rows, bx, bz), (2, rows, bx, bz)
    *fine, pay, far, near = pl.pallas_call(
        down_kernel,
        out_shape=(
            *(shape(*(half_field if number == 4 else field)) for number in range(7)),
            shape(2, by, bx, bz),
            shape(2, by - shared, bx, bz),
            shape(2, shared, bx, bz),
        ),
        in_specs=[in_vmem] * (6 + 2 * len(GROUPS)),
        out_specs=(in_vmem,) * 10,
        scratch_shapes=[vmem(*field), vmem(*field), vmem(1, rows, bx, bz), vmem(1, rows, bx, bz)],
        compiler_params=params,
        name="down",
    )(*blocks, *edges)
    far = lax.ppermute(far, "gy", [(0, 2), (2, 0), (1, 3), (3, 1)])
    near = lax.ppermute(near, "gy", swap_pairs)
    rows1 = by // 2 * lax.axis_size("gy") + 2 * shared
    rows2 = by // 4 * lax.axis_size("gy") + 2
    return pl.pallas_call(
        up_kernel,
        out_shape=(shape(bx, by, bz),) * 2,
        in_specs=[in_vmem] * 10,
        out_specs=(in_vmem,) * 2,
        scratch_shapes=[
            *[vmem(1, rows1, bx, bz)] * 9,
            *[vmem(1, rows2, bx, bz)] * 9,
            vmem(*field),
            vmem(*field),
            vmem(1, rows1, bx, bz),
            vmem(2, bx * by, bz),
            vmem(2, by, bx, bz),
        ],
        compiler_params=params,
        name="up",
    )(pay, far, near, *fine)


def two_rounds_fit(mesh, shape):
    counts = tuple(mesh.shape[name] for name in ("gx", "gy", "gz"))
    bx, by, bz = (size // count for size, count in zip(shape, counts))
    shared = by // 4
    reach_coarse = 4 * DEGREE + 2
    return (
        counts == (2, 4, 4)
        and LEVELS == 3
        and bx == 8
        and by % 8 == 0
        and bz == 128
        and halo_rows(by) <= by
        and by // 2 + reach_coarse + 1 <= 2 * by - shared
        and 2 * reach_coarse + DEGREE + 1 <= bz // 2
    )


def solution(mesh):
    in_specs = (P("gx", "gy", "gz"), P("gx", "gy", "gz"))
    out_specs = (P("gx", "gy", "gz"), P("gx", "gy", "gz"))

    def whole(right_side, coefficient):
        fits = two_rounds_fit(mesh, right_side.shape)
        return jax.shard_map(
            per_device_two_rounds if fits else per_device,
            mesh=mesh,
            in_specs=in_specs,
            out_specs=out_specs,
            check_vma=False,
        )(right_side, coefficient)

    return whole
```

```python
import jax
import jax.numpy as jnp
from jax import lax
from jax.experimental import pallas as pl
from jax.experimental.pallas import tpu as pltpu
from jax.sharding import PartitionSpec as P

LEVELS = 3
DEGREE = 4


cheb_low = 0.3
cheb_high = 2.0


def extended(block, sides, width):
    for axis, dim in sides:
        count = lax.axis_size(axis)
        forward = [(i, i + 1) for i in range(count - 1)]
        backward = [(target, source) for source, target in forward]
        low = lax.ppermute(
            lax.slice_in_dim(block, block.shape[dim] - width, None, axis=dim), axis, forward
        )
        high = lax.ppermute(lax.slice_in_dim(block, 0, width, axis=dim), axis, backward)
        block = jnp.concatenate([low, block, high], axis=dim)
    return block


def face_terms(padded):
    face_x = 0.5 * (padded[1:, 1:-1, 1:-1] + padded[:-1, 1:-1, 1:-1])
    face_y = 0.5 * (padded[1:-1, 1:, 1:-1] + padded[1:-1, :-1, 1:-1])
    face_z = 0.5 * (padded[1:-1, 1:-1, 1:] + padded[1:-1, 1:-1, :-1])
    diagonal = (
        face_x[1:]
        + face_x[:-1]
        + face_y[:, 1:]
        + face_y[:, :-1]
        + face_z[:, :, 1:]
        + face_z[:, :, :-1]
    )
    return (face_x, face_y, face_z, diagonal)


def apply_padded(padded, face_set, factor):
    face_x, face_y, face_z, diagonal = face_set
    flux_x = face_x * (padded[1:, 1:-1, 1:-1] - padded[:-1, 1:-1, 1:-1])
    flux_y = face_y * (padded[1:-1, 1:, 1:-1] - padded[1:-1, :-1, 1:-1])
    flux_z = face_z * (padded[1:-1, 1:-1, 1:] - padded[1:-1, 1:-1, :-1])
    result = (
        flux_x[:-1]
        - flux_x[1:]
        + (flux_y[:, :-1] - flux_y[:, 1:])
        + (flux_z[:, :, :-1] - flux_z[:, :, 1:])
    )
    return factor * result


def fine_halo(values):
    return extended(values, (("gx", 0), ("gy", 1), ("gz", 2)), 1)


def spread_halo(values):
    return extended(values, (("gx", 0), ("gy", 1), ("gz", 2)), 1)


def restrict(values):
    size_x, size_y, size_z = values.shape
    blocks = values.reshape(size_x // 2, 2, size_y // 2, 2, size_z // 2, 2)
    return jnp.mean(blocks, axis=(1, 3, 5))


def prolong(values):
    size_x, size_y, size_z = values.shape
    spread = jnp.broadcast_to(values[:, None, :, None, :, None], (size_x, 2, size_y, 2, size_z, 2))
    return spread.reshape(2 * size_x, 2 * size_y, 2 * size_z)


def trim_cells(values, layers):
    return values[
        layers : values.shape[0] - layers,
        layers : values.shape[1] - layers,
        layers : values.shape[2] - layers,
    ]


def trim_faces(face_set, layers):
    return tuple((trim_cells(member, layers) for member in face_set))


def inside_mask(shape, margin):
    count_x = shape[0]
    count_y = shape[1]
    count_z = shape[2]
    along_x = lax.axis_index("gx") * count_x + jnp.arange(
        -margin, count_x + margin, dtype=jnp.int32
    )
    along_y = lax.axis_index("gy") * count_y + jnp.arange(
        -margin, count_y + margin, dtype=jnp.int32
    )
    along_z = lax.axis_index("gz") * count_z + jnp.arange(
        -margin, count_z + margin, dtype=jnp.int32
    )
    valid_x = (along_x >= 0) & (along_x < count_x * lax.axis_size("gx"))
    valid_y = (along_y >= 0) & (along_y < count_y * lax.axis_size("gy"))
    valid_z = (along_z >= 0) & (along_z < count_z * lax.axis_size("gz"))
    return valid_x[:, None, None] & valid_y[None, :, None] & valid_z[None, None, :]


def deep_smooth(right_wide, start_wide, face_wide, valid_wide):
    centre = 0.5 * (cheb_high + cheb_low)
    half_width = 0.5 * (cheb_high - cheb_low)
    sigma_val = centre / half_width
    rho_now = 1.0 / sigma_val
    safe_diag = jnp.where(valid_wide, face_wide[3], 1.0)
    if start_wide is None:
        update = jnp.where(valid_wide, right_wide / (1.0 * safe_diag) / centre, 0.0)
        iterate = update
        lost = 0
    else:
        leftover = trim_cells(right_wide, 1) - apply_padded(
            start_wide, trim_faces(face_wide, 1), 1.0
        )
        update = jnp.where(
            trim_cells(valid_wide, 1), leftover / (1.0 * trim_cells(safe_diag, 1)) / centre, 0.0
        )
        iterate = trim_cells(start_wide, 1) + update
        lost = 1
    for sweep_no in range(DEGREE - 1):
        lost = lost + 1
        leftover = trim_cells(right_wide, lost) - apply_padded(
            iterate, trim_faces(face_wide, lost), 1.0
        )
        rho_next = 1.0 / (2.0 * sigma_val - rho_now)
        fresh = rho_next * rho_now * trim_cells(update, 1) + 2.0 * rho_next / half_width * (
            leftover / (1.0 * trim_cells(safe_diag, lost))
        )
        update = jnp.where(trim_cells(valid_wide, lost), fresh, 0.0)
        iterate = trim_cells(iterate, 1) + update
        rho_now = rho_next
    return (iterate, lost)


def smooth(right, initial, face_set, factor, padder):
    diagonal = face_set[3]
    centre = 0.5 * (cheb_high + cheb_low)
    half_width = 0.5 * (cheb_high - cheb_low)
    sigma_val = centre / half_width
    rho_now = 1.0 / sigma_val
    if initial is None:
        iterate = jnp.zeros_like(right)
        leftover = right
    else:
        iterate = initial
        leftover = right - apply_padded(padder(initial), face_set, factor)
    update = leftover / (factor * diagonal) / centre
    iterate = iterate + update
    for sweep_no in range(DEGREE - 1):
        leftover = right - apply_padded(padder(iterate), face_set, factor)
        rho_next = 1.0 / (2.0 * sigma_val - rho_now)
        update = rho_next * rho_now * update + 2.0 * rho_next / half_width * (
            leftover / (factor * diagonal)
        )
        iterate = iterate + update
        rho_now = rho_next
    return iterate


def per_device(right_side, coefficient):
    depth = DEGREE
    stacked = jnp.stack([right_side, coefficient])
    widened = extended(stacked, (("gx", 1), ("gy", 2), ("gz", 3)), depth + 1)
    right_wide = trim_cells(widened[0], 1)
    face_wide = face_terms(widened[1])
    valid_wide = inside_mask(right_side.shape, depth)
    fine_set = trim_faces(face_wide, depth)
    partial_value, lost = deep_smooth(right_wide, None, face_wide, valid_wide)
    leftover = right_side - apply_padded(partial_value, trim_faces(face_wide, depth), 1.0)
    iterate = trim_cells(partial_value, 1)
    coarse_right = restrict(leftover)
    coarse_coef = restrict(coefficient)
    rights = [coarse_right]
    face_sets = []
    iterates = []
    for level_no in range(1, LEVELS):
        factor = 0.25**level_no
        face_set = face_terms(spread_halo(coarse_coef))
        face_sets.append(face_set)
        current = smooth(rights[-1], None, face_set, factor, spread_halo)
        iterates.append(current)
        if level_no < LEVELS - 1:
            remains = rights[-1] - apply_padded(spread_halo(current), face_set, factor)
            rights.append(restrict(remains))
            coarse_coef = restrict(coarse_coef)
    level_no = 1
    slot_no = level_no - 1
    iterates[slot_no] = smooth(
        rights[slot_no],
        iterates[slot_no] + prolong(iterates[slot_no + 1]),
        face_sets[slot_no],
        0.25**level_no,
        spread_halo,
    )
    correction = iterates[0]
    start = iterate + prolong(correction)
    start_wide = extended(start, (("gx", 0), ("gy", 1), ("gz", 2)), depth)
    solution, lost = deep_smooth(right_wide, start_wide, face_wide, valid_wide)
    residual = right_side - apply_padded(fine_halo(solution), fine_set, 1.0)
    return (solution, residual)


UNROLL_FINE = 26
GROUPS = ((0, 1, 2), (4, 5, 3))
UNROLL_COARSE = 64


def place():
    at_x, at_y, at_z = (lax.axis_index(name) for name in ("gx", "gy", "gz"))
    return at_x, at_y, at_z, lax.rem(at_z, 2), lax.rem(at_y, 2)


def in_the_middle(at):
    return (at == 1) | (at == 2)


def smoothing_weights():
    centre = 0.5 * (cheb_high + cheb_low)
    half_width = 0.5 * (cheb_high - cheb_low)
    sigma_val = centre / half_width
    rho_now = 1.0 / sigma_val
    weights = [(0.0, 1.0 / centre)]
    for _ in range(DEGREE - 1):
        rho_next = 1.0 / (2.0 * sigma_val - rho_now)
        weights.append((rho_next * rho_now, 2.0 * rho_next / half_width))
        rho_now = rho_next
    return weights


def turn(values, shift, axis):
    return pltpu.roll(values, shift % values.shape[axis], axis)


def run(low, count, body, carry, unroll):
    steps = -(-count // unroll)
    unroll = -(-count // steps)

    def several(start, state, rows):
        pending = []
        for k in range(rows):
            state, stores = body(start + k, state)
            pending += stores
        for ref, i, values in pending:
            for part, value in enumerate(values):
                ref[part, i] = value
        return state

    whole = count // unroll
    if whole == 1:
        carry = several(low, carry, unroll)
    else:
        carry = lax.fori_loop(0, whole, lambda step, state: several(low + step * unroll, state, unroll), carry)
    if count > whole * unroll:
        carry = several(low + whole * unroll, carry, count - whole * unroll)
    return carry


def tile_place(shape, axis):
    return lax.broadcasted_iota(jnp.int32, shape, axis)


class Level:
    def __init__(self, refs, split, step, scale, unroll, pad=1):
        self.coef, self.right, self.face_x, self.face_y, self.face_z, self.edge_x, self.inverse, self.values, self.update = refs
        self.parts, self.rows = self.inverse.shape[:2]
        self.tile = self.inverse.shape[2:]
        self.split, self.step, self.half, self.unroll, self.pad = split, step, 0.5 * scale, unroll, pad
        self.first = tile_place(self.tile, 0) < step
        self.last = tile_place(self.tile, 0) >= self.tile[0] - step

    def read(self, ref, i):
        return [ref[part, i] for part in range(ref.shape[0])]

    def clear(self):
        for i in range(self.rows):
            self.coef[0, i] = self.values[0, i] = self.right[0, i] = jnp.zeros(self.tile, jnp.float32)

    def next_x(self, v, part):
        if self.split and part < 2:
            return v[part + 2]
        return jnp.where(self.last, 0.0, turn(v[part - 2 if self.split else part], -self.step, 0))

    def last_x(self, v, part, at_edge):
        if self.split and part >= 2:
            return v[part - 2]
        return jnp.where(self.first, at_edge[part], turn(v[part + 2 if self.split else part], self.step, 0))

    def next_z(self, v, part):
        if self.split and part % 2 == 0:
            return v[part + 1]
        return turn(v[part - 1 if self.split else part], -self.step, 1)

    def last_z(self, v, part):
        if self.split and part % 2 == 1:
            return v[part - 1]
        return turn(v[part + 1 if self.split else part], self.step, 1)

    def set_faces(self, use):
        half = self.half
        parts = range(self.parts)

        def body(i, carry):
            here, below = carry
            above = self.read(self.coef, i + 1)
            upper = [half * (here[p] + above[p]) for p in parts]
            along_x = [half * (here[p] + self.next_x(here, p)) for p in parts]
            along_z = [half * (here[p] + self.next_z(here, p)) for p in parts]
            edge = [half * here[p] for p in range(self.edge_x.shape[0])]
            inverse = []
            for p in parts:
                diagonal = (
                    (below[p] + upper[p])
                    + (along_x[p] + self.last_x(along_x, p, edge))
                    + (along_z[p] + self.last_z(along_z, p))
                )
                inside = here[p] > 0.0
                inverse.append(jnp.where(inside, 1.0 / diagonal, 0.0))
            stores = [
                (self.face_y, i, upper),
                (self.face_x, i, along_x),
                (self.face_z, i, along_z),
                (self.edge_x, i, edge),
                (self.inverse, i, inverse),
            ]
            return (above, upper), stores + use(i, here, inverse)

        low, high = self.pad, self.rows - self.pad
        here, before = self.read(self.coef, low), self.read(self.coef, low - 1)
        face = [half * (here[p] + before[p]) for p in parts]
        for p in parts:
            self.face_y[p, low - 1] = face[p]
        run(low, high - low, body, (here, face), self.unroll)

    def sweep(self, low, count, use):
        parts = range(self.parts)

        def body(i, carry):
            here, flux_low = carry
            above = self.read(self.values, i + 1)
            face_x, face_y, face_z, edge_x = (
                self.read(ref, i) for ref in (self.face_x, self.face_y, self.face_z, self.edge_x)
            )
            flux_high = [face_y[p] * (above[p] - here[p]) for p in parts]
            flux_x = [face_x[p] * (self.next_x(here, p) - here[p]) for p in parts]
            flux_z = [face_z[p] * (self.next_z(here, p) - here[p]) for p in parts]
            at_edge = [face * value for face, value in zip(edge_x, here)]
            applied = [
                (flux_low[p] - flux_high[p])
                + (self.last_x(flux_x, p, at_edge) - flux_x[p])
                + (self.last_z(flux_z, p) - flux_z[p])
                for p in parts
            ]
            return (above, flux_high), use(i, applied, here)

        here, before = self.read(self.values, low), self.read(self.values, low - 1)
        face = self.read(self.face_y, low - 1)
        run(low, count, body, (here, [face[p] * (here[p] - before[p]) for p in parts]), self.unroll)

    def from_zero(self, i, inverse):
        first = smoothing_weights()[0][1]
        right = self.read(self.right, i)
        step = [right[p] * (inverse[p] * first) for p in range(self.parts)]
        return [(self.update, i, step), (self.values, i, step)]

    def smooth(self, low, count, weight):
        keep, gain = weight

        def use(i, applied, here):
            right = self.read(self.right, i)
            inverse = self.read(self.inverse, i)
            step = [(right[p] - applied[p]) * (inverse[p] * gain) for p in range(self.parts)]
            if keep:
                update = self.read(self.update, i)
                step = [keep * update[p] + step[p] for p in range(self.parts)]
            return [(self.update, i, step), (self.values, i, [here[p] + step[p] for p in range(self.parts)])]

        self.sweep(low, count, use)


def total(items):
    items = list(items)
    while len(items) > 1:
        items = [sum(items[k : k + 2][1:], items[k]) for k in range(0, len(items), 2)]
    return items[0]


def exact_dot(left, right):
    return jnp.dot(left, right, precision=lax.Precision.HIGHEST, preferred_element_type=jnp.float32)


def parity_matrix(size, back):
    row, column = tile_place((size, size), 0), tile_place((size, size), 1)
    if back:
        row, column = column, row
    hit = column == row // 2 + (row % 2) * (size // 2)
    return jnp.where(hit, 1.0, 0.0).astype(jnp.float32)


def parity_place(x, count):
    return x // 2 + (x % 2) * (count // 2)


def halo_rows(by):
    return 2 * (by // 4) + DEGREE + 1


def split_kernel(fields, out, pair_out, inner_out, rows):
    _, bx, by, bz = fields.shape
    _, _, _, _, odd = place()
    halo = halo_rows(by)
    matrix = parity_matrix(bz, False)
    for which in (0, 1):
        moved = exact_dot(fields[which].reshape(bx * by, bz), matrix)
        for x in range(bx):
            at = parity_place(x, bx) * by
            rows[which, at : at + by] = moved[x * by : (x + 1) * by]
        for y in range(by):
            out[which, y] = rows[which, pl.ds(y, bx, stride=by), :]
    for which in (0, 1):
        pair_out[which] = out[which, pl.ds((1 - odd) * (by - halo), halo)]
        inner_out[which] = out[which, pl.ds(odd * (by - halo), halo)]


def pack_kernel(*refs):
    *blocks, across_out, beside_out = refs
    _, _, _, core, _ = place()
    tile = across_out.shape[1:]
    quarter = tile[1] // 4
    low = tile_place(tile, 1) % (2 * quarter) < quarter
    at = 0
    for block in blocks:
        for y in range(block.shape[1]):
            right, coef = block[0, y], block[1, y]
            first = jnp.where(low, right, turn(coef, quarter, 1))
            last = jnp.where(low, turn(coef, -quarter, 1), right)
            across_out[at] = jnp.where(core == 0, first, last)
            beside_out[at] = jnp.where(core == 0, last, first)
            at += 1


def down_kernel(mine, other, pair, pair_other, inner, inner_other, *refs):
    edges, refs = refs[: 2 * len(GROUPS)], refs[2 * len(GROUPS) :]
    right, face_x, face_y, face_z, edge_x, inverse, values, pay_out, far_out, near_out, coef, update, sums, coefs = refs
    level = Level((coef, right, face_x, face_y, face_z, edge_x, inverse, values, update), True, 1, 1.0, UNROLL_FINE)
    by, bx, bz = mine.shape[1:]
    halo = pair.shape[1]
    at_x, at_y, at_z, core, odd = place()
    tile = (bx, bz)
    lane = tile_place(tile, 1)
    quarter = bz // 4
    is_own = lane < bz // 2
    low = lane % (bz // 2) < quarter
    outside = (low == (core == 1)) & ~in_the_middle(at_z)
    top = tile_place(tile, 0) < bx // 2

    def columns(block, y, kind):
        blocks = (mine, other, pair, pair_other, inner, inner_other)
        number = next(number for number, group in enumerate(GROUPS) if kind in group)
        before = GROUPS[number][: GROUPS[number].index(kind)]
        at = y + sum(blocks[earlier].shape[1] for earlier in before)
        over, beside = edges[2 * number][at], edges[2 * number + 1][at]
        first = jnp.where(core == 1, over, beside)
        last = jnp.where(core == 1, beside, over)
        side, own = jnp.where(low, first, last), block[0, y]
        right_cells = [
            jnp.where(is_own, own, turn(side, bz // 2, 1)),
            jnp.where(is_own, turn(own, bz // 2, 1), side),
        ]
        side, own = jnp.where(low, last, first), block[1, y]
        up, down = turn(side, quarter, 1), turn(side, -quarter, 1)
        coef_cells = [
            jnp.where(is_own, own, jnp.where(outside, 0.0, jnp.where(low, up, down))),
            jnp.where(is_own, turn(own, bz // 2, 1), jnp.where(outside, 0.0, jnp.where(low, down, up))),
        ]
        return right_cells, coef_cells

    for kind, (near, far, row) in zip((0, 2, 4), (
        (mine, other, halo),
        (pair, pair_other, (1 - odd) * (halo + by)),
        (inner, inner_other, odd * (halo + by)),
    )):
        count = near.shape[1]

        def assemble(y, carry, near=near, far=far, row=row, kind=kind):
            both = zip(columns(near, y, kind), columns(far, y, kind + 1))
            stores = []
            for ref, (here, there) in zip((right, coef), both):
                for odd_z in (0, 1):
                    one = jnp.where(at_x == 0, here[odd_z], there[odd_z])
                    two = jnp.where(at_x == 0, there[odd_z], here[odd_z])
                    cells = jnp.where(top, one, turn(two, bx // 2, 0)), jnp.where(top, turn(one, bx // 2, 0), two)
                    for odd_x in (0, 1):
                        value = cells[odd_x]
                        if ref is coef and near is inner:
                            value = jnp.where(in_the_middle(at_y), value, 0.0)
                        stores.append((ref.at[pl.ds(2 * odd_x + odd_z, 1)], row + y, [value]))
            return carry, stores

        run(0, count, assemble, 0, 16)

    def begin(i, here, inverse):
        return level.from_zero(i, inverse) + [(coefs, i, [total(here)])]

    level.set_faces(begin)
    edge = 1
    for weight in smoothing_weights()[1:]:
        edge += 1
        level.smooth(edge, level.rows - 2 * edge, weight)

    def leftover(i, applied, here):
        right = level.read(level.right, i)
        return [(sums, i, [total(right[p] - applied[p] for p in range(level.parts))])]

    edge += 1
    level.sweep(edge, level.rows - 2 * edge, leftover)
    for which, ref in enumerate((sums, coefs)):
        for y in range(by):
            pay_out[which, y] = 0.125 * (ref[0, edge + 2 * y] + ref[0, edge + 2 * y + 1])
        shared = by // 4
        far_out[which] = pay_out[which, pl.ds(shared * (1 - odd), by - shared)]
        near_out[which] = pay_out[which, pl.ds(shared * (1 + odd), shared)]


def up_kernel(pay, far, near, right, face_x, face_y, face_z, edge_x, inverse, start, solution_out, residual_out, *refs):
    level1 = Level(refs[:9], False, 1, 0.25, UNROLL_COARSE, near.shape[1])
    level2 = Level(refs[9:18], False, 2, 0.0625, UNROLL_COARSE)
    values, update, sums, moved, rows_out = refs[18:]
    fine = Level((None, right, face_x, face_y, face_z, edge_x, inverse, values, update), True, 1, 1.0, UNROLL_FINE)
    by, bx, bz = pay.shape[1:]
    shared = near.shape[1]
    at_x, at_y, _, _, odd = place()
    weights = smoothing_weights()
    tile = (bx, bz)
    level1.clear()
    level2.clear()

    own1 = (by // 2) * at_y
    far1 = (by // 2) * (at_y + 2 - 4 * (at_y // 2)) + shared * (1 - odd)
    near1 = (by // 2) * (at_y + 1 - 2 * odd) + shared + shared * (1 - odd)
    for which, ref in enumerate((level1.right, level1.coef)):
        for piece, at in ((pay, own1), (far, far1), (near, near1)):
            for y in range(piece.shape[1]):
                ref[0, at + y] = piece[which, y]

    low1, high1 = level1.pad, level1.rows - level1.pad
    n2 = level2.rows - 1
    even_lane = tile_place(tile, 1) % 2 == 0
    even_row = tile_place(tile, 0) % 2 == 0

    def pair_cells(values):
        values = values + jnp.where(even_lane, turn(values, -1, 1), turn(values, 1, 1))
        return 0.125 * (values + jnp.where(even_row, turn(values, -1, 0), turn(values, 1, 0)))

    level1.set_faces(lambda i, here, inverse: level1.from_zero(i, inverse))
    for weight in weights[1:]:
        level1.smooth(low1, high1 - low1, weight)

    def leftover1(i, applied, here):
        return [(sums, i, [level1.right[0, i] - applied[0]])]

    level1.sweep(low1, high1 - low1, leftover1)
    for j in range(1, n2):
        level2.right[0, j] = pair_cells(sums[0, low1 + 2 * j - 2] + sums[0, low1 + 2 * j - 1])
        level2.coef[0, j] = pair_cells(level1.coef[0, low1 + 2 * j - 2] + level1.coef[0, low1 + 2 * j - 1])

    level2.set_faces(lambda i, here, inverse: level2.from_zero(i, inverse))
    for weight in weights[1:]:
        level2.smooth(1, n2 - 1, weight)

    for j in range(low1, high1):
        level1.values[0, j] = level1.values[0, j] + level2.values[0, 1 + (j - low1) // 2]
    reach = DEGREE + (DEGREE + 2) // 2
    for weight in weights:
        reach -= 1
        count = by // 2 + 2 * reach
        start1 = jnp.clip(shared + own1 - reach, low1, high1 - count)
        level1.smooth(start1, count, weight)

    halo = (fine.rows - by) // 2
    reach = DEGREE + 1
    base = shared + own1
    for y in range(-reach, by + reach):
        coarse = level1.values[0, base + y // 2]
        for part in range(fine.parts):
            values[part, halo + y] = start[part, halo + y] + coarse
    for weight in weights:
        reach -= 1
        fine.smooth(halo - reach, by + 2 * reach, weight)

    own_lane = tile_place(tile, 1) < bz // 2
    top = tile_place(tile, 0) < bx // 2

    def finish(i, applied, here):
        right_row = fine.read(right, i)
        stores = []
        for slot, field in enumerate((here, [right_row[p] - applied[p] for p in range(fine.parts)])):
            cells = []
            for odd_z in (0, 1):
                one, two = field[odd_z], field[2 + odd_z]
                cells.append(
                    jnp.where(
                        top,
                        jnp.where(at_x == 0, one, turn(one, bx // 2, 0)),
                        jnp.where(at_x == 0, turn(two, bx // 2, 0), two),
                    )
                )
            stores.append((rows_out.at[pl.ds(slot, 1)], i - halo, [jnp.where(own_lane, cells[0], turn(cells[1], bz // 2, 1))]))
        return stores

    fine.sweep(halo, by, finish)
    matrix = parity_matrix(bz, True)
    for slot, ref in enumerate((solution_out, residual_out)):
        moved[slot] = exact_dot(rows_out[slot].reshape(by * bx, bz), matrix)
        for x in range(bx):
            ref[x] = moved[slot, pl.ds(parity_place(x, bx), by, stride=bx), :]


def vmem(*shape):
    return pltpu.VMEM(shape, jnp.float32)


def per_device_two_rounds(right_side, coefficient):
    bx, by, bz = right_side.shape
    halo = halo_rows(by)
    shared = by // 4
    in_vmem = pl.BlockSpec(memory_space=pltpu.VMEM)
    params = pltpu.CompilerParams(vmem_limit_bytes=24 * 2**20)
    shape = lambda *sizes: jax.ShapeDtypeStruct(sizes, jnp.float32)

    mine, for_pair, for_inner = pl.pallas_call(
        split_kernel,
        out_shape=(shape(2, by, bx, bz), shape(2, halo, bx, bz), shape(2, halo, bx, bz)),
        in_specs=[in_vmem],
        out_specs=(in_vmem,) * 3,
        scratch_shapes=[vmem(2, bx * by, bz)],
        compiler_params=params,
        name="split",
    )(jnp.stack([right_side, coefficient]))

    pairs = [1, 0, 3, 2]
    inner = [0, 2, 1, 3]
    swap_pairs, swap_inner = list(enumerate(pairs)), list(enumerate(inner))

    def across_x(partner):
        return [(4 * x + y, 4 * (1 - x) + partner[y]) for x in (0, 1) for y in range(4)]

    blocks = {
        "mine": mine,
        "other": lax.ppermute(mine, "gx", [(0, 1), (1, 0)]),
        "pair": lax.ppermute(for_pair, "gy", swap_pairs),
        "pair_other": lax.ppermute(for_pair, ("gx", "gy"), across_x(pairs)),
        "inner": lax.ppermute(for_inner, "gy", swap_inner),
        "inner_other": lax.ppermute(for_inner, ("gx", "gy"), across_x(inner)),
    }
    blocks = list(blocks.values())
    def share(group):
        edges = shape(sum(block.shape[1] for block in group), bx, bz)
        to_mid, to_sib = pl.pallas_call(
            pack_kernel,
            out_shape=(edges, edges),
            in_specs=[in_vmem] * len(group),
            out_specs=(in_vmem,) * 2,
            compiler_params=params,
            name="pack",
        )(*group)
        return lax.ppermute(to_mid, "gz", swap_inner), lax.ppermute(to_sib, "gz", swap_pairs)

    edges = [part for group in GROUPS for part in share([blocks[kind] for kind in group])]

    rows = by + 2 * halo
    field, half_field = (4, rows, bx, bz), (2, rows, bx, bz)
    *fine, pay, far, near = pl.pallas_call(
        down_kernel,
        out_shape=(
            *(shape(*(half_field if number == 4 else field)) for number in range(7)),
            shape(2, by, bx, bz),
            shape(2, by - shared, bx, bz),
            shape(2, shared, bx, bz),
        ),
        in_specs=[in_vmem] * (6 + 2 * len(GROUPS)),
        out_specs=(in_vmem,) * 10,
        scratch_shapes=[vmem(*field), vmem(*field), vmem(1, rows, bx, bz), vmem(1, rows, bx, bz)],
        compiler_params=params,
        name="down",
    )(*blocks, *edges)
    far = lax.ppermute(far, "gy", [(0, 2), (2, 0), (1, 3), (3, 1)])
    near = lax.ppermute(near, "gy", swap_pairs)
    rows1 = by // 2 * lax.axis_size("gy") + 2 * shared
    rows2 = by // 4 * lax.axis_size("gy") + 2
    return pl.pallas_call(
        up_kernel,
        out_shape=(shape(bx, by, bz),) * 2,
        in_specs=[in_vmem] * 10,
        out_specs=(in_vmem,) * 2,
        scratch_shapes=[
            *[vmem(1, rows1, bx, bz)] * 9,
            *[vmem(1, rows2, bx, bz)] * 9,
            vmem(*field),
            vmem(*field),
            vmem(1, rows1, bx, bz),
            vmem(2, bx * by, bz),
            vmem(2, by, bx, bz),
        ],
        compiler_params=params,
        name="up",
    )(pay, far, near, *fine)


def two_rounds_fit(mesh, shape):
    counts = tuple(mesh.shape[name] for name in ("gx", "gy", "gz"))
    bx, by, bz = (size // count for size, count in zip(shape, counts))
    shared = by // 4
    reach_coarse = 4 * DEGREE + 2
    return (
        counts == (2, 4, 4)
        and LEVELS == 3
        and bx == 8
        and by % 8 == 0
        and bz == 128
        and halo_rows(by) <= by
        and by // 2 + reach_coarse + 1 <= 2 * by - shared
        and 2 * reach_coarse + DEGREE + 1 <= bz // 2
    )


def solution(mesh):
    in_specs = (P("gx", "gy", "gz"), P("gx", "gy", "gz"))
    out_specs = (P("gx", "gy", "gz"), P("gx", "gy", "gz"))

    def whole(right_side, coefficient):
        fits = two_rounds_fit(mesh, right_side.shape)
        return jax.shard_map(
            per_device_two_rounds if fits else per_device,
            mesh=mesh,
            in_specs=in_specs,
            out_specs=out_specs,
            check_vma=False,
        )(right_side, coefficient)

    return whole
```

```python
import jax
import jax.numpy as jnp
from jax import lax
from jax.experimental import pallas as pl
from jax.experimental.pallas import tpu as pltpu
from jax.sharding import PartitionSpec as P

LEVELS = 3
DEGREE = 4


cheb_low = 0.3
cheb_high = 2.0


def extended(block, sides, width):
    for axis, dim in sides:
        count = lax.axis_size(axis)
        forward = [(i, i + 1) for i in range(count - 1)]
        backward = [(target, source) for source, target in forward]
        low = lax.ppermute(
            lax.slice_in_dim(block, block.shape[dim] - width, None, axis=dim), axis, forward
        )
        high = lax.ppermute(lax.slice_in_dim(block, 0, width, axis=dim), axis, backward)
        block = jnp.concatenate([low, block, high], axis=dim)
    return block


def face_terms(padded):
    face_x = 0.5 * (padded[1:, 1:-1, 1:-1] + padded[:-1, 1:-1, 1:-1])
    face_y = 0.5 * (padded[1:-1, 1:, 1:-1] + padded[1:-1, :-1, 1:-1])
    face_z = 0.5 * (padded[1:-1, 1:-1, 1:] + padded[1:-1, 1:-1, :-1])
    diagonal = (
        face_x[1:]
        + face_x[:-1]
        + face_y[:, 1:]
        + face_y[:, :-1]
        + face_z[:, :, 1:]
        + face_z[:, :, :-1]
    )
    return (face_x, face_y, face_z, diagonal)


def apply_padded(padded, face_set, factor):
    face_x, face_y, face_z, diagonal = face_set
    flux_x = face_x * (padded[1:, 1:-1, 1:-1] - padded[:-1, 1:-1, 1:-1])
    flux_y = face_y * (padded[1:-1, 1:, 1:-1] - padded[1:-1, :-1, 1:-1])
    flux_z = face_z * (padded[1:-1, 1:-1, 1:] - padded[1:-1, 1:-1, :-1])
    result = (
        flux_x[:-1]
        - flux_x[1:]
        + (flux_y[:, :-1] - flux_y[:, 1:])
        + (flux_z[:, :, :-1] - flux_z[:, :, 1:])
    )
    return factor * result


def fine_halo(values):
    return extended(values, (("gx", 0), ("gy", 1), ("gz", 2)), 1)


def spread_halo(values):
    return extended(values, (("gx", 0), ("gy", 1), ("gz", 2)), 1)


def restrict(values):
    size_x, size_y, size_z = values.shape
    blocks = values.reshape(size_x // 2, 2, size_y // 2, 2, size_z // 2, 2)
    return jnp.mean(blocks, axis=(1, 3, 5))


def prolong(values):
    size_x, size_y, size_z = values.shape
    spread = jnp.broadcast_to(values[:, None, :, None, :, None], (size_x, 2, size_y, 2, size_z, 2))
    return spread.reshape(2 * size_x, 2 * size_y, 2 * size_z)


def trim_cells(values, layers):
    return values[
        layers : values.shape[0] - layers,
        layers : values.shape[1] - layers,
        layers : values.shape[2] - layers,
    ]


def trim_faces(face_set, layers):
    return tuple((trim_cells(member, layers) for member in face_set))


def inside_mask(shape, margin):
    count_x = shape[0]
    count_y = shape[1]
    count_z = shape[2]
    along_x = lax.axis_index("gx") * count_x + jnp.arange(
        -margin, count_x + margin, dtype=jnp.int32
    )
    along_y = lax.axis_index("gy") * count_y + jnp.arange(
        -margin, count_y + margin, dtype=jnp.int32
    )
    along_z = lax.axis_index("gz") * count_z + jnp.arange(
        -margin, count_z + margin, dtype=jnp.int32
    )
    valid_x = (along_x >= 0) & (along_x < count_x * lax.axis_size("gx"))
    valid_y = (along_y >= 0) & (along_y < count_y * lax.axis_size("gy"))
    valid_z = (along_z >= 0) & (along_z < count_z * lax.axis_size("gz"))
    return valid_x[:, None, None] & valid_y[None, :, None] & valid_z[None, None, :]


def deep_smooth(right_wide, start_wide, face_wide, valid_wide):
    centre = 0.5 * (cheb_high + cheb_low)
    half_width = 0.5 * (cheb_high - cheb_low)
    sigma_val = centre / half_width
    rho_now = 1.0 / sigma_val
    safe_diag = jnp.where(valid_wide, face_wide[3], 1.0)
    if start_wide is None:
        update = jnp.where(valid_wide, right_wide / (1.0 * safe_diag) / centre, 0.0)
        iterate = update
        lost = 0
    else:
        leftover = trim_cells(right_wide, 1) - apply_padded(
            start_wide, trim_faces(face_wide, 1), 1.0
        )
        update = jnp.where(
            trim_cells(valid_wide, 1), leftover / (1.0 * trim_cells(safe_diag, 1)) / centre, 0.0
        )
        iterate = trim_cells(start_wide, 1) + update
        lost = 1
    for sweep_no in range(DEGREE - 1):
        lost = lost + 1
        leftover = trim_cells(right_wide, lost) - apply_padded(
            iterate, trim_faces(face_wide, lost), 1.0
        )
        rho_next = 1.0 / (2.0 * sigma_val - rho_now)
        fresh = rho_next * rho_now * trim_cells(update, 1) + 2.0 * rho_next / half_width * (
            leftover / (1.0 * trim_cells(safe_diag, lost))
        )
        update = jnp.where(trim_cells(valid_wide, lost), fresh, 0.0)
        iterate = trim_cells(iterate, 1) + update
        rho_now = rho_next
    return (iterate, lost)


def smooth(right, initial, face_set, factor, padder):
    diagonal = face_set[3]
    centre = 0.5 * (cheb_high + cheb_low)
    half_width = 0.5 * (cheb_high - cheb_low)
    sigma_val = centre / half_width
    rho_now = 1.0 / sigma_val
    if initial is None:
        iterate = jnp.zeros_like(right)
        leftover = right
    else:
        iterate = initial
        leftover = right - apply_padded(padder(initial), face_set, factor)
    update = leftover / (factor * diagonal) / centre
    iterate = iterate + update
    for sweep_no in range(DEGREE - 1):
        leftover = right - apply_padded(padder(iterate), face_set, factor)
        rho_next = 1.0 / (2.0 * sigma_val - rho_now)
        update = rho_next * rho_now * update + 2.0 * rho_next / half_width * (
            leftover / (factor * diagonal)
        )
        iterate = iterate + update
        rho_now = rho_next
    return iterate


def per_device(right_side, coefficient):
    depth = DEGREE
    stacked = jnp.stack([right_side, coefficient])
    widened = extended(stacked, (("gx", 1), ("gy", 2), ("gz", 3)), depth + 1)
    right_wide = trim_cells(widened[0], 1)
    face_wide = face_terms(widened[1])
    valid_wide = inside_mask(right_side.shape, depth)
    fine_set = trim_faces(face_wide, depth)
    partial_value, lost = deep_smooth(right_wide, None, face_wide, valid_wide)
    leftover = right_side - apply_padded(partial_value, trim_faces(face_wide, depth), 1.0)
    iterate = trim_cells(partial_value, 1)
    coarse_right = restrict(leftover)
    coarse_coef = restrict(coefficient)
    rights = [coarse_right]
    face_sets = []
    iterates = []
    for level_no in range(1, LEVELS):
        factor = 0.25**level_no
        face_set = face_terms(spread_halo(coarse_coef))
        face_sets.append(face_set)
        current = smooth(rights[-1], None, face_set, factor, spread_halo)
        iterates.append(current)
        if level_no < LEVELS - 1:
            remains = rights[-1] - apply_padded(spread_halo(current), face_set, factor)
            rights.append(restrict(remains))
            coarse_coef = restrict(coarse_coef)
    level_no = 1
    slot_no = level_no - 1
    iterates[slot_no] = smooth(
        rights[slot_no],
        iterates[slot_no] + prolong(iterates[slot_no + 1]),
        face_sets[slot_no],
        0.25**level_no,
        spread_halo,
    )
    correction = iterates[0]
    start = iterate + prolong(correction)
    start_wide = extended(start, (("gx", 0), ("gy", 1), ("gz", 2)), depth)
    solution, lost = deep_smooth(right_wide, start_wide, face_wide, valid_wide)
    residual = right_side - apply_padded(fine_halo(solution), fine_set, 1.0)
    return (solution, residual)


UNROLL_FINE = 26
GROUPS = ((0, 1, 2), (4, 5, 3))
UNROLL_COARSE = 64


def place():
    at_x, at_y, at_z = (lax.axis_index(name) for name in ("gx", "gy", "gz"))
    return at_x, at_y, at_z, lax.rem(at_z, 2), lax.rem(at_y, 2)


def in_the_middle(at):
    return (at == 1) | (at == 2)


def smoothing_weights():
    centre = 0.5 * (cheb_high + cheb_low)
    half_width = 0.5 * (cheb_high - cheb_low)
    sigma_val = centre / half_width
    rho_now = 1.0 / sigma_val
    weights = [(0.0, 1.0 / centre)]
    for _ in range(DEGREE - 1):
        rho_next = 1.0 / (2.0 * sigma_val - rho_now)
        weights.append((rho_next * rho_now, 2.0 * rho_next / half_width))
        rho_now = rho_next
    return weights


def turn(values, shift, axis):
    return pltpu.roll(values, shift % values.shape[axis], axis)


def run(low, count, body, carry, unroll):
    steps = -(-count // unroll)
    unroll = -(-count // steps)

    def several(start, state, rows):
        pending = []
        for k in range(rows):
            state, stores = body(start + k, state)
            pending += stores
        for ref, i, values in pending:
            for part, value in enumerate(values):
                ref[part, i] = value
        return state

    whole = count // unroll
    if whole == 1:
        carry = several(low, carry, unroll)
    else:
        carry = lax.fori_loop(0, whole, lambda step, state: several(low + step * unroll, state, unroll), carry)
    if count > whole * unroll:
        carry = several(low + whole * unroll, carry, count - whole * unroll)
    return carry


def tile_place(shape, axis):
    return lax.broadcasted_iota(jnp.int32, shape, axis)


class Level:
    def __init__(self, refs, split, step, scale, unroll, pad=1):
        self.right, self.diagonal, *self.sides, self.values, self.update, self.coef, self.source = refs
        self.parts, self.rows = self.right.shape[:2]
        self.tile = self.right.shape[2:]
        self.split, self.step, self.half, self.unroll, self.pad = split, step, 0.5 * scale, unroll, pad
        self.first = tile_place(self.tile, 0) < step
        self.last = tile_place(self.tile, 0) >= self.tile[0] - step

    def read(self, ref, i):
        return [ref[part, i] for part in range(ref.shape[0])]

    def clear(self):
        for i in range(self.rows):
            self.coef[0, i] = self.values[0, i] = self.source[0, i] = jnp.zeros(self.tile, jnp.float32)

    def next_x(self, v, part):
        if self.split and part < 2:
            return v[part + 2]
        return turn(v[part - 2 if self.split else part], -self.step, 0)

    def last_x(self, v, part):
        if self.split and part >= 2:
            return v[part - 2]
        return turn(v[part + 2 if self.split else part], self.step, 0)

    def next_z(self, v, part):
        if self.split and part % 2 == 0:
            return v[part + 1]
        return turn(v[part - 1 if self.split else part], -self.step, 1)

    def last_z(self, v, part):
        if self.split and part % 2 == 1:
            return v[part - 1]
        return turn(v[part + 1 if self.split else part], self.step, 1)

    def begin(self, use):
        half = self.half
        parts = range(self.parts)
        first = smoothing_weights()[0][1]

        def body(i, carry):
            here, below = carry
            above = self.read(self.coef, i + 1)
            source = self.read(self.source, i)
            upper = [half * (here[p] + above[p]) for p in parts]
            to_next = [here[p] + self.next_x(here, p) for p in parts]
            along_x = []
            for p in parts:
                at_end = not self.split or p >= 2
                along_x.append(half * (jnp.where(self.last, here[p], to_next[p]) if at_end else to_next[p]))
            along_z = [half * (here[p] + self.next_z(here, p)) for p in parts]
            fields = [[] for _ in range(8)]
            for p in parts:
                to_last = self.last_x(along_x, p)
                faces = [upper[p], below[p], along_x[p], to_last, along_z[p], self.last_z(along_z, p)]
                inner = list(faces)
                if not self.split or p >= 2:
                    inner[2] = jnp.where(self.last, 0.0, faces[2])
                if not self.split or p < 2:
                    faces[3] = jnp.where(self.first, half * here[p], to_last)
                    inner[3] = jnp.where(self.first, 0.0, to_last)
                diagonal = (faces[0] + faces[1]) + (faces[2] + faces[3]) + (faces[4] + faces[5])
                inverse = jnp.where(here[p] > 0.0, 1.0 / diagonal, 0.0)
                for field, value in zip(fields, [source[p] * inverse, diagonal, *(face * inverse for face in inner)]):
                    field.append(value)
            step = [value * first for value in fields[0]]
            refs = (self.right, self.diagonal, *self.sides, self.values, self.update)
            stores = [(ref, i, field) for ref, field in zip(refs, [*fields, step, step])]
            return (above, upper), stores + use(i, here)

        low, high = self.pad, self.rows - self.pad
        here, before = self.read(self.coef, low), self.read(self.coef, low - 1)
        run(low, high - low, body, (here, [half * (here[p] + before[p]) for p in parts]), self.unroll)

    def sweep(self, low, count, use):
        parts = range(self.parts)

        def body(i, carry):
            below, here = carry
            above = self.read(self.values, i + 1)
            right = self.read(self.right, i)
            up, down, ahead, behind, right_z, left_z = (self.read(ref, i) for ref in self.sides)
            left = [
                ((right[p] - here[p]) + (up[p] * above[p] + down[p] * below[p]))
                + (ahead[p] * self.next_x(here, p) + behind[p] * self.last_x(here, p))
                + (right_z[p] * self.next_z(here, p) + left_z[p] * self.last_z(here, p))
                for p in parts
            ]
            return (here, above), use(i, left, here)

        run(low, count, body, (self.read(self.values, low - 1), self.read(self.values, low)), self.unroll)

    def smooth(self, low, count, weight):
        keep, gain = weight

        def use(i, left, here):
            step = [gain * left[p] for p in range(self.parts)]
            if keep:
                update = self.read(self.update, i)
                step = [keep * update[p] + step[p] for p in range(self.parts)]
            return [(self.update, i, step), (self.values, i, [here[p] + step[p] for p in range(self.parts)])]

        self.sweep(low, count, use)

    def residual(self, i, left):
        return [value * factor for value, factor in zip(left, self.read(self.diagonal, i))]


def total(items):
    items = list(items)
    while len(items) > 1:
        items = [sum(items[k : k + 2][1:], items[k]) for k in range(0, len(items), 2)]
    return items[0]


def exact_dot(left, right):
    return jnp.dot(left, right, precision=lax.Precision.HIGHEST, preferred_element_type=jnp.float32)


def parity_matrix(size, back):
    row, column = tile_place((size, size), 0), tile_place((size, size), 1)
    if back:
        row, column = column, row
    hit = column == row // 2 + (row % 2) * (size // 2)
    return jnp.where(hit, 1.0, 0.0).astype(jnp.float32)


def parity_place(x, count):
    return x // 2 + (x % 2) * (count // 2)


def halo_rows(by):
    return 2 * (by // 4) + DEGREE + 1


def split_kernel(fields, out, pair_out, inner_out, rows):
    _, bx, by, bz = fields.shape
    _, _, _, _, odd = place()
    halo = halo_rows(by)
    matrix = parity_matrix(bz, False)
    for which in (0, 1):
        moved = exact_dot(fields[which].reshape(bx * by, bz), matrix)
        for x in range(bx):
            at = parity_place(x, bx) * by
            rows[which, at : at + by] = moved[x * by : (x + 1) * by]
        for y in range(by):
            out[which, y] = rows[which, pl.ds(y, bx, stride=by), :]
    for which in (0, 1):
        pair_out[which] = out[which, pl.ds((1 - odd) * (by - halo), halo)]
        inner_out[which] = out[which, pl.ds(odd * (by - halo), halo)]


def pack_kernel(*refs):
    *blocks, across_out, beside_out = refs
    _, _, _, core, _ = place()
    tile = across_out.shape[1:]
    quarter = tile[1] // 4
    low = tile_place(tile, 1) % (2 * quarter) < quarter
    at = 0
    for block in blocks:
        for y in range(block.shape[1]):
            right, coef = block[0, y], block[1, y]
            first = jnp.where(low, right, turn(coef, quarter, 1))
            last = jnp.where(low, turn(coef, -quarter, 1), right)
            across_out[at] = jnp.where(core == 0, first, last)
            beside_out[at] = jnp.where(core == 0, last, first)
            at += 1


def down_kernel(mine, other, pair, pair_other, inner, inner_other, *refs):
    edges, refs = refs[: 2 * len(GROUPS)], refs[2 * len(GROUPS) :]
    fields, (pay_out, far_out, near_out), (update, coef, right, sums, coefs) = refs[:9], refs[9:12], refs[12:]
    level = Level((*fields, update, coef, right), True, 1, 1.0, UNROLL_FINE)
    by, bx, bz = mine.shape[1:]
    halo = pair.shape[1]
    at_x, at_y, at_z, core, odd = place()
    tile = (bx, bz)
    lane = tile_place(tile, 1)
    quarter = bz // 4
    is_own = lane < bz // 2
    low = lane % (bz // 2) < quarter
    outside = (low == (core == 1)) & ~in_the_middle(at_z)
    top = tile_place(tile, 0) < bx // 2

    def columns(block, y, kind):
        blocks = (mine, other, pair, pair_other, inner, inner_other)
        number = next(number for number, group in enumerate(GROUPS) if kind in group)
        before = GROUPS[number][: GROUPS[number].index(kind)]
        at = y + sum(blocks[earlier].shape[1] for earlier in before)
        over, beside = edges[2 * number][at], edges[2 * number + 1][at]
        first = jnp.where(core == 1, over, beside)
        last = jnp.where(core == 1, beside, over)
        side, own = jnp.where(low, first, last), block[0, y]
        right_cells = [
            jnp.where(is_own, own, turn(side, bz // 2, 1)),
            jnp.where(is_own, turn(own, bz // 2, 1), side),
        ]
        side, own = jnp.where(low, last, first), block[1, y]
        up, down = turn(side, quarter, 1), turn(side, -quarter, 1)
        coef_cells = [
            jnp.where(is_own, own, jnp.where(outside, 0.0, jnp.where(low, up, down))),
            jnp.where(is_own, turn(own, bz // 2, 1), jnp.where(outside, 0.0, jnp.where(low, down, up))),
        ]
        return right_cells, coef_cells

    for kind, (near, far, row) in zip((0, 2, 4), (
        (mine, other, halo),
        (pair, pair_other, (1 - odd) * (halo + by)),
        (inner, inner_other, odd * (halo + by)),
    )):
        count = near.shape[1]

        def assemble(y, carry, near=near, far=far, row=row, kind=kind):
            both = zip(columns(near, y, kind), columns(far, y, kind + 1))
            stores = []
            for ref, (here, there) in zip((right, coef), both):
                for odd_z in (0, 1):
                    one = jnp.where(at_x == 0, here[odd_z], there[odd_z])
                    two = jnp.where(at_x == 0, there[odd_z], here[odd_z])
                    cells = jnp.where(top, one, turn(two, bx // 2, 0)), jnp.where(top, turn(one, bx // 2, 0), two)
                    for odd_x in (0, 1):
                        value = cells[odd_x]
                        if ref is coef and near is inner:
                            value = jnp.where(in_the_middle(at_y), value, 0.0)
                        stores.append((ref.at[pl.ds(2 * odd_x + odd_z, 1)], row + y, [value]))
            return carry, stores

        run(0, count, assemble, 0, 16)

    level.begin(lambda i, here: [(coefs, i, [total(here)])])
    edge = 1
    for weight in smoothing_weights()[1:]:
        edge += 1
        level.smooth(edge, level.rows - 2 * edge, weight)

    def leftover(i, left, here):
        return [(sums, i, [total(level.residual(i, left))])]

    edge += 1
    level.sweep(edge, level.rows - 2 * edge, leftover)
    for which, ref in enumerate((sums, coefs)):
        for y in range(by):
            pay_out[which, y] = 0.125 * (ref[0, edge + 2 * y] + ref[0, edge + 2 * y + 1])
        shared = by // 4
        far_out[which] = pay_out[which, pl.ds(shared * (1 - odd), by - shared)]
        near_out[which] = pay_out[which, pl.ds(shared * (1 + odd), shared)]


def up_kernel(pay, far, near, *refs):
    fields, start, (solution_out, residual_out), refs = refs[:8], refs[8], refs[9:11], refs[11:]
    level1 = Level(refs[:12], False, 1, 0.25, UNROLL_COARSE, near.shape[1])
    level2 = Level(refs[12:24], False, 2, 0.0625, UNROLL_COARSE)
    values, update, sums, moved, rows_out = refs[24:]
    fine = Level((*fields, values, update, None, None), True, 1, 1.0, UNROLL_FINE)
    by, bx, bz = pay.shape[1:]
    shared = near.shape[1]
    at_x, at_y, _, _, odd = place()
    weights = smoothing_weights()
    tile = (bx, bz)
    level1.clear()
    level2.clear()

    own1 = (by // 2) * at_y
    far1 = (by // 2) * (at_y + 2 - 4 * (at_y // 2)) + shared * (1 - odd)
    near1 = (by // 2) * (at_y + 1 - 2 * odd) + shared + shared * (1 - odd)
    for which, ref in enumerate((level1.source, level1.coef)):
        for piece, at in ((pay, own1), (far, far1), (near, near1)):
            for y in range(piece.shape[1]):
                ref[0, at + y] = piece[which, y]

    low1, high1 = level1.pad, level1.rows - level1.pad
    n2 = level2.rows - 1
    even_lane = tile_place(tile, 1) % 2 == 0
    even_row = tile_place(tile, 0) % 2 == 0

    def pair_cells(values):
        values = values + jnp.where(even_lane, turn(values, -1, 1), turn(values, 1, 1))
        return 0.125 * (values + jnp.where(even_row, turn(values, -1, 0), turn(values, 1, 0)))

    level1.begin(lambda i, here: [])
    for weight in weights[1:]:
        level1.smooth(low1, high1 - low1, weight)

    def leftover1(i, left, here):
        return [(sums, i, level1.residual(i, left))]

    level1.sweep(low1, high1 - low1, leftover1)
    for j in range(1, n2):
        level2.source[0, j] = pair_cells(sums[0, low1 + 2 * j - 2] + sums[0, low1 + 2 * j - 1])
        level2.coef[0, j] = pair_cells(level1.coef[0, low1 + 2 * j - 2] + level1.coef[0, low1 + 2 * j - 1])

    level2.begin(lambda i, here: [])
    for weight in weights[1:]:
        level2.smooth(1, n2 - 1, weight)

    for j in range(low1, high1):
        level1.values[0, j] = level1.values[0, j] + level2.values[0, 1 + (j - low1) // 2]
    reach = DEGREE + (DEGREE + 2) // 2
    for weight in weights:
        reach -= 1
        count = by // 2 + 2 * reach
        start1 = jnp.clip(shared + own1 - reach, low1, high1 - count)
        level1.smooth(start1, count, weight)

    halo = (fine.rows - by) // 2
    reach = DEGREE + 1
    base = shared + own1
    for y in range(-reach, by + reach):
        coarse = level1.values[0, base + y // 2]
        for part in range(fine.parts):
            values[part, halo + y] = start[part, halo + y] + coarse
    for weight in weights:
        reach -= 1
        fine.smooth(halo - reach, by + 2 * reach, weight)

    own_lane = tile_place(tile, 1) < bz // 2
    top = tile_place(tile, 0) < bx // 2

    def finish(i, left, here):
        stores = []
        for slot, field in enumerate((here, fine.residual(i, left))):
            cells = []
            for odd_z in (0, 1):
                one, two = field[odd_z], field[2 + odd_z]
                cells.append(
                    jnp.where(
                        top,
                        jnp.where(at_x == 0, one, turn(one, bx // 2, 0)),
                        jnp.where(at_x == 0, turn(two, bx // 2, 0), two),
                    )
                )
            stores.append((rows_out.at[pl.ds(slot, 1)], i - halo, [jnp.where(own_lane, cells[0], turn(cells[1], bz // 2, 1))]))
        return stores

    fine.sweep(halo, by, finish)
    matrix = parity_matrix(bz, True)
    for slot, ref in enumerate((solution_out, residual_out)):
        moved[slot] = exact_dot(rows_out[slot].reshape(by * bx, bz), matrix)
        for x in range(bx):
            ref[x] = moved[slot, pl.ds(parity_place(x, bx), by, stride=bx), :]


def vmem(*shape):
    return pltpu.VMEM(shape, jnp.float32)


def per_device_two_rounds(right_side, coefficient):
    bx, by, bz = right_side.shape
    halo = halo_rows(by)
    shared = by // 4
    in_vmem = pl.BlockSpec(memory_space=pltpu.VMEM)
    params = pltpu.CompilerParams(vmem_limit_bytes=24 * 2**20)
    shape = lambda *sizes: jax.ShapeDtypeStruct(sizes, jnp.float32)

    mine, for_pair, for_inner = pl.pallas_call(
        split_kernel,
        out_shape=(shape(2, by, bx, bz), shape(2, halo, bx, bz), shape(2, halo, bx, bz)),
        in_specs=[in_vmem],
        out_specs=(in_vmem,) * 3,
        scratch_shapes=[vmem(2, bx * by, bz)],
        compiler_params=params,
        name="split",
    )(jnp.stack([right_side, coefficient]))

    pairs = [1, 0, 3, 2]
    inner = [0, 2, 1, 3]
    swap_pairs, swap_inner = list(enumerate(pairs)), list(enumerate(inner))

    def across_x(partner):
        return [(4 * x + y, 4 * (1 - x) + partner[y]) for x in (0, 1) for y in range(4)]

    blocks = {
        "mine": mine,
        "other": lax.ppermute(mine, "gx", [(0, 1), (1, 0)]),
        "pair": lax.ppermute(for_pair, "gy", swap_pairs),
        "pair_other": lax.ppermute(for_pair, ("gx", "gy"), across_x(pairs)),
        "inner": lax.ppermute(for_inner, "gy", swap_inner),
        "inner_other": lax.ppermute(for_inner, ("gx", "gy"), across_x(inner)),
    }
    blocks = list(blocks.values())
    def share(group):
        edges = shape(sum(block.shape[1] for block in group), bx, bz)
        to_mid, to_sib = pl.pallas_call(
            pack_kernel,
            out_shape=(edges, edges),
            in_specs=[in_vmem] * len(group),
            out_specs=(in_vmem,) * 2,
            compiler_params=params,
            name="pack",
        )(*group)
        return lax.ppermute(to_mid, "gz", swap_inner), lax.ppermute(to_sib, "gz", swap_pairs)

    edges = [part for group in GROUPS for part in share([blocks[kind] for kind in group])]

    rows = by + 2 * halo
    field = (4, rows, bx, bz)
    *fine, pay, far, near = pl.pallas_call(
        down_kernel,
        out_shape=(
            *[shape(*field)] * 9,
            shape(2, by, bx, bz),
            shape(2, by - shared, bx, bz),
            shape(2, shared, bx, bz),
        ),
        in_specs=[in_vmem] * (6 + 2 * len(GROUPS)),
        out_specs=(in_vmem,) * 12,
        scratch_shapes=[*[vmem(*field)] * 3, vmem(1, rows, bx, bz), vmem(1, rows, bx, bz)],
        compiler_params=params,
        name="down",
    )(*blocks, *edges)
    far = lax.ppermute(far, "gy", [(0, 2), (2, 0), (1, 3), (3, 1)])
    near = lax.ppermute(near, "gy", swap_pairs)
    rows1 = by // 2 * lax.axis_size("gy") + 2 * shared
    rows2 = by // 4 * lax.axis_size("gy") + 2
    return pl.pallas_call(
        up_kernel,
        out_shape=(shape(bx, by, bz),) * 2,
        in_specs=[in_vmem] * 12,
        out_specs=(in_vmem,) * 2,
        scratch_shapes=[
            *[vmem(1, rows1, bx, bz)] * 12,
            *[vmem(1, rows2, bx, bz)] * 12,
            vmem(*field),
            vmem(*field),
            vmem(1, rows1, bx, bz),
            vmem(2, bx * by, bz),
            vmem(2, by, bx, bz),
        ],
        compiler_params=params,
        name="up",
    )(pay, far, near, *fine)


def two_rounds_fit(mesh, shape):
    counts = tuple(mesh.shape[name] for name in ("gx", "gy", "gz"))
    bx, by, bz = (size // count for size, count in zip(shape, counts))
    shared = by // 4
    reach_coarse = 4 * DEGREE + 2
    return (
        counts == (2, 4, 4)
        and LEVELS == 3
        and bx == 8
        and by % 8 == 0
        and bz == 128
        and halo_rows(by) <= by
        and by // 2 + reach_coarse + 1 <= 2 * by - shared
        and 2 * reach_coarse + DEGREE + 1 <= bz // 2
    )


def solution(mesh):
    in_specs = (P("gx", "gy", "gz"), P("gx", "gy", "gz"))
    out_specs = (P("gx", "gy", "gz"), P("gx", "gy", "gz"))

    def whole(right_side, coefficient):
        fits = two_rounds_fit(mesh, right_side.shape)
        return jax.shard_map(
            per_device_two_rounds if fits else per_device,
            mesh=mesh,
            in_specs=in_specs,
            out_specs=out_specs,
            check_vma=False,
        )(right_side, coefficient)

    return whole
```

```python
import jax
import jax.numpy as jnp
from jax import lax
from jax.experimental import pallas as pl
from jax.experimental.pallas import tpu as pltpu
from jax.sharding import PartitionSpec as P

LEVELS = 3
DEGREE = 4


cheb_low = 0.3
cheb_high = 2.0


def extended(block, sides, width):
    for axis, dim in sides:
        count = lax.axis_size(axis)
        forward = [(i, i + 1) for i in range(count - 1)]
        backward = [(target, source) for source, target in forward]
        low = lax.ppermute(
            lax.slice_in_dim(block, block.shape[dim] - width, None, axis=dim), axis, forward
        )
        high = lax.ppermute(lax.slice_in_dim(block, 0, width, axis=dim), axis, backward)
        block = jnp.concatenate([low, block, high], axis=dim)
    return block


def face_terms(padded):
    face_x = 0.5 * (padded[1:, 1:-1, 1:-1] + padded[:-1, 1:-1, 1:-1])
    face_y = 0.5 * (padded[1:-1, 1:, 1:-1] + padded[1:-1, :-1, 1:-1])
    face_z = 0.5 * (padded[1:-1, 1:-1, 1:] + padded[1:-1, 1:-1, :-1])
    diagonal = (
        face_x[1:]
        + face_x[:-1]
        + face_y[:, 1:]
        + face_y[:, :-1]
        + face_z[:, :, 1:]
        + face_z[:, :, :-1]
    )
    return (face_x, face_y, face_z, diagonal)


def apply_padded(padded, face_set, factor):
    face_x, face_y, face_z, diagonal = face_set
    flux_x = face_x * (padded[1:, 1:-1, 1:-1] - padded[:-1, 1:-1, 1:-1])
    flux_y = face_y * (padded[1:-1, 1:, 1:-1] - padded[1:-1, :-1, 1:-1])
    flux_z = face_z * (padded[1:-1, 1:-1, 1:] - padded[1:-1, 1:-1, :-1])
    result = (
        flux_x[:-1]
        - flux_x[1:]
        + (flux_y[:, :-1] - flux_y[:, 1:])
        + (flux_z[:, :, :-1] - flux_z[:, :, 1:])
    )
    return factor * result


def fine_halo(values):
    return extended(values, (("gx", 0), ("gy", 1), ("gz", 2)), 1)


def spread_halo(values):
    return extended(values, (("gx", 0), ("gy", 1), ("gz", 2)), 1)


def restrict(values):
    size_x, size_y, size_z = values.shape
    blocks = values.reshape(size_x // 2, 2, size_y // 2, 2, size_z // 2, 2)
    return jnp.mean(blocks, axis=(1, 3, 5))


def prolong(values):
    size_x, size_y, size_z = values.shape
    spread = jnp.broadcast_to(values[:, None, :, None, :, None], (size_x, 2, size_y, 2, size_z, 2))
    return spread.reshape(2 * size_x, 2 * size_y, 2 * size_z)


def trim_cells(values, layers):
    return values[
        layers : values.shape[0] - layers,
        layers : values.shape[1] - layers,
        layers : values.shape[2] - layers,
    ]


def trim_faces(face_set, layers):
    return tuple((trim_cells(member, layers) for member in face_set))


def inside_mask(shape, margin):
    count_x = shape[0]
    count_y = shape[1]
    count_z = shape[2]
    along_x = lax.axis_index("gx") * count_x + jnp.arange(
        -margin, count_x + margin, dtype=jnp.int32
    )
    along_y = lax.axis_index("gy") * count_y + jnp.arange(
        -margin, count_y + margin, dtype=jnp.int32
    )
    along_z = lax.axis_index("gz") * count_z + jnp.arange(
        -margin, count_z + margin, dtype=jnp.int32
    )
    valid_x = (along_x >= 0) & (along_x < count_x * lax.axis_size("gx"))
    valid_y = (along_y >= 0) & (along_y < count_y * lax.axis_size("gy"))
    valid_z = (along_z >= 0) & (along_z < count_z * lax.axis_size("gz"))
    return valid_x[:, None, None] & valid_y[None, :, None] & valid_z[None, None, :]


def deep_smooth(right_wide, start_wide, face_wide, valid_wide):
    centre = 0.5 * (cheb_high + cheb_low)
    half_width = 0.5 * (cheb_high - cheb_low)
    sigma_val = centre / half_width
    rho_now = 1.0 / sigma_val
    safe_diag = jnp.where(valid_wide, face_wide[3], 1.0)
    if start_wide is None:
        update = jnp.where(valid_wide, right_wide / (1.0 * safe_diag) / centre, 0.0)
        iterate = update
        lost = 0
    else:
        leftover = trim_cells(right_wide, 1) - apply_padded(
            start_wide, trim_faces(face_wide, 1), 1.0
        )
        update = jnp.where(
            trim_cells(valid_wide, 1), leftover / (1.0 * trim_cells(safe_diag, 1)) / centre, 0.0
        )
        iterate = trim_cells(start_wide, 1) + update
        lost = 1
    for sweep_no in range(DEGREE - 1):
        lost = lost + 1
        leftover = trim_cells(right_wide, lost) - apply_padded(
            iterate, trim_faces(face_wide, lost), 1.0
        )
        rho_next = 1.0 / (2.0 * sigma_val - rho_now)
        fresh = rho_next * rho_now * trim_cells(update, 1) + 2.0 * rho_next / half_width * (
            leftover / (1.0 * trim_cells(safe_diag, lost))
        )
        update = jnp.where(trim_cells(valid_wide, lost), fresh, 0.0)
        iterate = trim_cells(iterate, 1) + update
        rho_now = rho_next
    return (iterate, lost)


def smooth(right, initial, face_set, factor, padder):
    diagonal = face_set[3]
    centre = 0.5 * (cheb_high + cheb_low)
    half_width = 0.5 * (cheb_high - cheb_low)
    sigma_val = centre / half_width
    rho_now = 1.0 / sigma_val
    if initial is None:
        iterate = jnp.zeros_like(right)
        leftover = right
    else:
        iterate = initial
        leftover = right - apply_padded(padder(initial), face_set, factor)
    update = leftover / (factor * diagonal) / centre
    iterate = iterate + update
    for sweep_no in range(DEGREE - 1):
        leftover = right - apply_padded(padder(iterate), face_set, factor)
        rho_next = 1.0 / (2.0 * sigma_val - rho_now)
        update = rho_next * rho_now * update + 2.0 * rho_next / half_width * (
            leftover / (factor * diagonal)
        )
        iterate = iterate + update
        rho_now = rho_next
    return iterate


def per_device(right_side, coefficient):
    depth = DEGREE
    stacked = jnp.stack([right_side, coefficient])
    widened = extended(stacked, (("gx", 1), ("gy", 2), ("gz", 3)), depth + 1)
    right_wide = trim_cells(widened[0], 1)
    face_wide = face_terms(widened[1])
    valid_wide = inside_mask(right_side.shape, depth)
    fine_set = trim_faces(face_wide, depth)
    partial_value, lost = deep_smooth(right_wide, None, face_wide, valid_wide)
    leftover = right_side - apply_padded(partial_value, trim_faces(face_wide, depth), 1.0)
    iterate = trim_cells(partial_value, 1)
    coarse_right = restrict(leftover)
    coarse_coef = restrict(coefficient)
    rights = [coarse_right]
    face_sets = []
    iterates = []
    for level_no in range(1, LEVELS):
        factor = 0.25**level_no
        face_set = face_terms(spread_halo(coarse_coef))
        face_sets.append(face_set)
        current = smooth(rights[-1], None, face_set, factor, spread_halo)
        iterates.append(current)
        if level_no < LEVELS - 1:
            remains = rights[-1] - apply_padded(spread_halo(current), face_set, factor)
            rights.append(restrict(remains))
            coarse_coef = restrict(coarse_coef)
    level_no = 1
    slot_no = level_no - 1
    iterates[slot_no] = smooth(
        rights[slot_no],
        iterates[slot_no] + prolong(iterates[slot_no + 1]),
        face_sets[slot_no],
        0.25**level_no,
        spread_halo,
    )
    correction = iterates[0]
    start = iterate + prolong(correction)
    start_wide = extended(start, (("gx", 0), ("gy", 1), ("gz", 2)), depth)
    solution, lost = deep_smooth(right_wide, start_wide, face_wide, valid_wide)
    residual = right_side - apply_padded(fine_halo(solution), fine_set, 1.0)
    return (solution, residual)


UNROLL_FINE = 26
GROUPS = ((0, 1, 2), (4, 5, 3))
UNROLL_COARSE = 64


def place():
    at_x, at_y, at_z = (lax.axis_index(name) for name in ("gx", "gy", "gz"))
    return at_x, at_y, at_z, lax.rem(at_z, 2), lax.rem(at_y, 2)


def in_the_middle(at):
    return (at == 1) | (at == 2)


def smoothing_weights():
    centre = 0.5 * (cheb_high + cheb_low)
    half_width = 0.5 * (cheb_high - cheb_low)
    sigma_val = centre / half_width
    rho_now = 1.0 / sigma_val
    weights = [(0.0, 1.0 / centre)]
    for _ in range(DEGREE - 1):
        rho_next = 1.0 / (2.0 * sigma_val - rho_now)
        weights.append((rho_next * rho_now, 2.0 * rho_next / half_width))
        rho_now = rho_next
    return weights


def turn(values, shift, axis):
    return pltpu.roll(values, shift % values.shape[axis], axis)


def run(low, count, body, carry, unroll):
    steps = -(-count // unroll)
    unroll = -(-count // steps)

    def several(start, state, rows):
        pending = []
        for k in range(rows):
            state, stores = body(start + k, state)
            pending += stores
        for ref, i, values in pending:
            for part, value in enumerate(values):
                ref[part, i] = value
        return state

    whole = count // unroll
    if whole == 1:
        carry = several(low, carry, unroll)
    else:
        carry = lax.fori_loop(0, whole, lambda step, state: several(low + step * unroll, state, unroll), carry)
    if count > whole * unroll:
        carry = several(low + whole * unroll, carry, count - whole * unroll)
    return carry


def tile_place(shape, axis):
    return lax.broadcasted_iota(jnp.int32, shape, axis)


class Level:
    def __init__(self, refs, split, step, scale, unroll, pad=1):
        self.right, self.diagonal, *self.sides, self.values, self.update, self.coef, self.source = refs
        self.parts, self.rows = self.right.shape[:2]
        self.tile = self.right.shape[2:]
        self.split, self.step, self.half, self.unroll, self.pad = split, step, 0.5 * scale, unroll, pad
        self.first = tile_place(self.tile, 0) < step
        self.last = tile_place(self.tile, 0) >= self.tile[0] - step

    def read(self, ref, i):
        return [ref[part, i] for part in range(ref.shape[0])]

    def clear(self):
        for i in range(self.rows):
            self.coef[0, i] = self.values[0, i] = self.source[0, i] = jnp.zeros(self.tile, jnp.float32)

    def next_x(self, v, part):
        if self.split and part < 2:
            return v[part + 2]
        return turn(v[part - 2 if self.split else part], -self.step, 0)

    def last_x(self, v, part):
        if self.split and part >= 2:
            return v[part - 2]
        return turn(v[part + 2 if self.split else part], self.step, 0)

    def next_z(self, v, part):
        if self.split and part % 2 == 0:
            return v[part + 1]
        return turn(v[part - 1 if self.split else part], -self.step, 1)

    def last_z(self, v, part):
        if self.split and part % 2 == 1:
            return v[part - 1]
        return turn(v[part + 1 if self.split else part], self.step, 1)

    def begin(self, use):
        half = self.half
        parts = range(self.parts)
        first = smoothing_weights()[0][1]

        def body(i, carry):
            here, below = carry
            above = self.read(self.coef, i + 1)
            source = self.read(self.source, i)
            upper = [half * (here[p] + above[p]) for p in parts]
            to_next = [here[p] + self.next_x(here, p) for p in parts]
            along_x = []
            for p in parts:
                at_end = not self.split or p >= 2
                along_x.append(half * (jnp.where(self.last, here[p], to_next[p]) if at_end else to_next[p]))
            along_z = [half * (here[p] + self.next_z(here, p)) for p in parts]
            fields = [[] for _ in range(8)]
            for p in parts:
                to_last = self.last_x(along_x, p)
                faces = [upper[p], below[p], along_x[p], to_last, along_z[p], self.last_z(along_z, p)]
                inner = list(faces)
                if not self.split or p >= 2:
                    inner[2] = jnp.where(self.last, 0.0, faces[2])
                if not self.split or p < 2:
                    faces[3] = jnp.where(self.first, half * here[p], to_last)
                    inner[3] = jnp.where(self.first, 0.0, to_last)
                diagonal = (faces[0] + faces[1]) + (faces[2] + faces[3]) + (faces[4] + faces[5])
                inverse = jnp.where(here[p] > 0.0, 1.0 / diagonal, 0.0)
                for field, value in zip(fields, [source[p] * inverse, diagonal, *(face * inverse for face in inner)]):
                    field.append(value)
            step = [value * first for value in fields[0]]
            refs = (self.right, self.diagonal, *self.sides, self.values, self.update)
            stores = [(ref, i, field) for ref, field in zip(refs, [*fields, step, step])]
            return (above, upper), stores + use(i, here)

        low, high = self.pad, self.rows - self.pad
        here, before = self.read(self.coef, low), self.read(self.coef, low - 1)
        run(low, high - low, body, (here, [half * (here[p] + before[p]) for p in parts]), self.unroll)

    def sweep(self, low, count, use):
        parts = range(self.parts)

        def body(i, carry):
            below, here = carry
            above = self.read(self.values, i + 1)
            right = self.read(self.right, i)
            up, down, ahead, behind, right_z, left_z = (self.read(ref, i) for ref in self.sides)
            left = [
                ((right[p] - here[p]) + (up[p] * above[p] + down[p] * below[p]))
                + (ahead[p] * self.next_x(here, p) + behind[p] * self.last_x(here, p))
                + (right_z[p] * self.next_z(here, p) + left_z[p] * self.last_z(here, p))
                for p in parts
            ]
            return (here, above), use(i, left, here)

        run(low, count, body, (self.read(self.values, low - 1), self.read(self.values, low)), self.unroll)

    def smooth(self, low, count, weight):
        keep, gain = weight

        def use(i, left, here):
            step = [gain * left[p] for p in range(self.parts)]
            if keep:
                update = self.read(self.update, i)
                step = [keep * update[p] + step[p] for p in range(self.parts)]
            return [(self.update, i, step), (self.values, i, [here[p] + step[p] for p in range(self.parts)])]

        self.sweep(low, count, use)

    def residual(self, i, left):
        return [value * factor for value, factor in zip(left, self.read(self.diagonal, i))]


def total(items):
    items = list(items)
    while len(items) > 1:
        items = [sum(items[k : k + 2][1:], items[k]) for k in range(0, len(items), 2)]
    return items[0]


def exact_dot(left, right):
    return jnp.dot(left, right, precision=lax.Precision.HIGHEST, preferred_element_type=jnp.float32)


def parity_matrix(size, back):
    row, column = tile_place((size, size), 0), tile_place((size, size), 1)
    if back:
        row, column = column, row
    hit = column == row // 2 + (row % 2) * (size // 2)
    return jnp.where(hit, 1.0, 0.0).astype(jnp.float32)


def parity_place(x, count):
    return x // 2 + (x % 2) * (count // 2)


def halo_rows(by):
    return 2 * (by // 4) + DEGREE + 1


def split_kernel(fields, out, pair_out, inner_out, rows):
    _, bx, by, bz = fields.shape
    _, _, _, _, odd = place()
    halo = halo_rows(by)
    matrix = parity_matrix(bz, False)
    for which in (0, 1):
        moved = exact_dot(fields[which].reshape(bx * by, bz), matrix)
        for x in range(bx):
            at = parity_place(x, bx) * by
            rows[which, at : at + by] = moved[x * by : (x + 1) * by]
        for y in range(by):
            out[which, y] = rows[which, pl.ds(y, bx, stride=by), :]
    for which in (0, 1):
        pair_out[which] = out[which, pl.ds((1 - odd) * (by - halo), halo)]
        inner_out[which] = out[which, pl.ds(odd * (by - halo), halo)]


def pack_kernel(*refs):
    *blocks, across_out, beside_out = refs
    _, _, _, core, _ = place()
    tile = across_out.shape[1:]
    quarter = tile[1] // 4
    low = tile_place(tile, 1) % (2 * quarter) < quarter
    at = 0
    for block in blocks:
        for y in range(block.shape[1]):
            right, coef = block[0, y], block[1, y]
            first = jnp.where(low, right, turn(coef, quarter, 1))
            last = jnp.where(low, turn(coef, -quarter, 1), right)
            across_out[at] = jnp.where(core == 0, first, last)
            beside_out[at] = jnp.where(core == 0, last, first)
            at += 1


def down_kernel(mine, other, pair, pair_other, inner, inner_other, *refs):
    edges, refs = refs[: 2 * len(GROUPS)], refs[2 * len(GROUPS) :]
    fields, (pay_out, far_out, near_out), (update, coef, right, sums, coefs) = refs[:9], refs[9:12], refs[12:]
    level = Level((*fields, update, coef, right), True, 1, 1.0, UNROLL_FINE)
    by, bx, bz = mine.shape[1:]
    halo = pair.shape[1]
    at_x, at_y, at_z, core, odd = place()
    tile = (bx, bz)
    lane = tile_place(tile, 1)
    quarter = bz // 4
    is_own = lane < bz // 2
    low = lane % (bz // 2) < quarter
    outside = (low == (core == 1)) & ~in_the_middle(at_z)
    top = tile_place(tile, 0) < bx // 2

    def columns(block, y, kind):
        blocks = (mine, other, pair, pair_other, inner, inner_other)
        number = next(number for number, group in enumerate(GROUPS) if kind in group)
        before = GROUPS[number][: GROUPS[number].index(kind)]
        at = y + sum(blocks[earlier].shape[1] for earlier in before)
        over, beside = edges[2 * number][at], edges[2 * number + 1][at]
        first = jnp.where(core == 1, over, beside)
        last = jnp.where(core == 1, beside, over)
        side, own = jnp.where(low, first, last), block[0, y]
        right_cells = [
            jnp.where(is_own, own, turn(side, bz // 2, 1)),
            jnp.where(is_own, turn(own, bz // 2, 1), side),
        ]
        side, own = jnp.where(low, last, first), block[1, y]
        up, down = turn(side, quarter, 1), turn(side, -quarter, 1)
        coef_cells = [
            jnp.where(is_own, own, jnp.where(outside, 0.0, jnp.where(low, up, down))),
            jnp.where(is_own, turn(own, bz // 2, 1), jnp.where(outside, 0.0, jnp.where(low, down, up))),
        ]
        return right_cells, coef_cells

    for kind, (near, far, row) in zip((0, 2, 4), (
        (mine, other, halo),
        (pair, pair_other, (1 - odd) * (halo + by)),
        (inner, inner_other, odd * (halo + by)),
    )):
        count = near.shape[1]

        def assemble(y, carry, near=near, far=far, row=row, kind=kind):
            both = zip(columns(near, y, kind), columns(far, y, kind + 1))
            stores = []
            for ref, (here, there) in zip((right, coef), both):
                for odd_z in (0, 1):
                    one = jnp.where(at_x == 0, here[odd_z], there[odd_z])
                    two = jnp.where(at_x == 0, there[odd_z], here[odd_z])
                    cells = jnp.where(top, one, turn(two, bx // 2, 0)), jnp.where(top, turn(one, bx // 2, 0), two)
                    for odd_x in (0, 1):
                        value = cells[odd_x]
                        if ref is coef and near is inner:
                            value = jnp.where(in_the_middle(at_y), value, 0.0)
                        stores.append((ref.at[pl.ds(2 * odd_x + odd_z, 1)], row + y, [value]))
            return carry, stores

        run(0, count, assemble, 0, 16)

    level.begin(lambda i, here: [(coefs, i, [total(here)])])
    edge = 1
    for weight in smoothing_weights()[1:]:
        edge += 1
        level.smooth(edge, level.rows - 2 * edge, weight)

    def leftover(i, left, here):
        return [(sums, i, [total(level.residual(i, left))])]

    edge += 1
    level.sweep(edge, level.rows - 2 * edge, leftover)
    for which, ref in enumerate((sums, coefs)):
        for y in range(by):
            pay_out[which, y] = 0.125 * (ref[0, edge + 2 * y] + ref[0, edge + 2 * y + 1])
        shared = by // 4
        far_out[which] = pay_out[which, pl.ds(shared * (1 - odd), by - shared)]
        near_out[which] = pay_out[which, pl.ds(shared * (1 + odd), shared)]


def up_kernel(pay, far, near, *refs):
    fields, start, (solution_out, residual_out), refs = refs[:8], refs[8], refs[9:11], refs[11:]
    level1 = Level(refs[:12], False, 1, 0.25, UNROLL_COARSE, near.shape[1])
    level2 = Level(refs[12:24], False, 2, 0.0625, UNROLL_COARSE)
    values, update, sums, moved, rows_out = refs[24:]
    fine = Level((*fields, values, update, None, None), True, 1, 1.0, UNROLL_FINE)
    by, bx, bz = pay.shape[1:]
    shared = near.shape[1]
    at_x, at_y, _, _, odd = place()
    weights = smoothing_weights()
    tile = (bx, bz)
    level1.clear()
    level2.clear()

    own1 = (by // 2) * at_y
    far1 = (by // 2) * (at_y + 2 - 4 * (at_y // 2)) + shared * (1 - odd)
    near1 = (by // 2) * (at_y + 1 - 2 * odd) + shared + shared * (1 - odd)
    for which, ref in enumerate((level1.source, level1.coef)):
        for piece, at in ((pay, own1), (far, far1), (near, near1)):
            for y in range(piece.shape[1]):
                ref[0, at + y] = piece[which, y]

    low1, high1 = level1.pad, level1.rows - level1.pad
    n2 = level2.rows - 1
    even_lane = tile_place(tile, 1) % 2 == 0
    even_row = tile_place(tile, 0) % 2 == 0

    def pair_cells(values):
        values = values + jnp.where(even_lane, turn(values, -1, 1), turn(values, 1, 1))
        return 0.125 * (values + jnp.where(even_row, turn(values, -1, 0), turn(values, 1, 0)))

    level1.begin(lambda i, here: [])
    for weight in weights[1:]:
        level1.smooth(low1, high1 - low1, weight)

    def leftover1(i, left, here):
        return [(sums, i, level1.residual(i, left))]

    level1.sweep(low1, high1 - low1, leftover1)
    for j in range(1, n2):
        level2.source[0, j] = pair_cells(sums[0, low1 + 2 * j - 2] + sums[0, low1 + 2 * j - 1])
        level2.coef[0, j] = pair_cells(level1.coef[0, low1 + 2 * j - 2] + level1.coef[0, low1 + 2 * j - 1])

    level2.begin(lambda i, here: [])
    for weight in weights[1:]:
        level2.smooth(1, n2 - 1, weight)

    for j in range(low1, high1):
        level1.values[0, j] = level1.values[0, j] + level2.values[0, 1 + (j - low1) // 2]
    reach = DEGREE + (DEGREE + 2) // 2
    for weight in weights:
        reach -= 1
        count = by // 2 + 2 * reach
        start1 = jnp.clip(shared + own1 - reach, low1, high1 - count)
        level1.smooth(start1, count, weight)

    halo = (fine.rows - by) // 2
    reach = DEGREE + 1
    base = shared + own1
    for y in range(-reach, by + reach):
        coarse = level1.values[0, base + y // 2]
        for part in range(fine.parts):
            values[part, halo + y] = start[part, halo + y] + coarse
    for weight in weights:
        reach -= 1
        fine.smooth(halo - reach, by + 2 * reach, weight)

    own_lane = tile_place(tile, 1) < bz // 2
    top = tile_place(tile, 0) < bx // 2

    def finish(i, left, here):
        stores = []
        for slot, field in enumerate((here, fine.residual(i, left))):
            cells = []
            for odd_z in (0, 1):
                one, two = field[odd_z], field[2 + odd_z]
                cells.append(
                    jnp.where(
                        top,
                        jnp.where(at_x == 0, one, turn(one, bx // 2, 0)),
                        jnp.where(at_x == 0, turn(two, bx // 2, 0), two),
                    )
                )
            stores.append((rows_out.at[pl.ds(slot, 1)], i - halo, [jnp.where(own_lane, cells[0], turn(cells[1], bz // 2, 1))]))
        return stores

    fine.sweep(halo, by, finish)
    matrix = parity_matrix(bz, True)
    for slot, ref in enumerate((solution_out, residual_out)):
        moved[slot] = exact_dot(rows_out[slot].reshape(by * bx, bz), matrix)
        for x in range(bx):
            ref[x] = moved[slot, pl.ds(parity_place(x, bx), by, stride=bx), :]


def vmem(*shape):
    return pltpu.VMEM(shape, jnp.float32)


def per_device_two_rounds(right_side, coefficient):
    bx, by, bz = right_side.shape
    halo = halo_rows(by)
    shared = by // 4
    in_vmem = pl.BlockSpec(memory_space=pltpu.VMEM)
    params = pltpu.CompilerParams(vmem_limit_bytes=24 * 2**20)
    shape = lambda *sizes: jax.ShapeDtypeStruct(sizes, jnp.float32)

    mine, for_pair, for_inner = pl.pallas_call(
        split_kernel,
        out_shape=(shape(2, by, bx, bz), shape(2, halo, bx, bz), shape(2, halo, bx, bz)),
        in_specs=[in_vmem],
        out_specs=(in_vmem,) * 3,
        scratch_shapes=[vmem(2, bx * by, bz)],
        compiler_params=params,
        name="split",
    )(jnp.stack([right_side, coefficient]))

    pairs = [1, 0, 3, 2]
    inner = [0, 2, 1, 3]
    swap_pairs = list(enumerate(pairs))

    def across_x(partner):
        return [(4 * x + y, 4 * (1 - x) + partner[y]) for x in (0, 1) for y in range(4)]

    swap_inner = [(4 * x + y, 4 * (1 - x if inner[y] == y else x) + inner[y]) for x in (0, 1) for y in range(4)]

    blocks = {
        "mine": mine,
        "other": lax.ppermute(mine, "gx", [(0, 1), (1, 0)]),
        "pair": lax.ppermute(for_pair, "gy", swap_pairs),
        "pair_other": lax.ppermute(for_pair, ("gx", "gy"), across_x(pairs)),
        "inner": lax.ppermute(for_inner, "gy", list(enumerate(inner))),
        "inner_other": lax.ppermute(for_inner, ("gx", "gy"), across_x(inner)),
    }
    blocks = list(blocks.values())
    def share(group):
        edges = shape(sum(block.shape[1] for block in group), bx, bz)
        to_mid, to_sib = pl.pallas_call(
            pack_kernel,
            out_shape=(edges, edges),
            in_specs=[in_vmem] * len(group),
            out_specs=(in_vmem,) * 2,
            compiler_params=params,
            name="pack",
        )(*group)
        return lax.ppermute(to_mid, ("gx", "gz"), swap_inner), lax.ppermute(to_sib, "gz", swap_pairs)

    edges = [part for group in GROUPS for part in share([blocks[kind] for kind in group])]

    rows = by + 2 * halo
    field = (4, rows, bx, bz)
    *fine, pay, far, near = pl.pallas_call(
        down_kernel,
        out_shape=(
            *[shape(*field)] * 9,
            shape(2, by, bx, bz),
            shape(2, by - shared, bx, bz),
            shape(2, shared, bx, bz),
        ),
        in_specs=[in_vmem] * (6 + 2 * len(GROUPS)),
        out_specs=(in_vmem,) * 12,
        scratch_shapes=[*[vmem(*field)] * 3, vmem(1, rows, bx, bz), vmem(1, rows, bx, bz)],
        compiler_params=params,
        name="down",
    )(*blocks, *edges)
    far = lax.ppermute(far, "gy", [(0, 2), (2, 0), (1, 3), (3, 1)])
    near = lax.ppermute(near, "gy", swap_pairs)
    rows1 = by // 2 * lax.axis_size("gy") + 2 * shared
    rows2 = by // 4 * lax.axis_size("gy") + 2
    return pl.pallas_call(
        up_kernel,
        out_shape=(shape(bx, by, bz),) * 2,
        in_specs=[in_vmem] * 12,
        out_specs=(in_vmem,) * 2,
        scratch_shapes=[
            *[vmem(1, rows1, bx, bz)] * 12,
            *[vmem(1, rows2, bx, bz)] * 12,
            vmem(*field),
            vmem(*field),
            vmem(1, rows1, bx, bz),
            vmem(2, bx * by, bz),
            vmem(2, by, bx, bz),
        ],
        compiler_params=params,
        name="up",
    )(pay, far, near, *fine)


def two_rounds_fit(mesh, shape):
    counts = tuple(mesh.shape[name] for name in ("gx", "gy", "gz"))
    bx, by, bz = (size // count for size, count in zip(shape, counts))
    shared = by // 4
    reach_coarse = 4 * DEGREE + 2
    return (
        counts == (2, 4, 4)
        and LEVELS == 3
        and bx == 8
        and by % 8 == 0
        and bz == 128
        and halo_rows(by) <= by
        and by // 2 + reach_coarse + 1 <= 2 * by - shared
        and 2 * reach_coarse + DEGREE + 1 <= bz // 2
    )


def solution(mesh):
    in_specs = (P("gx", "gy", "gz"), P("gx", "gy", "gz"))
    out_specs = (P("gx", "gy", "gz"), P("gx", "gy", "gz"))

    def whole(right_side, coefficient):
        fits = two_rounds_fit(mesh, right_side.shape)
        return jax.shard_map(
            per_device_two_rounds if fits else per_device,
            mesh=mesh,
            in_specs=in_specs,
            out_specs=out_specs,
            check_vma=False,
        )(right_side, coefficient)

    return whole
```
